32 devices in a mesh: dp: 4 (over z), ctx: 2 (over y), fsdp: 4 (over x, core).
Axes of the slice: x: 2, y: 2, z: 4, core: 2. Of those that a mesh axis runs over, the one named last changes fastest.
Arguments:
- layer_input: bfloat16 [4, 1024, 2560], P('dp', ('ctx', 'fsdp')), may hold values from -6 to 6
- segment_ids: int32 [4, 1024], P('dp'), may hold values from 0 to 3, as said below
- attn_gain: bfloat16 [2560], P('fsdp'), may hold values from 0.099609375 to 1.8984375
- query_down: bfloat16 [2560, 768], P('fsdp'), may hold values from -0.125 to 0.125
- query_gain: bfloat16 [768], P('fsdp'), may hold values from 0.099609375 to 1.8984375
- query_up: bfloat16 [768, 3840], P('fsdp'), may hold values from -0.21875 to 0.21875
- latent_down: bfloat16 [2560, 288], P('fsdp'), may hold values from -0.125 to 0.125
- latent_gain: bfloat16 [256], P('fsdp'), may hold values from 0.099609375 to 1.8984375
- latent_up: bfloat16 [256, 5120], P('fsdp'), may hold values from -0.375 to 0.375
- attn_output: bfloat16 [2560, 2560], P('fsdp'), may hold values from -4 to 4
- ffn_gain: bfloat16 [2560], P('fsdp'), may hold values from 0.099609375 to 1.8984375
- gate_up: bfloat16 [2, 6400, 2560], P(None, 'fsdp'), may hold values from -0.125 to 0.125
- down_proj: bfloat16 [6400, 2560], P('fsdp'), may hold values from -0.75 to 0.75
- cotangent: bfloat16 [4, 1024, 2560], P('dp', ('ctx', 'fsdp')), may hold values from -6 to 6
Outputs:
- layer_output: bfloat16 [4, 1024, 2560], P('dp', ('ctx', 'fsdp'))
- input_grad: float32 [4, 1024, 2560], P('dp', ('ctx', 'fsdp'))
- attn_gain_grad: float32 [2560], P('fsdp')
- query_down_grad: float32 [2560, 768], P('fsdp')
- query_gain_grad: float32 [768], P('fsdp')
- query_up_grad: float32 [768, 3840], P('fsdp')
- latent_down_grad: float32 [2560, 288], P('fsdp')
- latent_gain_grad: float32 [256], P('fsdp')
- latent_up_grad: float32 [256, 5120], P('fsdp')
- attn_output_grad: float32 [2560, 2560], P('fsdp')
- ffn_gain_grad: float32 [2560], P('fsdp')
- gate_up_grad: float32 [2, 6400, 2560], P(None, 'fsdp')
- down_proj_grad: float32 [6400, 2560], P('fsdp')
The draws below stay inside these ranges and needn't reach their ends.
Inputs may be any that keep to these rules, and one draw needn't show every extreme that they name: `segment_ids`: segment numbers never fall along a sequence and each sequence holds the 4 documents 0 to 3, each of one token or more. Document 1 holds exactly 896 tokens and begins within the first 126 tokens; the others hold fewer than 128 tokens each.
All inputs are finite; a program needn't handle non-finite values.
Results may differ from the reference program's by a relative error of at most 0.023.
Values may be sent and summed in bfloat16 or wider, within the bound.
A program may use at most 768 MiB of HBM per device.

```python
import math
import jax
import jax.numpy as jnp
from jax import lax

D = 2560
H = 40
DN = 64
DR = 32
DV = 64
QR = 768
KR = 256
FF = 6400
SPAN = 128
SEQ_LEN = 1024
SEQS = 4


def draw_segment_ids(key, part):
    key = jax.random.fold_in(key, 11)
    first_key, second_key = jax.random.split(key)
    first_len = jax.random.randint(first_key, (SEQS,), 1, SPAN - 1)
    spare = SPAN - 1 - first_len
    third_len = jax.random.randint(second_key, (SEQS,), 0, 1048576) % spare + 1
    end_one = first_len
    end_two = first_len + (SEQ_LEN - SPAN)
    end_three = end_two + third_len
    index_all = jnp.arange(SEQ_LEN, dtype=jnp.int32)[None, :]
    segments = (index_all >= end_one[:, None]).astype(jnp.int32)
    segments = segments + (index_all >= end_two[:, None]).astype(jnp.int32)
    segments = segments + (index_all >= end_three[:, None]).astype(jnp.int32)
    return segments.astype(jnp.int32)


def block_scale(rng, shape, shards, least, largest):
    def one(axis_at, shards_of):
        steps = jax.random.uniform(jax.random.fold_in(jax.random.fold_in(rng, 6), axis_at), (shards_of,), jnp.float32, least / len(shards), largest / len(shards))
        return jnp.repeat(jnp.exp(steps), shape[axis_at] // shards_of).reshape((-1,) + (1,) * (len(shape) - axis_at - 1))

    factor_of = one(*shards[0])
    for cut in shards[1:]:
        factor_of = factor_of * one(*cut)
    return factor_of


def gaussian(rng, shape, width, most, cuts=(), held_as=jnp.bfloat16):
    values = jax.random.normal(rng, shape, jnp.float32) * width
    if len(cuts) > 0:
        values = block_scale(rng, shape, cuts, -0.22, 0.18) * values
    return jnp.clip(values, min=-most, max=most).astype(held_as)


def setup_inputs(seed: int = 0) -> dict:
    streams_of = jax.random.split(jax.random.key(seed), 15)
    return {
        "layer_input": gaussian(streams_of[0], (SEQS, SEQ_LEN, D), 1.0, 6.0, ((0, 4), (1, 8))),
        "segment_ids": draw_segment_ids(jax.random.fold_in(streams_of[14], 71), 0),
        "attn_gain": jnp.clip(1.0 + 0.18 * jax.random.normal(streams_of[2], (D,), jnp.float32), 0.099609375, 1.8984375).astype(jnp.bfloat16),
        "query_down": gaussian(streams_of[3], (D, QR), D ** -0.5, 0.125, ((0, 4),)),
        "query_gain": jnp.clip(1.0 + 0.18 * jax.random.normal(streams_of[4], (QR,), jnp.float32), 0.099609375, 1.8984375).astype(jnp.bfloat16),
        "query_up": gaussian(streams_of[5], (QR, H * (DN + DR)), QR ** -0.5, 0.21875, ((0, 4),)),
        "latent_down": gaussian(streams_of[6], (D, KR + DR), D ** -0.5, 0.125, ((0, 4),)),
        "latent_gain": jnp.clip(1.0 + 0.18 * jax.random.normal(streams_of[7], (KR,), jnp.float32), 0.099609375, 1.8984375).astype(jnp.bfloat16),
        "latent_up": gaussian(streams_of[8], (KR, H * (DN + DV)), KR ** -0.5, 0.375, ((0, 4),)),
        "attn_output": gaussian(streams_of[9], (H * DV, D), 2 ** -0.5, 4.0, ((0, 4),)),
        "ffn_gain": jnp.clip(1.0 + 0.18 * jax.random.normal(streams_of[10], (D,), jnp.float32), 0.099609375, 1.8984375).astype(jnp.bfloat16),
        "gate_up": gaussian(streams_of[11], (2, FF, D), D ** -0.5, 0.125, ((1, 4),)),
        "down_proj": gaussian(streams_of[12], (FF, D), 64 ** -0.5, 0.75, ((0, 4),)),
        "cotangent": gaussian(streams_of[13], (SEQS, SEQ_LEN, D), 1.0, 6.0, ((0, 4), (1, 8))),
    }


EPS = 1e-05
RESIDUAL_SCALE = 1.4 / math.sqrt(62.0)
NEGATIVE = -1e+30
ROPE_BASE = 10000.0
HIGHEST = lax.Precision.HIGHEST

@jax.custom_vjp
def low(v):
    return lax.optimization_barrier(v.astype(jnp.bfloat16)).astype(jnp.float32)

@jax.custom_vjp
def low_back(v):
    return v

def low_keep(v):
    return (low(v), None)

def low_pass(kept, grad):
    return (grad,)

def back_keep(v):
    return (v, None)

def back_low(kept, grad):
    return (low(grad),)
low.defvjp(low_keep, low_pass)
low_back.defvjp(back_keep, back_low)

def normalize(values, gain):
    return values * lax.rsqrt(lax.optimization_barrier(jnp.mean(values * values, axis=-1, keepdims=True)) + EPS) * gain

def angles(positions):
    half = DR // 2
    frequency = ROPE_BASE ** (-jnp.arange(half, dtype=jnp.float32) / half)
    theta = positions[:, None] * frequency[None, :]
    return (jnp.cos(theta), jnp.sin(theta))

def rotate(values, cosine, sine):
    half = values.shape[-1] // 2
    first = values[..., :half]
    second = values[..., half:]
    return jnp.concatenate([first * cosine - second * sine, second * cosine + first * sine], axis=-1)

def matmul(left, right):
    return jnp.dot(left, right, precision=HIGHEST)

def attention(queries, key_value, key_rope, segments):
    length = queries.shape[0]
    block = min(256, length)
    scale = (DN + DR) ** (-0.5)
    key_index = jnp.arange(length, dtype=jnp.int32)

    def one_block(step):
        start = (step * block).astype(jnp.int32)
        query_part = lax.dynamic_slice_in_dim(queries, start, block, 0)
        query_segs = lax.dynamic_slice_in_dim(segments, start, block, 0)
        query_index = start + jnp.arange(block, dtype=jnp.int32)
        raw = jnp.einsum('tgd,lgd->gtl', query_part[..., :DN], key_value[..., :DN], precision=HIGHEST)
        raw = raw + jnp.einsum('tgd,ld->gtl', query_part[..., DN:], key_rope, precision=HIGHEST)
        scores = low_back(raw * scale)
        mask = (query_segs[:, None] == segments[None, :]) & (key_index[None, :] <= query_index[:, None])
        scores = jnp.where(mask[None], scores, NEGATIVE)
        peak = lax.optimization_barrier(jnp.max(scores, axis=-1, keepdims=True))
        weights = jnp.exp(scores - peak)
        probs = weights / lax.optimization_barrier(jnp.sum(weights, axis=-1, keepdims=True))
        probs_low = low(probs)
        return jnp.einsum('gtl,lgd->tgd', probs_low, key_value[..., DN:], precision=HIGHEST)
    blocks = lax.map(jax.checkpoint(one_block), jnp.arange(length // block, dtype=jnp.int32))
    return blocks.reshape(length, H, DV)

def layer(inputs, cosine, sine, segments, g_attn, w_qdown, g_query, w_qup, w_ldown, g_latent, w_lup, w_out, g_ffn, w_gate_up, w_down):
    length = inputs.shape[0]
    normed_in = low(normalize(inputs, g_attn))
    query_latent = low_back(matmul(normed_in, w_qdown))
    query_normed = low(normalize(query_latent, g_query))
    query_raw = low_back(matmul(query_normed, w_qup)).reshape(length, H, DN + DR)
    queries = low(jnp.concatenate([query_raw[..., :DN], rotate(query_raw[..., DN:], cosine[:, None, :], sine[:, None, :])], axis=-1))
    latent_raw = low_back(matmul(normed_in, w_ldown))
    latent = low(normalize(latent_raw[:, :KR], g_latent))
    key_rope = low(rotate(latent_raw[:, KR:], cosine, sine))
    key_value = low(matmul(latent, w_lup)).reshape(length, H, DN + DV)
    attended = attention(queries, key_value, key_rope, segments)
    attn_out = low(low_back(attended.reshape(length, H * DV)))
    branch = low_back(matmul(attn_out, w_out))
    resid = inputs + RESIDUAL_SCALE * branch
    ffn_in = low(normalize(resid, g_ffn))
    gate_and_up = low_back(jnp.einsum('td,kfd->ktf', ffn_in, w_gate_up, precision=HIGHEST))
    hidden = low(jax.nn.silu(gate_and_up[0]) * gate_and_up[1])
    ffn_branch = low_back(matmul(hidden, w_down))
    return resid + RESIDUAL_SCALE * ffn_branch

def reference(layer_input, segment_ids, attn_gain, query_down, query_gain, query_up, latent_down, latent_gain, latent_up, attn_output, ffn_gain, gate_up, down_proj, cotangent):
    weights = (attn_gain.astype(jnp.float32), query_down.astype(jnp.float32), query_gain.astype(jnp.float32), query_up.astype(jnp.float32), latent_down.astype(jnp.float32), latent_gain.astype(jnp.float32), latent_up.astype(jnp.float32), attn_output.astype(jnp.float32), ffn_gain.astype(jnp.float32), gate_up.astype(jnp.float32), down_proj.astype(jnp.float32))

    def per_sequence(totals, items):
        inputs, segments, grad_out = items
        length = segments.shape[0]
        index_all = jnp.arange(length, dtype=jnp.int32)
        doc_start = lax.optimization_barrier(jnp.sum((segments[None, :] < segments[:, None]).astype(jnp.int32), axis=1))
        positions = (index_all - doc_start).astype(jnp.float32)
        cosine, sine = angles(positions)

        def forward(values, *params):
            return layer(values, cosine, sine, segments, *params)
        result, pullback = jax.vjp(forward, inputs.astype(jnp.float32), *weights)
        grads = pullback(grad_out.astype(jnp.float32))
        totals = tuple((total + grad for total, grad in zip(totals, grads[1:])))
        return (totals, (result.astype(jnp.bfloat16), grads[0]))
    initial = tuple((jnp.zeros_like(weight) for weight in weights))
    totals, (outputs, input_grads) = lax.scan(per_sequence, initial, (layer_input, segment_ids, cotangent))
    return (outputs, input_grads, totals[0], totals[1], totals[2], totals[3], totals[4], totals[5], totals[6], totals[7], totals[8], totals[9], totals[10])
```

```python
import functools
import math

import jax
import jax.numpy as jnp
import numpy as np
from jax import lax
from jax.experimental import pallas as pl
from jax.experimental.pallas import tpu as pltpu
from jax.sharding import PartitionSpec as P

D = 2560
H = 40
DN = 64
DR = 32
DV = 64
QR = 768
KR = 256
LANES = 128
DOWN = QR + KR + DR
PACK = QR + KR + LANES
EXTRA = 32

EPS = 1e-05
RESIDUAL_SCALE = 1.4 / math.sqrt(62.0)
NEGATIVE = -1e30
ROPE_BASE = 10000.0
SCALE = (DN + DR) ** (-0.5)
f32 = jnp.float32
bf16 = jnp.bfloat16

NN = (((1,), (0,)), ((), ()))
NT = (((1,), (1,)), ((), ()))
TN = (((0,), (0,)), ((), ()))
MIB = 1024 * 1024


def dot(left, right, dims=NN):
    return lax.dot_general(left, right, dims, preferred_element_type=f32)


def normalize(values, gain):
    return values * lax.rsqrt(jnp.mean(values * values, axis=-1, keepdims=True) + EPS) * gain


def norm_back(values, gain, grad):
    primal, pullback = jax.vjp(normalize, values, gain)
    return pullback(grad)


def angles(positions):
    half = DR // 2
    frequency = ROPE_BASE ** (-jnp.arange(half, dtype=f32) / half)
    theta = positions[:, None] * frequency[None, :]
    return (jnp.cos(theta), jnp.sin(theta))


def rotate(values, cosine, sine):
    half = values.shape[-1] // 2
    first = values[..., :half]
    second = values[..., half:]
    return jnp.concatenate(
        [first * cosine - second * sine, second * cosine + first * sine], axis=-1
    )


def unrotate(grad, cosine, sine):
    return rotate(grad, cosine, -sine)


def swapped(values):
    lane = lax.broadcasted_iota(jnp.int32, values.shape, 1)
    up = pltpu.roll(values, LANES - DR // 2, 1)
    back = pltpu.roll(values, DR // 2, 1)
    return jnp.where(lane < DN + DR // 2, up, -back)


def allowed(seg_col, seg_row, first, rows, columns):
    query = first + lax.broadcasted_iota(jnp.int32, (rows, columns), 0)
    key = lax.broadcasted_iota(jnp.int32, (rows, columns), 1)
    return (seg_col[first : first + rows, :] == seg_row[:, :columns]) & (key <= query)


PLANE = ("ctx", "fsdp")
ALL = ("dp", "ctx", "fsdp")
MESH = pl.DeviceIdType.MESH


def seats():
    y = lax.axis_index("ctx")
    f = lax.axis_index("fsdp")
    core = lax.rem(f, 2)
    mate = {"fsdp": f + 1 - 2 * core}
    along_x = {"fsdp": lax.rem(f + 2, 4)}
    along_y = {"ctx": 1 - y}
    return y, f, core, mate, along_x, along_y


def greet(peers):
    barrier = pltpu.get_barrier_semaphore()
    for peer in peers:
        pl.semaphore_signal(barrier, inc=1, device_id=peer, device_id_type=MESH)
    pl.semaphore_wait(barrier, len(peers))


class Wires:
    def __init__(self, send, recv):
        self.send, self.recv, self.count = send, recv, 0

    def copy(self, src, dst, peer):
        at = self.count
        self.count += 1
        return pltpu.make_async_remote_copy(
            src_ref=src,
            dst_ref=dst,
            send_sem=self.send.at[at],
            recv_sem=self.recv.at[at],
            device_id=peer,
            device_id_type=MESH,
        )


class Spread:
    wires_needed = 9

    def __init__(self, wires, src, out, base, local):
        rows = src.shape[0]
        half = rows // 2
        y, f, core, mate, along_x, along_y = seats()
        x_f = lax.rem(f + 2, 4)
        me, x_seat, y_seat, far = y * 4 + f, y * 4 + x_f, (1 - y) * 4 + f, (1 - y) * 4 + x_f
        at = lambda seat, first, count: out.at[
            pl.ds(pl.multiple_of(base + seat * rows + first, 16), count)
        ]
        whole = lambda seat: at(seat, 0, rows)
        upper = lambda seat: at(seat, 0, half)
        lower = lambda seat: at(seat, half, half)
        self.keep = pltpu.make_async_copy(src, whole(me), local)
        self.mine = [wires.copy(src, whole(me), peer) for peer in (along_x, along_y, mate)]
        self.pass_y = wires.copy(upper(x_seat), upper(x_seat), along_y)
        self.pass_x = wires.copy(lower(y_seat), lower(y_seat), along_x)
        self.mate_x = wires.copy(whole(x_seat), whole(x_seat), mate)
        self.mate_y = wires.copy(whole(y_seat), whole(y_seat), mate)
        self.mate_u = wires.copy(upper(far), upper(far), mate)
        self.mate_l = wires.copy(lower(far), lower(far), mate)

    def start(self):
        for copy in self.mine:
            copy.start()
        self.keep.start()

    def relay(self):
        self.mine[0].wait_recv()
        self.pass_y.start()
        self.mate_x.start()
        self.mine[1].wait_recv()
        self.pass_x.start()
        self.mate_y.start()

    def finish(self):
        self.pass_y.wait_recv()
        self.mate_u.start()
        self.pass_x.wait_recv()
        self.mate_l.start()
        for copy in (self.mine[2], self.mate_x, self.mate_y, self.mate_u, self.mate_l):
            copy.wait_recv()
        rest = [self.pass_y, self.pass_x, self.mate_x, self.mate_y, self.mate_u, self.mate_l]
        for copy in self.mine + rest:
            copy.wait_send()
        self.keep.wait()


class Light:
    wires_needed = 6

    def __init__(self, wires, src, far_src, stage, out, base, local):
        rows = src.shape[0]
        y, f, core, mate, along_x, along_y = seats()
        x_f = lax.rem(f + 2, 4)
        me, x_seat, y_seat, far = y * 4 + f, y * 4 + x_f, (1 - y) * 4 + f, (1 - y) * 4 + x_f
        at = lambda seat: out.at[pl.ds(pl.multiple_of(base + seat * rows, 16), rows)]
        self.fetch = [
            pltpu.make_async_copy(src, stage.at[0], local.at[0]),
            pltpu.make_async_copy(far_src, stage.at[1], local.at[1]),
        ]
        self.keep = [
            pltpu.make_async_copy(stage.at[0], at(me), local.at[2]),
            pltpu.make_async_copy(stage.at[1], at(far), local.at[3]),
        ]
        self.mine = [wires.copy(stage.at[0], at(me), peer) for peer in (along_x, along_y, mate)]
        self.far = wires.copy(stage.at[1], at(far), mate)
        self.mate_x = wires.copy(at(x_seat), at(x_seat), mate)
        self.mate_y = wires.copy(at(y_seat), at(y_seat), mate)

    def load(self):
        for copy in self.fetch:
            copy.start()

    def start(self):
        for copy in self.fetch:
            copy.wait()
        for copy in self.mine + [self.far] + self.keep:
            copy.start()

    def relay(self):
        self.mine[0].wait_recv()
        self.mate_x.start()
        self.mine[1].wait_recv()
        self.mate_y.start()

    def finish(self):
        for copy in (self.mine[2], self.far, self.mate_x, self.mate_y):
            copy.wait_recv()
        for copy in self.mine + [self.far, self.mate_x, self.mate_y]:
            copy.wait_send()
        for copy in self.keep:
            copy.wait()


def turn_z(step):
    return lax.rem(lax.axis_index("dp") + step, lax.axis_size("dp"))


def attend_kernel(
    block, units, lat, wq, wl, cos, sin, seg_col, seg_row, *rest
):
    sources, rest = rest[:units], rest[units:]
    (q_out, k_out, kv_out, o_out, lse_out), rest = rest[:5], rest[5:]
    length = lat.shape[0]
    if units:
        out, local, send, recv = rest
        unit = Spread(Wires(send, recv), sources[0], out, 0, local.at[0])

        @pl.when(pl.program_id(0) == 0)
        def _():
            seat = seats()
            greet(seat[3:])
            unit.start()

        @pl.when(pl.program_id(0) == 3)
        def _():
            unit.relay()

    lane = lax.broadcasted_iota(jnp.int32, (length, LANES), 1)
    query = dot(lat[:, :QR], wq[...])
    query = (query * cos[...] - swapped(query) * sin[...]).astype(bf16)
    both = dot(lat[:, QR : QR + KR], wl[...]).astype(bf16)
    key = jnp.where(lane < DN, both, lat[:, QR + KR :])
    q_out[...] = query
    k_out[...] = key
    kv_out[...] = both
    for first in range(0, length, block):
        last = first + block
        scores = dot(query[first:last], key[:last], NT) * SCALE
        scores = jnp.where(allowed(seg_col, seg_row, first, block, last), scores, NEGATIVE)
        peak = jnp.max(scores, axis=-1, keepdims=True)
        weights = jnp.exp(scores - peak)
        total = jnp.sum(weights, axis=-1, keepdims=True)
        probs = (weights * (1.0 / total)).astype(bf16)
        o_out[first:last, :] = dot(probs, both[:last]).astype(bf16)
        lse_out[0, first:last, :] = peak + jnp.log(total)
    if units:

        @pl.when(pl.program_id(0) == pl.num_programs(0) - 1)
        def _():
            unit.finish()


def attend(lat, wq, wl, cos, sin, seg_col, seg_row, cot=None, tokens=0, name_id=0):
    length = lat.shape[0]
    heads = wq.shape[1] // LANES
    whole = lambda shape: pl.BlockSpec(shape, lambda h: (0,) * len(shape))
    mine = lambda rows: pl.BlockSpec((rows, LANES), lambda h: (0, h))
    anywhere = [pl.BlockSpec(memory_space=pl.ANY)]
    wide = jax.ShapeDtypeStruct((length, heads * LANES), bf16)
    units = 0 if cot is None else 1
    wires = Spread.wires_needed
    params = dict(collective_id=name_id, has_side_effects=True) if units else {}
    return pl.pallas_call(
        functools.partial(attend_kernel, min(256, length), units),
        grid=(heads,),
        in_specs=[
            whole((length, PACK)),
            mine(QR),
            mine(KR),
            whole((length, LANES)),
            whole((length, LANES)),
            whole((length, 1)),
            whole((1, length)),
        ]
        + [whole((length // 8, D))] * units,
        out_specs=[mine(length)] * 4
        + [pl.BlockSpec((1, length, 1), lambda h: (h, 0, 0))]
        + anywhere * units,
        out_shape=[wide] * 4
        + [jax.ShapeDtypeStruct((heads, length, 1), f32)]
        + [jax.ShapeDtypeStruct((tokens, D), bf16)] * units,
        scratch_shapes=[
            pltpu.SemaphoreType.DMA((1,)),
            pltpu.SemaphoreType.DMA((wires,)),
            pltpu.SemaphoreType.DMA((wires,)),
        ]
        if units
        else [],
        compiler_params=pltpu.CompilerParams(vmem_limit_bytes=56 * MIB, **params),
        cost_estimate=pl.CostEstimate(
            flops=heads * length * (length * 4 * LANES + 2 * LANES * (QR + KR)),
            bytes_accessed=heads * length * LANES * 16,
            transcendentals=heads * length * length,
        ),
    )(lat, wq, wl, cos, sin, seg_col, seg_row, *([cot] if units else []))


def attend_back_kernel(
    block, units, gb, wo, q, k, kv, o, lse, cos, sin, seg_col, seg_row, *rest
):
    sources, rest = rest[: 5 * units], rest[5 * units :]
    (gq_out, gkv_out, rope_out, wo_out), rest = rest[:4], rest[4:]
    length = gb.shape[0]
    if units:
        x_z, cot_z, cot_far, _, _ = sources
        x_all, cot_all, dk, dv, stage, local, send, recv = rest
        wires = Wires(send, recv)
        z = turn_z(1)
        fetch = pltpu.make_async_copy(x_z.at[z], stage.at[2], local.at[5])
        first_unit = Spread(wires, stage.at[2], x_all, length, local.at[4])
        second_unit = Light(
            wires, cot_z.at[z], cot_far.at[z], stage, cot_all, length, local
        )

        @pl.when(pl.program_id(0) == 0)
        def _():
            fetch.start()
            second_unit.load()
            seat = seats()
            greet(seat[3:])
            fetch.wait()
            first_unit.start()
            second_unit.start()

        @pl.when(pl.program_id(0) == 3)
        def _():
            first_unit.relay()
            second_unit.relay()

    else:
        dk, dv = rest
    wo_out[...] = dot(o[...], gb[...], TN)[LANES - DV :].astype(bf16)
    lane = lax.broadcasted_iota(jnp.int32, (length, LANES), 1)
    grad = dot(gb[...], wo[...], NT).astype(bf16)
    dk[...] = jnp.zeros_like(dk)
    dv[...] = jnp.zeros_like(dv)
    for first in range(0, length, block):
        last = first + block
        scores = dot(q[first:last, :], k[:last, :], NT) * SCALE
        probs = jnp.exp(scores - lse[0, first:last, :])
        probs = jnp.where(allowed(seg_col, seg_row, first, block, last), probs, 0.0)
        grad_probs = dot(grad[first:last], kv[:last, :], NT)
        delta = jnp.sum(probs * grad_probs, axis=-1, keepdims=True)
        grad_scores = (probs * (grad_probs - delta)).astype(bf16)
        gq = dot(grad_scores, k[:last, :]) * SCALE
        gq = gq * cos[first:last, :] + swapped(gq) * sin[first:last, :]
        gq_out[first:last, :] = gq.astype(bf16)
        dk[:last, :] += dot(grad_scores, q[first:last, :], TN) * SCALE
        dv[:last, :] += dot(probs.astype(bf16), grad[first:last], TN)
    gkv_out[...] = jnp.where(lane < DN, dk[...], dv[...]).astype(bf16)

    @pl.when(pl.program_id(0) == 0)
    def _():
        rope_out[...] = dk[...]

    @pl.when(pl.program_id(0) > 0)
    def _():
        rope_out[...] += dk[...]

    if units:

        @pl.when(pl.program_id(0) == pl.num_programs(0) - 1)
        def _():
            first_unit.finish()
            second_unit.finish()


def attend_back(gb, wo, q, k, kv, o, lse, cos, sin, seg_col, seg_row, bulk=(), tokens=0, name_id=0):
    units = 1 if bulk else 0
    wires = Spread.wires_needed + Light.wires_needed
    anywhere = [pl.BlockSpec(memory_space=pl.ANY)]
    params = dict(collective_id=name_id, has_side_effects=True) if units else {}
    length = gb.shape[0]
    heads = q.shape[1] // LANES
    whole = lambda shape: pl.BlockSpec(shape, lambda h: (0,) * len(shape))
    mine = pl.BlockSpec((length, LANES), lambda h: (0, h))
    wide = jax.ShapeDtypeStruct((length, heads * LANES), bf16)
    return pl.pallas_call(
        functools.partial(attend_back_kernel, min(256, length), units),
        grid=(heads,),
        in_specs=[
            whole((length, D)),
            pl.BlockSpec((LANES, D), lambda h: (h, 0)),
            mine,
            mine,
            mine,
            mine,
            pl.BlockSpec((1, length, 1), lambda h: (h, 0, 0)),
            whole((length, LANES)),
            whole((length, LANES)),
            whole((length, 1)),
            whole((1, length)),
        ]
        + anywhere * (5 * units),
        out_specs=[
            mine,
            mine,
            whole((length, LANES)),
            pl.BlockSpec((DV, D), lambda h: (h, 0)),
        ]
        + anywhere * (2 * units),
        input_output_aliases={14: 4, 15: 5} if units else {},
        out_shape=[
            wide,
            wide,
            jax.ShapeDtypeStruct((length, LANES), f32),
            jax.ShapeDtypeStruct((heads * DV, D), bf16),
        ]
        + [jax.ShapeDtypeStruct((tokens, D), bf16)] * (2 * units),
        scratch_shapes=[pltpu.VMEM((length, LANES), f32), pltpu.VMEM((length, LANES), f32)]
        + [
            pltpu.VMEM((3, length // 8, D), bf16),
            pltpu.SemaphoreType.DMA((6,)),
            pltpu.SemaphoreType.DMA((wires,)),
            pltpu.SemaphoreType.DMA((wires,)),
        ]
        * units,
        compiler_params=pltpu.CompilerParams(vmem_limit_bytes=56 * MIB, **params),
        cost_estimate=pl.CostEstimate(
            flops=heads * length * (length * 10 * LANES + 4 * LANES * D),
            bytes_accessed=heads * length * LANES * 16 + length * D * 2,
            transcendentals=heads * length * length,
        ),
    )(gb, wo, q, k, kv, o, lse, cos, sin, seg_col, seg_row, *bulk)


def hidden_block(x, cot, w_gu, w_down, h_out, g_out, parts):
    units = w_down.shape[0]
    step = units // parts
    for part in range(parts):
        rows = slice(part * step, (part + 1) * step)
        gate = dot(w_gu[0, rows, :], x, NT)
        upper = dot(w_gu[1, rows, :], x, NT)
        grad = dot(w_down[rows, :], cot, NT) * RESIDUAL_SCALE
        sigma = jax.nn.sigmoid(gate)
        silu = gate * sigma
        h_out[rows, :] = (silu * upper).astype(bf16)
        g_out[0, rows, :] = (grad * upper * sigma * (1.0 + gate * (1.0 - sigma))).astype(bf16)
        g_out[1, rows, :] = (grad * silu).astype(bf16)


def ffn_own_kernel(place, x, cot, w_gu, w_down, h_out, g_out, y_out, gx_out):
    hidden_block(x[...], cot[...], w_gu, w_down, h_out, g_out, 2)
    y_out[...] = dot(h_out[...], w_down[...], TN).astype(bf16)
    gx_out[...] = (dot(g_out[0], w_gu[0], TN) + dot(g_out[1], w_gu[1], TN)).astype(bf16)


def ffn_rest_kernel(place, x, cot, w_gu, w_down, h_in, g_in, h_out, g_out):
    hidden_block(x[...], cot[...], w_gu, w_down, h_out, g_out, 2)


def ffn_shapes(units, tokens):
    return [
        jax.ShapeDtypeStruct((units, tokens), bf16),
        jax.ShapeDtypeStruct((2, units, tokens), bf16),
    ]


def ffn_own(place, x, cot_all, w_gu, w_down):
    units = w_down.shape[0]
    tokens = cot_all.shape[0]
    block = min(256, x.shape[0])
    steps = x.shape[0] // block
    kept = pl.Buffered(1)
    return pl.pallas_call(
        ffn_own_kernel,
        grid_spec=pltpu.PrefetchScalarGridSpec(
            num_scalar_prefetch=1,
            grid=(steps,),
            in_specs=[
                pl.BlockSpec((block, D), lambda i, p: (i, 0)),
                pl.BlockSpec((block, D), lambda i, p: (p[0] * steps + i, 0)),
                pl.BlockSpec((2, units, D), lambda i, p: (0, 0, 0), pipeline_mode=kept),
                pl.BlockSpec((units, D), lambda i, p: (0, 0), pipeline_mode=kept),
            ],
            out_specs=[
                pl.BlockSpec((units, block), lambda i, p: (0, p[0] * steps + i)),
                pl.BlockSpec((2, units, block), lambda i, p: (0, 0, p[0] * steps + i)),
                pl.BlockSpec((block, D), lambda i, p: (i, 0)),
                pl.BlockSpec((block, D), lambda i, p: (i, 0)),
            ],
        ),
        out_shape=ffn_shapes(units, tokens) + [jax.ShapeDtypeStruct((x.shape[0], D), bf16)] * 2,
        compiler_params=pltpu.CompilerParams(vmem_limit_bytes=60 * MIB),
        cost_estimate=pl.CostEstimate(
            flops=12 * x.shape[0] * units * D, bytes_accessed=6 * units * D, transcendentals=0
        ),
    )(place, x, cot_all, w_gu, w_down)


def ffn_rest(place, x_all, cot_all, w_gu, w_down, h_all, g_all, own):
    units = w_down.shape[0]
    tokens = x_all.shape[0]
    block = min(256, own)
    steps = own // block
    blocks = tokens // block
    kept = pl.Buffered(1)
    at = lambda i, p: lax.rem((p[0] + 1) * steps + i, blocks)
    return pl.pallas_call(
        ffn_rest_kernel,
        grid_spec=pltpu.PrefetchScalarGridSpec(
            num_scalar_prefetch=1,
            grid=(blocks - steps,),
            in_specs=[
                pl.BlockSpec((block, D), lambda i, p: (at(i, p), 0)),
                pl.BlockSpec((block, D), lambda i, p: (at(i, p), 0)),
                pl.BlockSpec((2, units, D), lambda i, p: (0, 0, 0), pipeline_mode=kept),
                pl.BlockSpec((units, D), lambda i, p: (0, 0), pipeline_mode=kept),
                pl.BlockSpec(memory_space=pl.ANY),
                pl.BlockSpec(memory_space=pl.ANY),
            ],
            out_specs=[
                pl.BlockSpec((units, block), lambda i, p: (0, at(i, p))),
                pl.BlockSpec((2, units, block), lambda i, p: (0, 0, at(i, p))),
            ],
        ),
        out_shape=ffn_shapes(units, tokens),
        input_output_aliases={5: 0, 6: 1},
        compiler_params=pltpu.CompilerParams(vmem_limit_bytes=60 * MIB),
        cost_estimate=pl.CostEstimate(
            flops=6 * (tokens - own) * units * D,
            bytes_accessed=6 * units * D + 10 * tokens * D,
            transcendentals=0,
        ),
    )(place, x_all, cot_all, w_gu, w_down, h_all, g_all)


def remote_call(kernel, name_id, out_shape, scratch, wires, operands):
    return pl.pallas_call(
        kernel,
        out_shape=out_shape,
        in_specs=[pl.BlockSpec(memory_space=pltpu.VMEM)] * len(operands),
        out_specs=jax.tree.map(lambda _: pl.BlockSpec(memory_space=pltpu.VMEM), out_shape),
        scratch_shapes=scratch
        + [pltpu.SemaphoreType.DMA((wires,)), pltpu.SemaphoreType.DMA((wires,))],
        compiler_params=pltpu.CompilerParams(
            collective_id=name_id, has_side_effects=True, vmem_limit_bytes=56 * MIB
        ),
    )(*operands)


def gather_plane_steps(wires, x, out):
    rows = x.shape[0]
    half = rows // 2
    y, f, core, mate, along_x, along_y = seats()
    me = y * 4 + f
    x_seat = y * 4 + lax.rem(f + 2, 4)
    y_seat = (1 - y) * 4 + f
    far = (1 - y) * 4 + lax.rem(f + 2, 4)
    whole = lambda seat: out.at[pl.ds(seat * rows, rows)]
    upper = lambda seat: out.at[pl.ds(seat * rows, half)]
    lower = lambda seat: out.at[pl.ds(seat * rows + half, half)]
    mine_x = wires.copy(x, whole(me), along_x)
    mine_y = wires.copy(x, whole(me), along_y)
    mine_m = wires.copy(x, whole(me), mate)
    mine_x.start()
    mine_y.start()
    mine_m.start()
    out[pl.ds(me * rows, rows), :] = x[...]
    pass_y = wires.copy(upper(x_seat), upper(x_seat), along_y)
    pass_x = wires.copy(lower(y_seat), lower(y_seat), along_x)
    mate_x = wires.copy(whole(x_seat), whole(x_seat), mate)
    mate_y = wires.copy(whole(y_seat), whole(y_seat), mate)
    mate_u = wires.copy(upper(far), upper(far), mate)
    mate_l = wires.copy(lower(far), lower(far), mate)
    mine_x.wait_recv()
    pass_y.start()
    mate_x.start()
    mine_y.wait_recv()
    pass_x.start()
    mate_y.start()
    pass_y.wait_recv()
    mate_u.start()
    pass_x.wait_recv()
    mate_l.start()
    for copy in (mine_m, mate_x, mate_y, mate_u, mate_l):
        copy.wait_recv()
    for copy in (mine_x, mine_y, mine_m, pass_y, pass_x, mate_x, mate_y, mate_u, mate_l):
        copy.wait_send()


def plane_gather_kernel(x, out, send, recv):
    y, f, core, mate, along_x, along_y = seats()
    greet([mate, along_x, along_y])
    gather_plane_steps(Wires(send, recv), x, out)


def plane_gather(x, name_id):
    shape = jax.ShapeDtypeStruct((8 * x.shape[0], x.shape[1]), x.dtype)
    return remote_call(plane_gather_kernel, name_id, shape, [], 9, (x,))


def scatter_plane_steps(wires, part, out, own, from_mate, from_x, from_y, last, relay, fill=None):
    rows = out.shape[0]
    half = rows // 2
    y, f, core, mate, along_x, along_y = seats()
    x_f = lax.rem(f + 2, 4)
    turn = 1 - 2 * core
    seat = [(1 - y) * 4 + x_f, y * 4 + x_f, (1 - y) * 4 + f, y * 4 + f]
    upper, lower = slice(0, half), slice(half, rows)
    to_mate = [
        wires.copy(part.at[pl.ds((s + turn) * rows, rows)], from_mate.at[i], mate)
        for i, s in enumerate(seat)
    ]
    for copy in to_mate:
        copy.start()
    far_x = wires.copy(own.at[0, upper], from_x.at[0], along_x)
    far_y = wires.copy(own.at[0, lower], from_y.at[0], along_y)
    near_x = wires.copy(own.at[1, upper], from_x.at[1], along_x)
    near_y = wires.copy(own.at[2, lower], from_y.at[1], along_y)
    relay_y = wires.copy(relay.at[0], last.at[0], along_y)
    relay_x = wires.copy(relay.at[1], last.at[1], along_x)
    starts = ([far_x, far_y], [near_x], [near_y], [])
    for i in range(4):
        to_mate[i].wait_recv()
        own[i] = part[pl.ds(seat[i] * rows, rows), :] + from_mate[i]
        for copy in starts[i]:
            copy.start()
    if fill is not None:
        fill()
    far_x.wait_recv()
    relay[0] = own[2, upper] + from_x[0]
    relay_y.start()
    far_y.wait_recv()
    relay[1] = own[1, lower] + from_y[0]
    relay_x.start()
    near_x.wait_recv()
    near_y.wait_recv()
    relay_y.wait_recv()
    relay_x.wait_recv()
    add = lambda a, b, c: (a.astype(f32) + b.astype(f32) + c.astype(f32)).astype(out.dtype)
    out[upper, :] = add(own[3, upper], from_x[1], last[0])
    out[lower, :] = add(own[3, lower], from_y[1], last[1])
    for copy in to_mate + [far_x, far_y, near_x, near_y, relay_y, relay_x]:
        copy.wait_send()


def plane_scatter_kernel(part, out, own, from_mate, from_x, from_y, last, relay, send, recv):
    greet(seats()[3:])
    wires = Wires(send, recv)
    scatter_plane_steps(wires, part, out, own, from_mate, from_x, from_y, last, relay)


def plane_scatter(part, name_id):
    rows, width = part.shape[0] // 8, part.shape[1]
    shape = jax.ShapeDtypeStruct((rows, width), part.dtype)
    buffer = lambda count, depth: pltpu.VMEM((count, depth, width), part.dtype)
    scratch = [buffer(4, rows), buffer(4, rows)] + [buffer(2, rows // 2)] * 4
    return remote_call(plane_scatter_kernel, name_id, shape, scratch, 10, (part,))


def take_columns(weight, first, width):
    begin = min(first // LANES * LANES, weight.shape[1] - 2 * LANES)
    window = weight[:, begin : begin + 2 * LANES].astype(f32)
    shift = (2 * LANES - (first - begin)) % (2 * LANES)
    window = (pltpu.roll(window, shift, 1) if shift else window)[:, :LANES]
    lane = lax.broadcasted_iota(jnp.int32, window.shape, 1)
    return jnp.where(lane < width, window, 0.0).astype(bf16)


def front_kernel(
    pieces,
    heads,
    x,
    qd,
    ld,
    gain_a,
    gain_f,
    gain_q,
    gain_l,
    qup,
    lup,
    seg_col,
    seg_row,
    freq,
    lat,
    wq,
    wl,
    w_in,
    raw_out,
    n_out,
    gains_out,
    cos_out,
    sin_out,
    w,
    gains,
    gains_all,
    qpack,
    own,
    send,
    recv,
):
    rows = w.shape[0]
    half = rows // 2
    piece = half // pieces
    span = x.shape[0]
    length = cos_out.shape[0]
    y, f, core, mate, along_x, along_y = seats()
    x_f = lax.rem(f + 2, 4)
    m_f = f + 1 - 2 * core
    c_f = 3 - f
    cross = {"fsdp": c_f}
    wires = Wires(send, recv)

    w[:, :QR] = qd[...]
    w[:, QR:] = jnp.zeros((rows, PACK - QR), bf16)
    w[:, QR:DOWN] = ld[...]
    gains[...] = jnp.zeros_like(gains)
    gains[0:1, : gain_a.shape[1]] = gain_a[...].astype(f32)
    gains[1:2, : gain_f.shape[1]] = gain_f[...].astype(f32)
    gains[2:3, : gain_q.shape[1]] = gain_q[...].astype(f32)
    gains[3:4, : gain_l.shape[1]] = gain_l[...].astype(f32)
    greet([mate, along_x, along_y, cross])

    gains_x = wires.copy(gains, gains_all.at[f], along_x)
    gains_m = wires.copy(gains, gains_all.at[f], mate)
    gains_r = wires.copy(gains_all.at[x_f], gains_all.at[x_f], mate)
    spot = lambda owner, side, i: pl.ds(owner * rows + side * half + i * piece, piece)
    across = [
        wires.copy(w.at[pl.ds(y * half + i * piece, piece)], w_in.at[spot(f, y, i)], along_x)
        for i in range(pieces)
    ]
    mine = wires.copy(w, w_in.at[pl.ds(f * rows, rows)], mate)
    same = lambda side, peer: [
        wires.copy(w_in.at[spot(x_f, side, i)], w_in.at[spot(x_f, side, i)], peer)
        for i in range(pieces)
    ]
    trade = same(y, along_y)
    to_mate = same(y, mate)
    rest = same(1 - y, mate)
    gains_x.start()
    gains_m.start()
    for copy in across:
        copy.start()
    mine.start()
    gains_all[f] = gains[...]
    w_in[pl.ds(f * rows, rows), :] = w[...]

    q_rows, l_rows = qup.shape[0], lup.shape[0]
    for seat in range(4):
        for head in range(heads):
            first = lambda ctx: ((seat * 2 + ctx) * heads + head) * (DN + DR)
            column = jnp.where(
                y == 0,
                take_columns(qup, first(0), DN + DR).astype(f32),
                take_columns(qup, first(1), DN + DR).astype(f32),
            )
            qpack[seat, :, head * LANES : (head + 1) * LANES] = column.astype(bf16)
    width = heads * LANES
    kv_part = lambda seat: lup.at[:, pl.ds(pl.multiple_of((seat * 2 + y) * width, LANES), width)]
    q_spot = wq.at[pl.ds(f * q_rows, q_rows)]
    l_spot = wl.at[pl.ds(f * l_rows, l_rows)]
    swaps = []
    for seat, peer in ((x_f, along_x), (c_f, cross), (m_f, mate)):
        swaps.append(wires.copy(qpack.at[seat], q_spot, peer))
        swaps.append(wires.copy(kv_part(seat), l_spot, peer))
    for copy in swaps:
        copy.start()
    wq[pl.ds(f * q_rows, q_rows), :] = qpack[f]
    wl[pl.ds(f * l_rows, l_rows), :] = lup[
        :, pl.ds(pl.multiple_of((f * 2 + y) * width, LANES), width)
    ]

    index = lax.broadcasted_iota(jnp.int32, (length, 1), 0).astype(f32)
    seg = seg_col[...]
    doc_start = jnp.zeros((length, 1), f32)
    for number in range(1, 4):
        start = jnp.sum((seg_row[...] < number).astype(f32), axis=1, keepdims=True)
        doc_start = jnp.where(seg == number, start, doc_start)
    theta = (index - doc_start) * freq[...]
    lane = lax.broadcasted_iota(jnp.int32, (length, LANES), 1)
    turned = (lane >= DN) & (lane < DN + DR)
    cos_out[...] = jnp.where(turned, jnp.cos(theta), jnp.where(lane < DN, 1.0, 0.0))
    sin_out[...] = jnp.where(turned, jnp.sin(theta), 0.0)

    gains_x.wait_recv()
    gains_r.start()
    gains_m.wait_recv()
    gains_r.wait_recv()
    shard = gain_a.shape[1]
    full = [gains_all[i] for i in range(4)]
    g_attn = jnp.concatenate([full[i][0:1, :shard] for i in range(4)], axis=1)
    g_ffn = jnp.concatenate([full[i][1:2, :shard] for i in range(4)], axis=1)
    placed = [full[0]]
    for i in range(1, 4):
        placed.append(pltpu.roll(full[i], i * gain_q.shape[1], 1))
    g_query = sum(p[2:3] for p in placed)
    placed = [full[0]]
    for i in range(1, 4):
        placed.append(pltpu.roll(full[i], i * gain_l.shape[1], 1))
    g_latent = sum(p[3:4] for p in placed)[:, :KR]
    gains_out[...] = jnp.zeros_like(gains_out)
    gains_out[0:1, :] = g_attn
    gains_out[1:2, :] = g_ffn
    gains_out[2:3, :QR] = g_query
    gains_out[3:4, :KR] = g_latent

    inputs = x[...].astype(f32)
    n_out[...] = normalize(inputs, g_attn).astype(bf16)

    def term(owner):
        left = n_out[:, pl.ds(pl.multiple_of(owner * rows, LANES), rows)]
        return dot(left, w_in[pl.ds(owner * rows, rows), :])

    raw_out[...] = term(f)
    for i in range(pieces):
        across[i].wait_recv()
        trade[i].start()
        to_mate[i].start()
    mine.wait_recv()
    raw_out[...] += term(m_f)
    for i in range(pieces):
        trade[i].wait_recv()
        rest[i].start()
    raw_out[...] += term(x_f)
    for copy in to_mate + rest:
        copy.wait_recv()
    raw_out[...] += term(c_f)

    me = y * 4 + f
    cos = cos_out[pl.ds(me * span, span), :]
    sin = sin_out[pl.ds(me * span, span), :]
    own[:, :QR] = normalize(raw_out[:, :QR], g_query).astype(bf16)
    own[:, QR : QR + KR] = normalize(raw_out[:, QR : QR + KR], g_latent).astype(bf16)
    rope = pltpu.roll(raw_out[:, QR + KR :], DN, 1)
    own[:, QR + KR :] = (rope * cos - swapped(rope) * sin).astype(bf16)
    gather_plane_steps(wires, own, lat)

    for copy in swaps:
        copy.wait_recv()
    for copy in [gains_x, gains_m, gains_r, mine] + across + trade + to_mate + rest + swaps:
        copy.wait_send()


def front(x, qd, ld, gains, qup, lup, seg_col, seg_row, heads, name_id):
    freq = ROPE_BASE ** (-np.arange(DR // 2, dtype=np.float32) / (DR // 2))
    freq = np.concatenate([np.zeros(DN), freq, freq, np.zeros(LANES - DN - DR)])
    freq = jnp.asarray(freq[None], f32)
    span, length = x.shape[0], seg_col.shape[0]
    rows, width = qd.shape[0], heads * LANES
    shape = jax.ShapeDtypeStruct
    shapes = (
        shape((length, PACK), bf16),
        shape((QR, width), bf16),
        shape((KR, width), bf16),
        shape((4 * rows, PACK), bf16),
        shape((span, PACK), f32),
        shape((span, D), bf16),
        shape((8, D), f32),
        shape((length, LANES), f32),
        shape((length, LANES), f32),
    )
    pieces = 4
    scratch = [
        pltpu.VMEM((rows, PACK), bf16),
        pltpu.VMEM((8, QR), f32),
        pltpu.VMEM((4, 8, QR), f32),
        pltpu.VMEM((4, qup.shape[0], width), bf16),
        pltpu.VMEM((span, PACK), bf16),
    ]
    operands = (x, qd, ld) + tuple(g[None] for g in gains) + (qup, lup, seg_col, seg_row, freq)
    return remote_call(
        functools.partial(front_kernel, pieces, heads),
        name_id,
        shapes,
        scratch,
        4 + 4 * pieces + 6 + 9,
        operands,
    )


def ffn_group_kernel(
    columns,
    x,
    cot_all,
    w_gu,
    w_down,
    h_out,
    g_out,
    gx_out,
    y_keep,
    y_send,
    x_all,
    wg,
    wd,
    xs,
    cs,
    hv,
    gv,
    ht,
    gt,
    gx_part,
    y_part,
    g_mate,
    y_mate,
    sent,
    from_x,
    local,
    send,
    recv,
):
    units = wd.shape[0]
    span = x.shape[0]
    block = 2 * span
    width = D // columns
    y, f, core, mate, along_x, along_y = seats()
    group = y * 4 * span
    chip = lax.div(f, 2)
    load_gu = pltpu.make_async_copy(w_gu, wg, local.at[0])
    load_down = pltpu.make_async_copy(w_down, wd, local.at[1])
    load_gu.start()
    load_down.start()
    load_cot = []
    for at, which in enumerate((chip, 1 - chip)):
        where = pl.ds(pl.multiple_of(group + which * block, LANES), block)
        load_cot.append(pltpu.make_async_copy(cot_all.at[where], cs.at[at], local.at[6 + at]))
        load_cot[at].start()
    greet([mate, along_x, along_y])
    wires = Wires(send, recv)
    x_f = lax.rem(f + 2, 4)
    me, y_seat, far = y * 4 + f, (1 - y) * 4 + f, (1 - y) * 4 + x_f
    half = span // 2
    place = lambda seat, first, rows: x_all.at[
        pl.ds(pl.multiple_of(seat * span + first, 16), rows)
    ]
    mine = pl.ds(core * span, span)
    other = pl.ds((1 - core) * span, span)
    x_x = wires.copy(x, xs.at[1, mine], along_x)
    x_m = wires.copy(x, xs.at[0, mine], mate)
    x_x.start()
    x_m.start()
    xs[0, mine] = x[...]
    x_r = wires.copy(xs.at[1, mine], xs.at[1, mine], mate)
    x_y = wires.copy(x, place(me, 0, span), along_y)
    x_y.start()
    pass_y = wires.copy(
        xs.at[1, pl.ds(core * span, half)], place(y * 4 + x_f, 0, half), along_y
    )
    pass_x = wires.copy(place(y_seat, half, half), place(y_seat, half, half), along_x)
    mate_y = wires.copy(place(y_seat, 0, span), place(y_seat, 0, span), mate)
    mate_u = wires.copy(place(far, 0, half), place(far, 0, half), mate)
    mate_l = wires.copy(place(far, half, half), place(far, half, half), mate)
    keep_x = [
        pltpu.make_async_copy(
            xs.at[at], place(y * 4 + which * 2, 0, block), local.at[8 + at]
        )
        for at, which in enumerate((chip, 1 - chip))
    ]
    y_m = [wires.copy(y_part.at[i, other], y_mate.at[i], mate) for i in range(2)]
    cols = [slice(i * width, (i + 1) * width) for i in range(columns)]
    to_mate = lambda at: [
        wires.copy(gx_part.at[at, other, c], g_mate.at[at, :, c], mate) for c in cols
    ]
    g_near, g_far = to_mate(0), to_mate(1)
    g_x = [wires.copy(sent.at[:, c], from_x.at[:, c], along_x) for c in cols]

    cut = units // 2 // LANES * LANES

    def hidden(at):
        tokens = slice(at * block, (at + 1) * block)
        for rows in (slice(0, cut), slice(cut, units)):
            gate = dot(wg[0, rows, :], xs[at], NT)
            upper = dot(wg[1, rows, :], xs[at], NT)
            grad = dot(wd[rows, :], cs[at], NT) * RESIDUAL_SCALE
            sigma = jax.nn.sigmoid(gate)
            silu = gate * sigma
            value = silu * upper
            hv[at, rows, :] = value.astype(bf16)
            ht[tokens, rows] = value.T.astype(bf16)
            value = grad * upper * sigma * (1.0 + gate * (1.0 - sigma))
            gv[at, 0, rows, :] = value.astype(bf16)
            gt[0, tokens, rows] = value.T.astype(bf16)
            value = grad * silu
            gv[at, 1, rows, :] = value.astype(bf16)
            gt[1, tokens, rows] = value.T.astype(bf16)
        which = chip if at == 0 else 1 - chip
        where = pl.ds(pl.multiple_of(group + which * block, LANES), block)
        out_h = pltpu.make_async_copy(hv.at[at], h_out.at[:, where], local.at[2 + 2 * at])
        out_g = pltpu.make_async_copy(gv.at[at], g_out.at[:, :, where], local.at[3 + 2 * at])
        out_h.start()
        out_g.start()
        return [out_h, out_g]

    load_gu.wait()
    load_down.wait()
    x_m.wait_recv()
    for copy in load_cot:
        copy.wait()
    stores = hidden(0)
    x_x.wait_recv()
    x_r.start()
    pass_y.start()
    x_y.wait_recv()
    pass_x.start()
    mate_y.start()
    x_r.wait_recv()
    for copy in keep_x:
        copy.start()
    stores += hidden(1) + keep_x

    def pass_on(i):
        g_far[i].wait_recv()
        sent[:, cols[i]] = gx_part[1, mine, cols[i]] + g_mate[1, :, cols[i]]
        g_x[i].start()

    for i, c in enumerate(cols):
        total = dot(gt[0], wg[0, :, c]) + dot(gt[1], wg[1, :, c])
        gx_part[:, :, c] = total.astype(bf16).reshape(2, block, width)
        g_far[i].start()
        g_near[i].start()
        if i > 0:
            pass_on(i - 1)
    pass_y.wait_recv()
    mate_u.start()
    pass_x.wait_recv()
    mate_l.start()
    for i, c in enumerate(cols):
        y_part[:, :, c] = dot(ht[...], wd[:, c]).astype(bf16).reshape(2, block, width)
        if i == 0:
            pass_on(columns - 1)
    for copy in y_m:
        copy.start()
    for i, c in enumerate(cols):
        g_near[i].wait_recv()
        g_x[i].wait_recv()
        keep = gx_part[0, mine, c].astype(f32) + g_mate[0, :, c].astype(f32)
        gx_out[:, c] = (keep + from_x[:, c].astype(f32)).astype(bf16)
    for copy in y_m:
        copy.wait_recv()
    y_keep[...] = y_part[0, mine] + y_mate[0]
    y_send[...] = y_part[1, mine] + y_mate[1]
    for copy in (mate_y, mate_u, mate_l):
        copy.wait_recv()
    plane = [x_y, pass_y, pass_x, mate_y, mate_u, mate_l]
    for copy in [x_x, x_m, x_r] + y_m + g_near + g_far + g_x + plane:
        copy.wait_send()
    for copy in stores:
        copy.wait()


def ffn_group(x, cot_all, w_gu, w_down, name_id):
    tokens = cot_all.shape[0]
    span = x.shape[0]
    units = w_down.shape[0]
    columns = 5
    wires = 11 + 3 * columns
    anywhere = pl.BlockSpec(memory_space=pl.ANY)
    vmem = pl.BlockSpec(memory_space=pltpu.VMEM)
    buffer = lambda *shape: pltpu.VMEM(shape, bf16)
    return pl.pallas_call(
        functools.partial(ffn_group_kernel, columns),
        out_shape=ffn_shapes(units, tokens)
        + [jax.ShapeDtypeStruct((span, D), bf16)] * 3
        + [jax.ShapeDtypeStruct((tokens, D), bf16)],
        in_specs=[vmem, anywhere, anywhere, anywhere],
        out_specs=[anywhere, anywhere, vmem, vmem, vmem, anywhere],
        scratch_shapes=[
            buffer(2, units, D),
            buffer(units, D),
            buffer(2, 2 * span, D),
            buffer(2, 2 * span, D),
            buffer(2, units, 2 * span),
            buffer(2, 2, units, 2 * span),
            buffer(4 * span, units),
            buffer(2, 4 * span, units),
            buffer(2, 2 * span, D),
            buffer(2, 2 * span, D),
            buffer(2, span, D),
            buffer(2, span, D),
            buffer(span, D),
            buffer(span, D),
            pltpu.SemaphoreType.DMA((10,)),
            pltpu.SemaphoreType.DMA((wires,)),
            pltpu.SemaphoreType.DMA((wires,)),
        ],
        compiler_params=pltpu.CompilerParams(
            collective_id=name_id, has_side_effects=True, vmem_limit_bytes=62 * MIB
        ),
        cost_estimate=pl.CostEstimate(
            flops=12 * 4 * span * units * D, bytes_accessed=6 * units * D, transcendentals=0
        ),
    )(x, cot_all, w_gu, w_down)


def ffn_others_kernel(
    span,
    x_z,
    cot_z,
    x_far,
    cot_far,
    x_in,
    cot_in,
    h_in,
    g_in,
    w_gu,
    w_down,
    x_all,
    cot_all,
    h_out,
    g_out,
    wg,
    wd,
    xb,
    cb,
    hb,
    gb,
    stage,
    loads,
    local,
    slots_in,
    slots_out,
    send,
    recv,
):
    length = 8 * span
    block = 2 * span
    y = lax.axis_index("ctx")
    load_gu = pltpu.make_async_copy(w_gu, wg, loads.at[0])
    load_down = pltpu.make_async_copy(w_down, wd, loads.at[1])
    load_gu.start()
    load_down.start()
    greet(seats()[3:])
    wires = Wires(send, recv)
    def unit(r, own, far, out, at):
        z = turn_z(r)
        return Light(
            wires, own.at[z], far.at[z], stage.at[at], out, r * length, local.at[at]
        )

    x_unit = {r: unit(r, x_z, x_far, x_all, r - 2) for r in (2, 3)}
    c_unit = {r: unit(r, cot_z, cot_far, cot_all, r) for r in (2, 3)}
    for one in (x_unit[2], c_unit[2], x_unit[3], c_unit[3]):
        one.load()
    x_unit[2].start()
    c_unit[2].start()

    def where(i):
        first = jnp.where(i < 2, (1 - y) * 4 * span + i * block, length + (i - 2) * block)
        return pl.ds(pl.multiple_of(first, LANES), block)

    def fetch(i):
        slot = lax.rem(i, 2)
        return [
            pltpu.make_async_copy(x_all.at[where(i)], xb.at[slot], slots_in.at[0, slot]),
            pltpu.make_async_copy(cot_all.at[where(i)], cb.at[slot], slots_in.at[1, slot]),
        ]

    def store(i):
        slot = lax.rem(i, 2)
        return [
            pltpu.make_async_copy(hb.at[slot], h_out.at[:, where(i)], slots_out.at[0, slot]),
            pltpu.make_async_copy(gb.at[slot], g_out.at[:, :, where(i)], slots_out.at[1, slot]),
        ]

    count = 14
    for copy in fetch(0):
        copy.start()
    load_gu.wait()
    load_down.wait()

    def step(i, carry):
        slot = lax.rem(i, 2)
        for copy in fetch(i):
            copy.wait()

        @pl.when(i >= 2)
        def _():
            for copy in store(i - 2):
                copy.wait()

        def between(number, *steps):
            @pl.when(i == number)
            def _():
                for one in steps:
                    one()

        between(3, x_unit[2].relay, c_unit[2].relay, x_unit[3].start)
        between(4, c_unit[3].start)
        between(5, x_unit[2].finish, c_unit[2].finish)
        between(8, x_unit[3].relay, c_unit[3].relay)
        between(9, x_unit[3].finish, c_unit[3].finish)

        @pl.when(i + 1 < count)
        def _():
            for copy in fetch(i + 1):
                copy.start()

        hidden_block(xb[slot], cb[slot], wg, wd, hb.at[slot], gb.at[slot], 2)
        for copy in store(i):
            copy.start()
        return carry

    lax.fori_loop(0, count, step, 0)
    for i in (count - 2, count - 1):
        for copy in store(i):
            copy.wait()


def ffn_others(x_z, cot_z, x_far, cot_far, x_all, cot_all, h_all, g_all, w_gu, w_down, name_id):
    units = w_down.shape[0]
    tokens = x_all.shape[0]
    span = x_z.shape[1]
    block = 2 * span
    wires = 4 * Light.wires_needed
    anywhere = pl.BlockSpec(memory_space=pl.ANY)
    buffer = lambda *shape: pltpu.VMEM(shape, bf16)
    return pl.pallas_call(
        functools.partial(ffn_others_kernel, span),
        out_shape=[jax.ShapeDtypeStruct((tokens, D), bf16)] * 2 + ffn_shapes(units, tokens),
        in_specs=[anywhere] * 10,
        out_specs=[anywhere] * 4,
        input_output_aliases={4: 0, 5: 1, 6: 2, 7: 3},
        scratch_shapes=[
            buffer(2, units, D),
            buffer(units, D),
            buffer(2, block, D),
            buffer(2, block, D),
            buffer(2, units, block),
            buffer(2, 2, units, block),
            buffer(4, 2, span, D),
            pltpu.SemaphoreType.DMA((2,)),
            pltpu.SemaphoreType.DMA((4, 4)),
            pltpu.SemaphoreType.DMA((2, 2)),
            pltpu.SemaphoreType.DMA((2, 2)),
            pltpu.SemaphoreType.DMA((wires,)),
            pltpu.SemaphoreType.DMA((wires,)),
        ],
        compiler_params=pltpu.CompilerParams(
            collective_id=name_id, has_side_effects=True, vmem_limit_bytes=60 * MIB
        ),
        cost_estimate=pl.CostEstimate(
            flops=6 * (tokens - 4 * span) * units * D,
            bytes_accessed=6 * units * D + 10 * tokens * D,
            transcendentals=0,
        ),
    )(x_z, cot_z, x_far, cot_far, x_all, cot_all, h_all, g_all, w_gu, w_down)


def norm_back_rows(values, gain, grad):
    inverse = lax.rsqrt(jnp.mean(values * values, axis=-1, keepdims=True) + EPS)
    unit = values * inverse
    scaled = gain * grad
    return (scaled - unit * jnp.mean(unit * scaled, axis=-1, keepdims=True)) * inverse


def finish_kernel(
    gq,
    gkv,
    rope,
    lat,
    wq,
    wl,
    w_in,
    raw,
    n,
    x,
    grad_resid,
    gains,
    cos_all,
    sin_all,
    ffn_gain,
    part,
    input_grad,
    lat_part,
    lat_sum,
    own,
    from_mate,
    from_x,
    from_y,
    last,
    relay,
    n_all,
    ups,
    raw_own,
    raw_all,
    down,
    traded,
    send,
    recv,
):
    span = x.shape[0]
    length = gq.shape[0]
    width = gq.shape[1]
    rows = w_in.shape[0] // 4
    q_rows, l_rows = QR // 4, KR // 4
    y, f, core, mate, along_x, along_y = seats()
    x_f, m_f, c_f = lax.rem(f + 2, 4), f + 1 - 2 * core, 3 - f
    cross = {"fsdp": c_f}
    others = ((x_f, along_x), (c_f, cross), (m_f, mate))
    greet([mate, along_x, along_y, cross])
    wires = Wires(send, recv)
    columns = lambda seat: pl.ds(pl.multiple_of(seat * rows, LANES), rows)
    mine = pl.ds(f * span, span)
    n_sends = [wires.copy(n.at[:, columns(seat)], n_all.at[mine], peer) for seat, peer in others]
    for copy in n_sends:
        copy.start()
    n_all[mine, :] = n[:, columns(f)]

    each = span + EXTRA
    for first in range(0, length, 512):
        some = slice(first, first + 512)
        q_part = dot(gq[some, :], wq[...], NT).astype(bf16)
        l_part = dot(gkv[some, :], wl[...], NT).astype(bf16)
        r_part = rope[some, :].astype(bf16)
        for at in range(0, 512, span):
            here = (first + at) // span * each
            lat_part[here : here + span, :QR] = q_part[at : at + span]
            lat_part[here : here + span, QR : QR + KR] = l_part[at : at + span]
            lat_part[here : here + span, QR + KR :] = r_part[at : at + span]
    for seat in range(8):
        here = seat * each + span
        piece = ffn_gain[:, seat % 4 * rows : (seat % 4 + 1) * rows]
        lat_part[here : here + EXTRA, :] = jnp.zeros((EXTRA, PACK), bf16)
        lat_part[here : here + EXTRA, :rows] = jnp.broadcast_to(piece, (EXTRA, rows)).astype(bf16)

    swap_rows = q_rows + l_rows
    swaps = [
        wires.copy(ups.at[seat], part.at[pl.ds(f * swap_rows, swap_rows)], peer)
        for seat, peer in others
    ]

    def column_gradients():
        q_grad = dot(lat[:, :QR], gq[...], TN).astype(bf16)
        l_grad = dot(lat[:, QR : QR + KR], gkv[...], TN).astype(bf16)
        for seat in range(4):
            ups[seat, :q_rows] = q_grad[seat * q_rows : (seat + 1) * q_rows]
            ups[seat, q_rows:] = l_grad[seat * l_rows : (seat + 1) * l_rows]
        part[pl.ds(f * swap_rows, swap_rows), :] = ups[f]

    scatter_plane_steps(
        wires, lat_part, lat_sum, own, from_mate, from_x, from_y, last, relay, column_gradients
    )

    me = pl.ds((y * 4 + f) * span, span)
    grad = lat_sum[:span, :].astype(f32)
    raw_own[:, :QR] = norm_back_rows(raw[:, :QR], gains[2:3, :QR], grad[:, :QR]).astype(bf16)
    raw_own[:, QR : QR + KR] = norm_back_rows(
        raw[:, QR : QR + KR], gains[3:4, :KR], grad[:, QR : QR + KR]
    ).astype(bf16)
    turned = grad[:, QR + KR :]
    lane = lax.broadcasted_iota(jnp.int32, turned.shape, 1)
    turned = turned * cos_all[me, :] + swapped(turned) * sin_all[me, :]
    turned = jnp.where((lane >= DN) & (lane < DN + DR), turned, 0.0)
    raw_own[:, QR + KR :] = pltpu.roll(turned, LANES - DN, 1).astype(bf16)
    raw_x = wires.copy(raw_own, raw_all.at[mine], along_x)
    raw_m = wires.copy(raw_own, raw_all.at[mine], mate)
    theirs = raw_all.at[pl.ds(x_f * span, span)]
    raw_r = wires.copy(theirs, theirs, mate)
    raw_x.start()
    raw_m.start()
    for copy in swaps:
        copy.start()
    raw_all[mine, :] = raw_own[...]
    for copy in n_sends:
        copy.wait_recv()
    raw_x.wait_recv()
    raw_r.start()
    raw_m.wait_recv()
    raw_r.wait_recv()

    down[...] = dot(n_all[...], raw_all[...], TN).astype(bf16)
    half = rows // 2
    trade = wires.copy(down.at[pl.ds((1 - y) * half, half)], traded, along_y)
    trade.start()
    inputs = x[...].astype(f32)
    grad_in = dot(raw_own[...], w_in[...], NT)
    input_grad[...] = grad_resid[...] + norm_back_rows(inputs, gains[0:1, :], grad_in)
    first = 4 * swap_rows
    last_rows = part.shape[0] - first - 2 * half
    part[first + 2 * half :, :] = jnp.zeros((last_rows, width), bf16)
    part[first + 2 * half :, :rows] = lat_sum[span : span + last_rows, :rows]
    trade.wait_recv()
    kept = down[pl.ds(y * half, half), :] + traded[...]
    part[first : first + half, :] = kept[:, :width]
    part[first + half : first + 2 * half, :] = jnp.zeros((half, width), bf16)
    part[first + half : first + 2 * half, : PACK - width] = kept[:, width:]
    for copy in swaps:
        copy.wait_recv()
    for copy in n_sends + swaps + [raw_x, raw_m, raw_r, trade]:
        copy.wait_send()


def finish(operands, name_id):
    gq, x, w_in = operands[0], operands[9], operands[6]
    span, width, rows = x.shape[0], gq.shape[1], w_in.shape[0] // 4
    part_rows = QR + KR + rows + 16
    each = span + EXTRA
    buffer = lambda *shape: pltpu.VMEM(shape, bf16)
    return remote_call(
        finish_kernel,
        name_id,
        (jax.ShapeDtypeStruct((part_rows, width), bf16), jax.ShapeDtypeStruct((span, D), f32)),
        [
            buffer(8 * each, PACK),
            buffer(each, PACK),
            buffer(4, each, PACK),
            buffer(4, each, PACK),
        ]
        + [buffer(2, each // 2, PACK)] * 4
        + [
            buffer(4 * span, rows),
            buffer(4, (QR + KR) // 4, width),
            buffer(span, PACK),
            buffer(4 * span, PACK),
            buffer(rows, PACK),
            buffer(rows // 2, PACK),
        ],
        20,
        operands,
    )


def gain_grad(gain, pairs):
    return sum(jnp.sum(w.astype(f32) * grad, axis=1) for w, grad in pairs) / gain


def unpack_kernel(
    total, qup, lup, qd, ld, gain_a, gain_q, gain_l, up, lu, out, qg, lg, a_out, q_out, l_out, f_out
):
    width = total.shape[2]
    heads = width // LANES
    q_rows, l_rows = qup.shape[0], lup.shape[0]
    rows = q_rows + l_rows
    each = heads * DV
    base = D // width * each
    lane = lax.broadcasted_iota(jnp.int32, (q_rows, LANES), 1)
    own = DN + DR

    def head(number):
        seat, side = number // (2 * heads), number // heads % 2
        at = number % heads * LANES
        begin = base + seat * rows
        return total[side, begin : begin + q_rows, at : at + LANES].astype(f32)

    turn = lambda values, by: pltpu.roll(values, by % LANES, 1)
    q_sum = jnp.zeros((q_rows, 1), f32)
    for first in range(0, H, 4):
        a, b, c, d = (head(first + i) for i in range(4))
        merged = (
            jnp.where(lane < own, a, turn(b, own)),
            jnp.where(lane < 2 * own - LANES, turn(b, -32), turn(c, 2 * own - LANES)),
            jnp.where(lane < own - DN, turn(c, -DN), turn(d, own - DN)),
        )
        for i, values in enumerate(merged):
            at = first * own + i * LANES
            up[:, at : at + LANES] = values
            q_sum += jnp.sum(values * qup[:, at : at + LANES].astype(f32), axis=1, keepdims=True)
    q_out[...] = q_sum / gain_q[...].astype(f32)
    l_sum = jnp.zeros((l_rows, 1), f32)
    for seat in range(4):
        for side in range(2):
            at = (seat * 2 + side) * width
            first = base + seat * rows + q_rows
            values = total[side, first : first + l_rows, :].astype(f32)
            lu[:, at : at + width] = values
            l_sum += jnp.sum(values * lup[:, at : at + width].astype(f32), axis=1, keepdims=True)
    l_out[...] = l_sum / gain_l[...].astype(f32)
    for part in range(D // width):
        for side in range(2):
            at = part * each
            out[side * each : (side + 1) * each, part * width : (part + 1) * width] = total[
                side, at : at + each, :
            ].astype(f32)
    first = base + 4 * rows
    half = qd.shape[0] // 2
    f_out[...] = total[0, first + 2 * half : first + 2 * half + 1, : f_out.shape[1]].astype(f32)
    for side in range(2):
        mine = slice(side * half, (side + 1) * half)
        left = total[side, first : first + half, :].astype(f32)
        right = total[side, first + half : first + 2 * half, : PACK - width].astype(f32)
        qg[mine, :width] = left
        qg[mine, width:] = right[:, : QR - width]
        lg[mine, :] = right[:, QR - width : DOWN - width]
        weighted = jnp.sum(left * qd[mine, :width].astype(f32), axis=1, keepdims=True)
        weighted += jnp.sum(
            right[:, : QR - width] * qd[mine, width:].astype(f32), axis=1, keepdims=True
        )
        weighted += jnp.sum(
            right[:, QR - width : DOWN - width] * ld[mine, :].astype(f32), axis=1, keepdims=True
        )
        a_out[mine, :] = weighted / gain_a[mine, :].astype(f32)


def unpack(total, qup, lup, qd, ld, gain_a, gain_q, gain_l):
    shape = lambda *dims: jax.ShapeDtypeStruct(dims, f32)
    rows = lambda weight: weight.shape[0]
    return pl.pallas_call(
        unpack_kernel,
        out_shape=(
            shape(*qup.shape),
            shape(*lup.shape),
            shape(rows(qd), D),
            shape(*qd.shape),
            shape(*ld.shape),
            shape(rows(qd), 1),
            shape(rows(qup), 1),
            shape(rows(lup), 1),
            shape(1, rows(qd)),
        ),
        compiler_params=pltpu.CompilerParams(vmem_limit_bytes=60 * MIB),
        cost_estimate=pl.CostEstimate(flops=0, bytes_accessed=24 * MIB, transcendentals=0),
    )(total, qup, lup, qd, ld, gain_a[:, None], gain_q[:, None], gain_l[:, None])


def body(
    layer_input,
    segment_ids,
    attn_gain,
    query_down,
    query_gain,
    query_up,
    latent_down,
    latent_gain,
    latent_up,
    attn_output,
    ffn_gain,
    gate_up,
    down_proj,
    cotangent,
):
    span = layer_input.shape[1]
    length = segment_ids.shape[1]
    n_f = lax.axis_size("fsdp")
    n_c = lax.axis_size("ctx")
    n_h = n_c if H % (n_f * n_c) == 0 else 1
    square = n_f == 4 and n_c == 2 and lax.axis_size("dp") == 4
    heads = H // (n_f * n_h)
    ctx = lax.axis_index("ctx") if n_h > 1 else 0
    fsdp = lax.axis_index("fsdp")
    group = lax.axis_index(("dp", "ctx"))
    place = jnp.reshape(group, (1,)).astype(jnp.int32)
    offset = lax.axis_index(PLANE) * span

    seg = segment_ids[0]
    seg_col = seg[:, None]
    seg_row = seg[None, :]
    own_q = heads * (DN + DR)
    own_kv = heads * (DN + DV)

    def own_columns(weight, width):
        rows = weight.shape[0]
        parts = weight.reshape(rows, n_f, n_h, width)
        parts = lax.dynamic_index_in_dim(parts, ctx, 2, keepdims=False)
        parts = jnp.transpose(parts, (1, 0, 2))
        return lax.all_to_all(parts, "fsdp", 0, 0, tiled=False).reshape(rows * n_f, width)

    wo = lax.dynamic_slice_in_dim(attn_output, ctx * heads * DV, heads * DV, 0)
    wo = jnp.pad(wo.reshape(heads, DV, D), ((0, 0), (LANES - DV, 0), (0, 0)))
    wo = wo.reshape(heads * LANES, D)
    def gather_plane(shard, name_id):
        if square:
            return plane_gather(shard, name_id)
        return lax.all_gather(shard, PLANE, axis=0, tiled=True)

    def scatter_plane(part, name_id):
        if square:
            return plane_scatter(part, name_id)
        if n_h > 1:
            return lax.psum_scatter(part, PLANE, scatter_dimension=0, tiled=True)
        half = length // n_c
        part = lax.dynamic_slice_in_dim(part, lax.axis_index("ctx") * half, half, 0)
        return lax.psum_scatter(part, "fsdp", scatter_dimension=0, tiled=True)

    def gather_heads(part):
        return lax.all_gather(part, "ctx", axis=0) if n_h > 1 else part[None]

    inputs = layer_input[0].astype(f32)
    grad_out = cotangent[0].astype(f32)
    if square:
        lat, wq, wl, w_down_in, raw, normed_in, gains, cos_all, sin_all = front(
            layer_input[0],
            query_down,
            latent_down,
            (attn_gain, ffn_gain, query_gain, latent_gain),
            query_up,
            latent_up,
            seg_col,
            seg_row,
            heads,
            1,
        )
        g_attn, g_ffn, g_query, g_latent = gains[0], gains[1], gains[2, :QR], gains[3, :KR]
    else:
        gather = lambda shard: lax.all_gather(shard, "fsdp", axis=0, tiled=True)
        g_attn, g_ffn, g_query, g_latent = (
            gather(g).astype(f32) for g in (attn_gain, ffn_gain, query_gain, latent_gain)
        )
        blank = jnp.zeros((query_down.shape[0], PACK - DOWN), bf16)
        w_down_in = gather(jnp.concatenate([query_down, latent_down, blank], axis=1))
        wq = own_columns(query_up, own_q).reshape(QR, heads, DN + DR)
        wq = jnp.pad(wq, ((0, 0), (0, 0), (0, LANES - DN - DR))).reshape(QR, heads * LANES)
        wl = own_columns(latent_up, own_kv)
        starts = [jnp.sum((seg < number).astype(jnp.int32)) for number in range(4)]
        doc_start = sum(jnp.where(seg == number, starts[number], 0) for number in range(1, 4))
        cosine, sine = angles((jnp.arange(length, dtype=jnp.int32) - doc_start).astype(f32))
        ones = jnp.ones((length, DN), f32)
        rest = jnp.zeros((length, LANES - DN - DR), f32)
        cos_all = jnp.concatenate([ones, cosine, cosine, rest], axis=1)
        sin_all = jnp.concatenate([0.0 * ones, sine, sine, rest], axis=1)
        cos_own = lax.dynamic_slice_in_dim(cosine, offset, span, 0)
        sin_own = lax.dynamic_slice_in_dim(sine, offset, span, 0)
        normed_in = normalize(inputs, g_attn).astype(bf16)
        raw = dot(normed_in, w_down_in)
        query_normed = normalize(raw[:, :QR], g_query).astype(bf16)
        latent = normalize(raw[:, QR : QR + KR], g_latent).astype(bf16)
        key_rope = rotate(raw[:, QR + KR : DOWN], cos_own, sin_own).astype(bf16)
        key_rope = jnp.pad(key_rope, ((0, 0), (DN, LANES - DN - DR)))
        lat = jnp.concatenate([query_normed, latent, key_rope], axis=1)
        lat = lax.all_gather(lat, PLANE, axis=0, tiled=True)
    query_latent = raw[:, :QR]
    latent_pre = raw[:, QR : QR + KR]
    operands = (lat, wq, wl, cos_all, sin_all, seg_col, seg_row)
    if square:
        cot_z = lax.all_gather(cotangent[0], "dp", axis=0)
        q, k, kv, o, lse, cot_all = attend(*operands, cotangent[0], 4 * length, 2)
        diagonal = ((1 - ctx) * 4 + (fsdp + 2) % 4) * span
        cot_far = lax.all_gather(
            lax.dynamic_slice(cot_all, (diagonal, 0), (span, D)), "dp", axis=0
        )
    else:
        cot_all = lax.all_gather(cotangent[0], ALL, axis=0, tiled=True)
        q, k, kv, o, lse = attend(*operands)
    branch = scatter_plane(dot(o, wo).astype(bf16), 3)
    resid = inputs + RESIDUAL_SCALE * branch.astype(f32)

    ffn_in = normalize(resid, g_ffn).astype(bf16)
    own = n_f * span
    if square:
        ffn_in, cot_z = lax.optimization_barrier((ffn_in, cot_z))
        x_z = lax.all_gather(ffn_in, "dp", axis=0)
        h_all, g_all, gx, y_keep, y_send, x_all = ffn_group(
            ffn_in, cot_all, gate_up, down_proj, 4
        )
        x_far = lax.all_gather(lax.dynamic_slice(x_all, (diagonal, 0), (span, D)), "dp", axis=0)
    else:
        x_own = lax.all_gather(ffn_in, "fsdp", axis=0, tiled=True)
        h_all, g_all, y_part, gx_part = ffn_own(place, x_own, cot_all, gate_up, down_proj)
        gx = lax.psum_scatter(gx_part, "fsdp", scatter_dimension=0, tiled=True)
        y = lax.psum_scatter(y_part, "fsdp", scatter_dimension=0, tiled=True).astype(f32)
    gx = gx.astype(f32)
    grad_resid_add, ffn_gain_part = norm_back(resid, g_ffn, gx)
    grad_resid = grad_out + grad_resid_add
    gb = (RESIDUAL_SCALE * grad_resid).astype(bf16)
    if square:
        gb, cot_far = lax.optimization_barrier((gb, cot_far))
    gb = gather_plane(gb, 6)
    operands = (gb, wo, q, k, kv, o, lse, cos_all, sin_all, seg_col, seg_row)
    if square:
        bulk = (x_z, cot_z, cot_far, x_all, cot_all)
        gq, gkv, rope, out_part, x_all, cot_all = attend_back(*operands, bulk, 4 * length, 9)
        rope, out_part, x_z, x_far = lax.optimization_barrier((rope, out_part, x_z, x_far))
        width = heads * LANES
        out_part = [out_part[:, at : at + width] for at in range(0, D, width)]
        out_total = lax.psum(jnp.concatenate(out_part[:-1], axis=0), "dp")
    else:
        x_all = lax.all_gather(ffn_in, ALL, axis=0, tiled=True)
        gq, gkv, rope, out_part = attend_back(*operands)
    width = heads * LANES
    q_rows, l_rows = QR // n_f, KR // n_f
    if square:
        part, input_grad = finish(
            (
                gq,
                gkv,
                rope,
                lat,
                wq,
                wl,
                w_down_in,
                raw,
                normed_in,
                layer_input[0],
                grad_resid,
                gains,
                cos_all,
                sin_all,
                ffn_gain_part[None],
            ),
            7,
        )
    else:
        lat_part = jnp.concatenate([dot(gq, wq, NT), dot(gkv, wl, NT), rope], axis=1).astype(bf16)
        extra = jnp.pad(ffn_gain_part.astype(bf16).reshape(n_f, -1), ((0, 0), (0, PACK - D // n_f)))
        extra = jnp.broadcast_to(extra[None, :, None], (n_c, n_f, EXTRA, PACK))
        extra = extra.reshape(n_c * n_f, EXTRA, PACK)
        lat_part = jnp.concatenate([lat_part.reshape(n_c * n_f, span, PACK), extra], axis=1)
        lat_sum = scatter_plane(lat_part.reshape(-1, PACK), 7).astype(f32)
        lat_grad = lat_sum[:span]
        ffn_gain_plane = lat_sum[span, : D // n_f]
        query_pre = norm_back(query_latent, g_query, lat_grad[:, :QR])[0]
        latent_back = norm_back(latent_pre, g_latent, lat_grad[:, QR : QR + KR])[0]
        rope_back = unrotate(lat_grad[:, QR + KR + DN : QR + KR + DN + DR], cos_own, sin_own)
        raw_grad = jnp.concatenate(
            [query_pre, latent_back, rope_back, jnp.zeros((span, PACK - DOWN), f32)], axis=1
        ).astype(bf16)
        input_add = norm_back(inputs, g_attn, dot(raw_grad, w_down_in, NT))[0]
        input_grad = grad_resid + input_add

        own_rows = D // n_f
        n_all = lax.all_to_all(
            jnp.transpose(normed_in.reshape(span, n_f, own_rows), (1, 0, 2)), "fsdp", 0, 0
        ).reshape(n_f * span, own_rows)
        raw_all = lax.all_gather(raw_grad, "fsdp", axis=0, tiled=True)
        down_in_part = dot(n_all, raw_all, TN)[:, :DOWN]
        gain_column = ffn_gain_plane[:, None] / n_c
        blank = jnp.zeros((own_rows, PACK - DOWN - 1), f32)
        down_in_part = jnp.concatenate([down_in_part, gain_column, blank], axis=1).astype(bf16)
        width = heads * LANES
        out_part = [out_part[:, at : at + width] for at in range(0, D, width)]
        up_part = dot(lat[:, :QR], gq, TN).astype(bf16).reshape(n_f, -1, width)
        lup_part = dot(lat[:, QR : QR + KR], gkv, TN).astype(bf16).reshape(n_f, -1, width)
        swap = lax.all_to_all(jnp.concatenate([up_part, lup_part], axis=1), "fsdp", 0, 0)
        q_rows, l_rows = QR // n_f, KR // n_f
        pieces = [swap.reshape(-1, width)] + out_part
        part = jnp.concatenate(pieces, axis=0)

    if square:
        part, x_z, y_keep, y_send, out_total = lax.optimization_barrier(
            (part, x_z, y_keep, y_send, out_total)
        )
        total = lax.psum(jnp.concatenate([out_part[-1], part], axis=0), "dp")
        y_far = lax.ppermute(y_send, "fsdp", [(i, (i + 2) % 4) for i in range(4)])
        y = y_keep.astype(f32) + y_far.astype(f32)
        x_all, cot_all, h_all, g_all = ffn_others(
            x_z, cot_z, x_far, cot_far, x_all, cot_all, h_all, g_all, gate_up, down_proj, 10
        )
    else:
        part, x_all = lax.optimization_barrier((part, x_all))
        total = lax.psum(part, "dp")
        h_all, g_all = ffn_rest(place, x_all, cot_all, gate_up, down_proj, h_all, g_all, own)
    output = resid + RESIDUAL_SCALE * y
    if square:
        out_total, total, h_all = lax.optimization_barrier((out_total, total, h_all))
        total = jnp.concatenate([out_total, total], axis=0)
    else:
        total, h_all = lax.optimization_barrier((total, h_all))
    total = gather_heads(total)
    gate_up_grad = lax.dot_general(g_all, x_all, (((2,), (0,)), ((), ())), preferred_element_type=f32)
    down_grad = dot(h_all, cot_all) * RESIDUAL_SCALE

    if square:
        up_grad, lup_grad, out_grad, q_down_grad, l_down_grad, ga, gq, gl, gf = unpack(
            total,
            query_up,
            latent_up,
            query_down,
            latent_down,
            attn_gain,
            query_gain,
            latent_gain,
        )
        gain_grads = [ga[:, 0], gq[:, 0], gl[:, 0], gf[0]]
    else:
        down_in_sum = lax.psum(down_in_part, ("dp", "ctx")).astype(f32)
        swapped_rows = n_f * (q_rows + l_rows)
        both = total[:, :swapped_rows].reshape(n_h, n_f, q_rows + l_rows, heads, LANES)
        up_grad = jnp.transpose(both[:, :, :q_rows, :, : DN + DR], (2, 1, 0, 3, 4))
        up_grad = up_grad.reshape(q_rows, -1).astype(f32)
        lup_grad = jnp.transpose(both[:, :, q_rows:], (2, 1, 0, 3, 4))
        lup_grad = lup_grad.reshape(l_rows, -1).astype(f32)
        out_grad = total[:, swapped_rows:].reshape(n_h, D // width, heads * DV, width)
        out_grad = jnp.transpose(out_grad, (0, 2, 1, 3)).reshape(-1, D).astype(f32)
        q_down_grad = down_in_sum[:, :QR]
        l_down_grad = down_in_sum[:, QR:DOWN]
        downs = [(query_down, q_down_grad), (latent_down, l_down_grad)]
        gain_grads = [
            gain_grad(attn_gain.astype(f32), downs),
            gain_grad(query_gain.astype(f32), [(query_up, up_grad)]),
            gain_grad(latent_gain.astype(f32), [(latent_up, lup_grad)]),
            down_in_sum[:, DOWN],
        ]

    return (
        output.astype(bf16)[None],
        input_grad[None],
        gain_grads[0],
        q_down_grad,
        gain_grads[1],
        up_grad,
        l_down_grad,
        gain_grads[2],
        lup_grad,
        out_grad,
        gain_grads[3],
        gate_up_grad,
        down_grad,
    )


def solution(mesh):
    in_specs = (
        P("dp", ("ctx", "fsdp"), None),
        P("dp", None),
        P("fsdp"),
        P("fsdp", None),
        P("fsdp"),
        P("fsdp", None),
        P("fsdp", None),
        P("fsdp"),
        P("fsdp", None),
        P("fsdp", None),
        P("fsdp"),
        P(None, "fsdp", None),
        P("fsdp", None),
        P("dp", ("ctx", "fsdp"), None),
    )
    out_specs = (
        P("dp", ("ctx", "fsdp"), None),
        P("dp", ("ctx", "fsdp"), None),
        P("fsdp"),
        P("fsdp", None),
        P("fsdp"),
        P("fsdp", None),
        P("fsdp", None),
        P("fsdp"),
        P("fsdp", None),
        P("fsdp", None),
        P("fsdp"),
        P(None, "fsdp", None),
        P("fsdp", None),
    )
    return jax.shard_map(body, mesh=mesh, in_specs=in_specs, out_specs=out_specs, check_vma=False)
```

```python
import functools
import math

import jax
import jax.numpy as jnp
import numpy as np
from jax import lax
from jax.experimental import pallas as pl
from jax.experimental.pallas import tpu as pltpu
from jax.sharding import PartitionSpec as P

D = 2560
H = 40
DN = 64
DR = 32
DV = 64
QR = 768
KR = 256
LANES = 128
DOWN = QR + KR + DR
PACK = QR + KR + LANES
EXTRA = 32

EPS = 1e-05
RESIDUAL_SCALE = 1.4 / math.sqrt(62.0)
NEGATIVE = -1e30
ROPE_BASE = 10000.0
SCALE = (DN + DR) ** (-0.5)
f32 = jnp.float32
bf16 = jnp.bfloat16

NN = (((1,), (0,)), ((), ()))
NT = (((1,), (1,)), ((), ()))
TN = (((0,), (0,)), ((), ()))
MIB = 1024 * 1024


def dot(left, right, dims=NN):
    return lax.dot_general(left, right, dims, preferred_element_type=f32)


def normalize(values, gain):
    return values * lax.rsqrt(jnp.mean(values * values, axis=-1, keepdims=True) + EPS) * gain


def norm_back(values, gain, grad):
    primal, pullback = jax.vjp(normalize, values, gain)
    return pullback(grad)


def angles(positions):
    half = DR // 2
    frequency = ROPE_BASE ** (-jnp.arange(half, dtype=f32) / half)
    theta = positions[:, None] * frequency[None, :]
    return (jnp.cos(theta), jnp.sin(theta))


def rotate(values, cosine, sine):
    half = values.shape[-1] // 2
    first = values[..., :half]
    second = values[..., half:]
    return jnp.concatenate(
        [first * cosine - second * sine, second * cosine + first * sine], axis=-1
    )


def unrotate(grad, cosine, sine):
    return rotate(grad, cosine, -sine)


def swapped(values):
    lane = lax.broadcasted_iota(jnp.int32, values.shape, 1)
    up = pltpu.roll(values, LANES - DR // 2, 1)
    back = pltpu.roll(values, DR // 2, 1)
    return jnp.where(lane < DN + DR // 2, up, -back)


def allowed(seg_col, seg_row, first, rows, columns):
    query = first + lax.broadcasted_iota(jnp.int32, (rows, columns), 0)
    key = lax.broadcasted_iota(jnp.int32, (rows, columns), 1)
    return (seg_col[first : first + rows, :] == seg_row[:, :columns]) & (key <= query)


PLANE = ("ctx", "fsdp")
ALL = ("dp", "ctx", "fsdp")
MESH = pl.DeviceIdType.MESH


def seats():
    y = lax.axis_index("ctx")
    f = lax.axis_index("fsdp")
    core = lax.rem(f, 2)
    mate = {"fsdp": f + 1 - 2 * core}
    along_x = {"fsdp": lax.rem(f + 2, 4)}
    along_y = {"ctx": 1 - y}
    return y, f, core, mate, along_x, along_y


def greet(peers):
    barrier = pltpu.get_barrier_semaphore()
    for peer in peers:
        pl.semaphore_signal(barrier, inc=1, device_id=peer, device_id_type=MESH)
    pl.semaphore_wait(barrier, len(peers))


class Wires:
    def __init__(self, send, recv):
        self.send, self.recv, self.count = send, recv, 0

    def copy(self, src, dst, peer):
        at = self.count
        self.count += 1
        return pltpu.make_async_remote_copy(
            src_ref=src,
            dst_ref=dst,
            send_sem=self.send.at[at],
            recv_sem=self.recv.at[at],
            device_id=peer,
            device_id_type=MESH,
        )


class Spread:
    wires_needed = 9

    def __init__(self, wires, src, out, base, local):
        rows = src.shape[0]
        half = rows // 2
        y, f, core, mate, along_x, along_y = seats()
        x_f = lax.rem(f + 2, 4)
        me, x_seat, y_seat, far = y * 4 + f, y * 4 + x_f, (1 - y) * 4 + f, (1 - y) * 4 + x_f
        at = lambda seat, first, count: out.at[
            pl.ds(pl.multiple_of(base + seat * rows + first, 16), count)
        ]
        whole = lambda seat: at(seat, 0, rows)
        upper = lambda seat: at(seat, 0, half)
        lower = lambda seat: at(seat, half, half)
        self.keep = pltpu.make_async_copy(src, whole(me), local)
        self.mine = [wires.copy(src, whole(me), peer) for peer in (along_x, along_y, mate)]
        self.pass_y = wires.copy(upper(x_seat), upper(x_seat), along_y)
        self.pass_x = wires.copy(lower(y_seat), lower(y_seat), along_x)
        self.mate_x = wires.copy(whole(x_seat), whole(x_seat), mate)
        self.mate_y = wires.copy(whole(y_seat), whole(y_seat), mate)
        self.mate_u = wires.copy(upper(far), upper(far), mate)
        self.mate_l = wires.copy(lower(far), lower(far), mate)

    def start(self):
        for copy in self.mine:
            copy.start()
        self.keep.start()

    def relay(self):
        self.mine[0].wait_recv()
        self.pass_y.start()
        self.mate_x.start()
        self.mine[1].wait_recv()
        self.pass_x.start()
        self.mate_y.start()

    def finish(self):
        self.pass_y.wait_recv()
        self.mate_u.start()
        self.pass_x.wait_recv()
        self.mate_l.start()
        for copy in (self.mine[2], self.mate_x, self.mate_y, self.mate_u, self.mate_l):
            copy.wait_recv()
        rest = [self.pass_y, self.pass_x, self.mate_x, self.mate_y, self.mate_u, self.mate_l]
        for copy in self.mine + rest:
            copy.wait_send()
        self.keep.wait()


class Light:
    wires_needed = 6

    def __init__(self, wires, src, far_src, stage, out, base, local):
        rows = src.shape[0]
        y, f, core, mate, along_x, along_y = seats()
        x_f = lax.rem(f + 2, 4)
        me, x_seat, y_seat, far = y * 4 + f, y * 4 + x_f, (1 - y) * 4 + f, (1 - y) * 4 + x_f
        at = lambda seat: out.at[pl.ds(pl.multiple_of(base + seat * rows, 16), rows)]
        self.fetch = [
            pltpu.make_async_copy(src, stage.at[0], local.at[0]),
            pltpu.make_async_copy(far_src, stage.at[1], local.at[1]),
        ]
        self.keep = [
            pltpu.make_async_copy(stage.at[0], at(me), local.at[2]),
            pltpu.make_async_copy(stage.at[1], at(far), local.at[3]),
        ]
        self.mine = [wires.copy(stage.at[0], at(me), peer) for peer in (along_x, along_y, mate)]
        self.far = wires.copy(stage.at[1], at(far), mate)
        self.mate_x = wires.copy(at(x_seat), at(x_seat), mate)
        self.mate_y = wires.copy(at(y_seat), at(y_seat), mate)

    def load(self):
        for copy in self.fetch:
            copy.start()

    def start(self):
        for copy in self.fetch:
            copy.wait()
        for copy in self.mine + [self.far] + self.keep:
            copy.start()

    def relay(self):
        self.mine[0].wait_recv()
        self.mate_x.start()
        self.mine[1].wait_recv()
        self.mate_y.start()

    def finish(self):
        for copy in (self.mine[2], self.far, self.mate_x, self.mate_y):
            copy.wait_recv()
        for copy in self.mine + [self.far, self.mate_x, self.mate_y]:
            copy.wait_send()
        for copy in self.keep:
            copy.wait()


def turn_z(step):
    return lax.rem(lax.axis_index("dp") + step, lax.axis_size("dp"))


def attend_kernel(
    block, units, lat, wq, wl, cos, sin, seg_col, seg_row, *rest
):
    sources, rest = rest[:units], rest[units:]
    (q_out, k_out, kv_out, o_out, lse_out), rest = rest[:5], rest[5:]
    length = lat.shape[0]
    if units:
        out, local, send, recv = rest
        unit = Spread(Wires(send, recv), sources[0], out, 0, local.at[0])

        @pl.when(pl.program_id(0) == 0)
        def _():
            seat = seats()
            greet(seat[3:])
            unit.start()

        @pl.when(pl.program_id(0) == 3)
        def _():
            unit.relay()

    lane = lax.broadcasted_iota(jnp.int32, (length, LANES), 1)
    query = dot(lat[:, :QR], wq[...])
    query = (query * cos[...] - swapped(query) * sin[...]).astype(bf16)
    both = dot(lat[:, QR : QR + KR], wl[...]).astype(bf16)
    key = jnp.where(lane < DN, both, lat[:, QR + KR :])
    q_out[...] = query
    k_out[...] = key
    kv_out[...] = both
    for first in range(0, length, block):
        last = first + block
        scores = dot(query[first:last], key[:last], NT) * SCALE
        scores = jnp.where(allowed(seg_col, seg_row, first, block, last), scores, NEGATIVE)
        peak = jnp.max(scores, axis=-1, keepdims=True)
        weights = jnp.exp(scores - peak)
        total = jnp.sum(weights, axis=-1, keepdims=True)
        probs = (weights * (1.0 / total)).astype(bf16)
        o_out[first:last, :] = dot(probs, both[:last]).astype(bf16)
        lse_out[0, first:last, :] = peak + jnp.log(total)
    if units:

        @pl.when(pl.program_id(0) == pl.num_programs(0) - 1)
        def _():
            unit.finish()


def attend(lat, wq, wl, cos, sin, seg_col, seg_row, cot=None, tokens=0, name_id=0):
    length = lat.shape[0]
    heads = wq.shape[1] // LANES
    whole = lambda shape: pl.BlockSpec(shape, lambda h: (0,) * len(shape))
    mine = lambda rows: pl.BlockSpec((rows, LANES), lambda h: (0, h))
    anywhere = [pl.BlockSpec(memory_space=pl.ANY)]
    wide = jax.ShapeDtypeStruct((length, heads * LANES), bf16)
    units = 0 if cot is None else 1
    wires = Spread.wires_needed
    params = dict(collective_id=name_id, has_side_effects=True) if units else {}
    return pl.pallas_call(
        functools.partial(attend_kernel, min(256, length), units),
        grid=(heads,),
        in_specs=[
            whole((length, PACK)),
            mine(QR),
            mine(KR),
            whole((length, LANES)),
            whole((length, LANES)),
            whole((length, 1)),
            whole((1, length)),
        ]
        + [whole((length // 8, D))] * units,
        out_specs=[mine(length)] * 4
        + [pl.BlockSpec((1, length, 1), lambda h: (h, 0, 0))]
        + anywhere * units,
        out_shape=[wide] * 4
        + [jax.ShapeDtypeStruct((heads, length, 1), f32)]
        + [jax.ShapeDtypeStruct((tokens, D), bf16)] * units,
        scratch_shapes=[
            pltpu.SemaphoreType.DMA((1,)),
            pltpu.SemaphoreType.DMA((wires,)),
            pltpu.SemaphoreType.DMA((wires,)),
        ]
        if units
        else [],
        compiler_params=pltpu.CompilerParams(vmem_limit_bytes=56 * MIB, **params),
        cost_estimate=pl.CostEstimate(
            flops=heads * length * (length * 4 * LANES + 2 * LANES * (QR + KR)),
            bytes_accessed=heads * length * LANES * 16,
            transcendentals=heads * length * length,
        ),
    )(lat, wq, wl, cos, sin, seg_col, seg_row, *([cot] if units else []))


def attend_back_kernel(
    block, units, gb, wo, q, k, kv, o, lse, cos, sin, seg_col, seg_row, *rest
):
    sources, rest = rest[: 5 * units], rest[5 * units :]
    (gq_out, gkv_out, rope_out, wo_out), rest = rest[:4], rest[4:]
    length = gb.shape[0]
    if units:
        x_z, cot_z, cot_far, _, _ = sources
        x_all, cot_all, dk, dv, stage, local, send, recv = rest
        wires = Wires(send, recv)
        z = turn_z(1)
        fetch = pltpu.make_async_copy(x_z.at[z], stage.at[2], local.at[5])
        first_unit = Spread(wires, stage.at[2], x_all, length, local.at[4])
        second_unit = Light(
            wires, cot_z.at[z], cot_far.at[z], stage, cot_all, length, local
        )

        @pl.when(pl.program_id(0) == 0)
        def _():
            fetch.start()
            second_unit.load()
            seat = seats()
            greet(seat[3:])
            fetch.wait()
            first_unit.start()
            second_unit.start()

        @pl.when(pl.program_id(0) == 3)
        def _():
            first_unit.relay()
            second_unit.relay()

    else:
        dk, dv = rest
    wo_out[...] = dot(o[...], gb[...], TN)[LANES - DV :].astype(bf16)
    lane = lax.broadcasted_iota(jnp.int32, (length, LANES), 1)
    grad = dot(gb[...], wo[...], NT).astype(bf16)
    dk[...] = jnp.zeros_like(dk)
    dv[...] = jnp.zeros_like(dv)
    for first in range(0, length, block):
        last = first + block
        scores = dot(q[first:last, :], k[:last, :], NT) * SCALE
        probs = jnp.exp(scores - lse[0, first:last, :])
        probs = jnp.where(allowed(seg_col, seg_row, first, block, last), probs, 0.0)
        grad_probs = dot(grad[first:last], kv[:last, :], NT)
        delta = jnp.sum(probs * grad_probs, axis=-1, keepdims=True)
        grad_scores = (probs * (grad_probs - delta)).astype(bf16)
        gq = dot(grad_scores, k[:last, :]) * SCALE
        gq = gq * cos[first:last, :] + swapped(gq) * sin[first:last, :]
        gq_out[first:last, :] = gq.astype(bf16)
        dk[:last, :] += dot(grad_scores, q[first:last, :], TN) * SCALE
        dv[:last, :] += dot(probs.astype(bf16), grad[first:last], TN)
    gkv_out[...] = jnp.where(lane < DN, dk[...], dv[...]).astype(bf16)

    @pl.when(pl.program_id(0) == 0)
    def _():
        rope_out[...] = dk[...]

    @pl.when(pl.program_id(0) > 0)
    def _():
        rope_out[...] += dk[...]

    if units:

        @pl.when(pl.program_id(0) == pl.num_programs(0) - 1)
        def _():
            first_unit.finish()
            second_unit.finish()


def attend_back(gb, wo, q, k, kv, o, lse, cos, sin, seg_col, seg_row, bulk=(), tokens=0, name_id=0):
    units = 1 if bulk else 0
    wires = Spread.wires_needed + Light.wires_needed
    anywhere = [pl.BlockSpec(memory_space=pl.ANY)]
    params = dict(collective_id=name_id, has_side_effects=True) if units else {}
    length = gb.shape[0]
    heads = q.shape[1] // LANES
    whole = lambda shape: pl.BlockSpec(shape, lambda h: (0,) * len(shape))
    mine = pl.BlockSpec((length, LANES), lambda h: (0, h))
    wide = jax.ShapeDtypeStruct((length, heads * LANES), bf16)
    return pl.pallas_call(
        functools.partial(attend_back_kernel, min(256, length), units),
        grid=(heads,),
        in_specs=[
            whole((length, D)),
            pl.BlockSpec((LANES, D), lambda h: (h, 0)),
            mine,
            mine,
            mine,
            mine,
            pl.BlockSpec((1, length, 1), lambda h: (h, 0, 0)),
            whole((length, LANES)),
            whole((length, LANES)),
            whole((length, 1)),
            whole((1, length)),
        ]
        + anywhere * (5 * units),
        out_specs=[
            mine,
            mine,
            whole((length, LANES)),
            pl.BlockSpec((DV, D), lambda h: (h, 0)),
        ]
        + anywhere * (2 * units),
        input_output_aliases={14: 4, 15: 5} if units else {},
        out_shape=[
            wide,
            wide,
            jax.ShapeDtypeStruct((length, LANES), f32),
            jax.ShapeDtypeStruct((heads * DV, D), bf16),
        ]
        + [jax.ShapeDtypeStruct((tokens, D), bf16)] * (2 * units),
        scratch_shapes=[pltpu.VMEM((length, LANES), f32), pltpu.VMEM((length, LANES), f32)]
        + [
            pltpu.VMEM((3, length // 8, D), bf16),
            pltpu.SemaphoreType.DMA((6,)),
            pltpu.SemaphoreType.DMA((wires,)),
            pltpu.SemaphoreType.DMA((wires,)),
        ]
        * units,
        compiler_params=pltpu.CompilerParams(vmem_limit_bytes=56 * MIB, **params),
        cost_estimate=pl.CostEstimate(
            flops=heads * length * (length * 10 * LANES + 4 * LANES * D),
            bytes_accessed=heads * length * LANES * 16 + length * D * 2,
            transcendentals=heads * length * length,
        ),
    )(gb, wo, q, k, kv, o, lse, cos, sin, seg_col, seg_row, *bulk)


def hidden_block(x, cot, w_gu, w_down, h_out, g_out, parts):
    units = w_down.shape[0]
    step = units // parts
    for part in range(parts):
        rows = slice(part * step, (part + 1) * step)
        gate = dot(w_gu[0, rows, :], x, NT)
        upper = dot(w_gu[1, rows, :], x, NT)
        grad = dot(w_down[rows, :], cot, NT) * RESIDUAL_SCALE
        sigma = jax.nn.sigmoid(gate)
        silu = gate * sigma
        h_out[rows, :] = (silu * upper).astype(bf16)
        g_out[0, rows, :] = (grad * upper * sigma * (1.0 + gate * (1.0 - sigma))).astype(bf16)
        g_out[1, rows, :] = (grad * silu).astype(bf16)


def ffn_own_kernel(place, x, cot, w_gu, w_down, h_out, g_out, y_out, gx_out):
    hidden_block(x[...], cot[...], w_gu, w_down, h_out, g_out, 2)
    y_out[...] = dot(h_out[...], w_down[...], TN).astype(bf16)
    gx_out[...] = (dot(g_out[0], w_gu[0], TN) + dot(g_out[1], w_gu[1], TN)).astype(bf16)


def ffn_rest_kernel(place, x, cot, w_gu, w_down, h_in, g_in, h_out, g_out):
    hidden_block(x[...], cot[...], w_gu, w_down, h_out, g_out, 2)


def ffn_shapes(units, tokens):
    return [
        jax.ShapeDtypeStruct((units, tokens), bf16),
        jax.ShapeDtypeStruct((2, units, tokens), bf16),
    ]


def ffn_own(place, x, cot_all, w_gu, w_down):
    units = w_down.shape[0]
    tokens = cot_all.shape[0]
    block = min(256, x.shape[0])
    steps = x.shape[0] // block
    kept = pl.Buffered(1)
    return pl.pallas_call(
        ffn_own_kernel,
        grid_spec=pltpu.PrefetchScalarGridSpec(
            num_scalar_prefetch=1,
            grid=(steps,),
            in_specs=[
                pl.BlockSpec((block, D), lambda i, p: (i, 0)),
                pl.BlockSpec((block, D), lambda i, p: (p[0] * steps + i, 0)),
                pl.BlockSpec((2, units, D), lambda i, p: (0, 0, 0), pipeline_mode=kept),
                pl.BlockSpec((units, D), lambda i, p: (0, 0), pipeline_mode=kept),
            ],
            out_specs=[
                pl.BlockSpec((units, block), lambda i, p: (0, p[0] * steps + i)),
                pl.BlockSpec((2, units, block), lambda i, p: (0, 0, p[0] * steps + i)),
                pl.BlockSpec((block, D), lambda i, p: (i, 0)),
                pl.BlockSpec((block, D), lambda i, p: (i, 0)),
            ],
        ),
        out_shape=ffn_shapes(units, tokens) + [jax.ShapeDtypeStruct((x.shape[0], D), bf16)] * 2,
        compiler_params=pltpu.CompilerParams(vmem_limit_bytes=60 * MIB),
        cost_estimate=pl.CostEstimate(
            flops=12 * x.shape[0] * units * D, bytes_accessed=6 * units * D, transcendentals=0
        ),
    )(place, x, cot_all, w_gu, w_down)


def ffn_rest(place, x_all, cot_all, w_gu, w_down, h_all, g_all, own):
    units = w_down.shape[0]
    tokens = x_all.shape[0]
    block = min(256, own)
    steps = own // block
    blocks = tokens // block
    kept = pl.Buffered(1)
    at = lambda i, p: lax.rem((p[0] + 1) * steps + i, blocks)
    return pl.pallas_call(
        ffn_rest_kernel,
        grid_spec=pltpu.PrefetchScalarGridSpec(
            num_scalar_prefetch=1,
            grid=(blocks - steps,),
            in_specs=[
                pl.BlockSpec((block, D), lambda i, p: (at(i, p), 0)),
                pl.BlockSpec((block, D), lambda i, p: (at(i, p), 0)),
                pl.BlockSpec((2, units, D), lambda i, p: (0, 0, 0), pipeline_mode=kept),
                pl.BlockSpec((units, D), lambda i, p: (0, 0), pipeline_mode=kept),
                pl.BlockSpec(memory_space=pl.ANY),
                pl.BlockSpec(memory_space=pl.ANY),
            ],
            out_specs=[
                pl.BlockSpec((units, block), lambda i, p: (0, at(i, p))),
                pl.BlockSpec((2, units, block), lambda i, p: (0, 0, at(i, p))),
            ],
        ),
        out_shape=ffn_shapes(units, tokens),
        input_output_aliases={5: 0, 6: 1},
        compiler_params=pltpu.CompilerParams(vmem_limit_bytes=60 * MIB),
        cost_estimate=pl.CostEstimate(
            flops=6 * (tokens - own) * units * D,
            bytes_accessed=6 * units * D + 10 * tokens * D,
            transcendentals=0,
        ),
    )(place, x_all, cot_all, w_gu, w_down, h_all, g_all)


def remote_call(kernel, name_id, out_shape, scratch, wires, operands):
    return pl.pallas_call(
        kernel,
        out_shape=out_shape,
        in_specs=[pl.BlockSpec(memory_space=pltpu.VMEM)] * len(operands),
        out_specs=jax.tree.map(lambda _: pl.BlockSpec(memory_space=pltpu.VMEM), out_shape),
        scratch_shapes=scratch
        + [pltpu.SemaphoreType.DMA((wires,)), pltpu.SemaphoreType.DMA((wires,))],
        compiler_params=pltpu.CompilerParams(
            collective_id=name_id, has_side_effects=True, vmem_limit_bytes=56 * MIB
        ),
    )(*operands)


def gather_plane_steps(wires, x, out):
    rows = x.shape[0]
    half = rows // 2
    y, f, core, mate, along_x, along_y = seats()
    me = y * 4 + f
    x_seat = y * 4 + lax.rem(f + 2, 4)
    y_seat = (1 - y) * 4 + f
    far = (1 - y) * 4 + lax.rem(f + 2, 4)
    whole = lambda seat: out.at[pl.ds(seat * rows, rows)]
    upper = lambda seat: out.at[pl.ds(seat * rows, half)]
    lower = lambda seat: out.at[pl.ds(seat * rows + half, half)]
    mine_x = wires.copy(x, whole(me), along_x)
    mine_y = wires.copy(x, whole(me), along_y)
    mine_m = wires.copy(x, whole(me), mate)
    mine_x.start()
    mine_y.start()
    mine_m.start()
    out[pl.ds(me * rows, rows), :] = x[...]
    pass_y = wires.copy(upper(x_seat), upper(x_seat), along_y)
    pass_x = wires.copy(lower(y_seat), lower(y_seat), along_x)
    mate_x = wires.copy(whole(x_seat), whole(x_seat), mate)
    mate_y = wires.copy(whole(y_seat), whole(y_seat), mate)
    mate_u = wires.copy(upper(far), upper(far), mate)
    mate_l = wires.copy(lower(far), lower(far), mate)
    mine_x.wait_recv()
    pass_y.start()
    mate_x.start()
    mine_y.wait_recv()
    pass_x.start()
    mate_y.start()
    pass_y.wait_recv()
    mate_u.start()
    pass_x.wait_recv()
    mate_l.start()
    for copy in (mine_m, mate_x, mate_y, mate_u, mate_l):
        copy.wait_recv()
    for copy in (mine_x, mine_y, mine_m, pass_y, pass_x, mate_x, mate_y, mate_u, mate_l):
        copy.wait_send()


def plane_gather_kernel(x, out, send, recv):
    y, f, core, mate, along_x, along_y = seats()
    greet([mate, along_x, along_y])
    gather_plane_steps(Wires(send, recv), x, out)


def plane_gather(x, name_id):
    shape = jax.ShapeDtypeStruct((8 * x.shape[0], x.shape[1]), x.dtype)
    return remote_call(plane_gather_kernel, name_id, shape, [], 9, (x,))


def scatter_plane_steps(wires, part, out, own, from_mate, from_x, from_y, last, relay, fill=None):
    rows = out.shape[0]
    half = rows // 2
    y, f, core, mate, along_x, along_y = seats()
    x_f = lax.rem(f + 2, 4)
    turn = 1 - 2 * core
    seat = [(1 - y) * 4 + x_f, y * 4 + x_f, (1 - y) * 4 + f, y * 4 + f]
    upper, lower = slice(0, half), slice(half, rows)
    to_mate = [
        wires.copy(part.at[pl.ds((s + turn) * rows, rows)], from_mate.at[i], mate)
        for i, s in enumerate(seat)
    ]
    for copy in to_mate:
        copy.start()
    far_x = wires.copy(own.at[0, upper], from_x.at[0], along_x)
    far_y = wires.copy(own.at[0, lower], from_y.at[0], along_y)
    near_x = wires.copy(own.at[1, upper], from_x.at[1], along_x)
    near_y = wires.copy(own.at[2, lower], from_y.at[1], along_y)
    relay_y = wires.copy(relay.at[0], last.at[0], along_y)
    relay_x = wires.copy(relay.at[1], last.at[1], along_x)
    starts = ([far_x, far_y], [near_x], [near_y], [])
    for i in range(4):
        to_mate[i].wait_recv()
        own[i] = part[pl.ds(seat[i] * rows, rows), :] + from_mate[i]
        for copy in starts[i]:
            copy.start()
    if fill is not None:
        fill()
    far_x.wait_recv()
    relay[0] = own[2, upper] + from_x[0]
    relay_y.start()
    far_y.wait_recv()
    relay[1] = own[1, lower] + from_y[0]
    relay_x.start()
    near_x.wait_recv()
    near_y.wait_recv()
    relay_y.wait_recv()
    relay_x.wait_recv()
    add = lambda a, b, c: (a.astype(f32) + b.astype(f32) + c.astype(f32)).astype(out.dtype)
    out[upper, :] = add(own[3, upper], from_x[1], last[0])
    out[lower, :] = add(own[3, lower], from_y[1], last[1])
    for copy in to_mate + [far_x, far_y, near_x, near_y, relay_y, relay_x]:
        copy.wait_send()


def plane_scatter_kernel(part, out, own, from_mate, from_x, from_y, last, relay, send, recv):
    greet(seats()[3:])
    wires = Wires(send, recv)
    scatter_plane_steps(wires, part, out, own, from_mate, from_x, from_y, last, relay)


def plane_scatter(part, name_id):
    rows, width = part.shape[0] // 8, part.shape[1]
    shape = jax.ShapeDtypeStruct((rows, width), part.dtype)
    buffer = lambda count, depth: pltpu.VMEM((count, depth, width), part.dtype)
    scratch = [buffer(4, rows), buffer(4, rows)] + [buffer(2, rows // 2)] * 4
    return remote_call(plane_scatter_kernel, name_id, shape, scratch, 10, (part,))


def take_columns(weight, first, width):
    begin = min(first // LANES * LANES, weight.shape[1] - 2 * LANES)
    window = weight[:, begin : begin + 2 * LANES].astype(f32)
    shift = (2 * LANES - (first - begin)) % (2 * LANES)
    window = (pltpu.roll(window, shift, 1) if shift else window)[:, :LANES]
    lane = lax.broadcasted_iota(jnp.int32, window.shape, 1)
    return jnp.where(lane < width, window, 0.0).astype(bf16)


def front_kernel(
    pieces,
    heads,
    x,
    qd,
    ld,
    gain_a,
    gain_f,
    gain_q,
    gain_l,
    qup,
    lup,
    seg_col,
    seg_row,
    freq,
    lat,
    wq,
    wl,
    w_in,
    raw_out,
    n_out,
    gains_out,
    cos_out,
    sin_out,
    w,
    gains,
    gains_all,
    qpack,
    own,
    send,
    recv,
):
    rows = w.shape[0]
    half = rows // 2
    piece = half // pieces
    span = x.shape[0]
    length = cos_out.shape[0]
    y, f, core, mate, along_x, along_y = seats()
    x_f = lax.rem(f + 2, 4)
    m_f = f + 1 - 2 * core
    c_f = 3 - f
    cross = {"fsdp": c_f}
    wires = Wires(send, recv)

    w[:, :QR] = qd[...]
    w[:, QR:] = jnp.zeros((rows, PACK - QR), bf16)
    w[:, QR:DOWN] = ld[...]
    gains[...] = jnp.zeros_like(gains)
    gains[0:1, : gain_a.shape[1]] = gain_a[...].astype(f32)
    gains[1:2, : gain_f.shape[1]] = gain_f[...].astype(f32)
    gains[2:3, : gain_q.shape[1]] = gain_q[...].astype(f32)
    gains[3:4, : gain_l.shape[1]] = gain_l[...].astype(f32)
    greet([mate, along_x, along_y, cross])

    gains_x = wires.copy(gains, gains_all.at[f], along_x)
    gains_m = wires.copy(gains, gains_all.at[f], mate)
    gains_r = wires.copy(gains_all.at[x_f], gains_all.at[x_f], mate)
    spot = lambda owner, side, i: pl.ds(owner * rows + side * half + i * piece, piece)
    across = [
        wires.copy(w.at[pl.ds(y * half + i * piece, piece)], w_in.at[spot(f, y, i)], along_x)
        for i in range(pieces)
    ]
    mine = wires.copy(w, w_in.at[pl.ds(f * rows, rows)], mate)
    same = lambda side, peer: [
        wires.copy(w_in.at[spot(x_f, side, i)], w_in.at[spot(x_f, side, i)], peer)
        for i in range(pieces)
    ]
    trade = same(y, along_y)
    to_mate = same(y, mate)
    rest = same(1 - y, mate)
    gains_x.start()
    gains_m.start()
    for copy in across:
        copy.start()
    mine.start()
    gains_all[f] = gains[...]
    w_in[pl.ds(f * rows, rows), :] = w[...]

    q_rows, l_rows = qup.shape[0], lup.shape[0]
    for seat in range(4):
        for head in range(heads):
            first = lambda ctx: ((seat * 2 + ctx) * heads + head) * (DN + DR)
            column = jnp.where(
                y == 0,
                take_columns(qup, first(0), DN + DR).astype(f32),
                take_columns(qup, first(1), DN + DR).astype(f32),
            )
            qpack[seat, :, head * LANES : (head + 1) * LANES] = column.astype(bf16)
    width = heads * LANES
    kv_part = lambda seat: lup.at[:, pl.ds(pl.multiple_of((seat * 2 + y) * width, LANES), width)]
    q_spot = wq.at[pl.ds(f * q_rows, q_rows)]
    l_spot = wl.at[pl.ds(f * l_rows, l_rows)]
    swaps = []
    for seat, peer in ((x_f, along_x), (c_f, cross), (m_f, mate)):
        swaps.append(wires.copy(qpack.at[seat], q_spot, peer))
        swaps.append(wires.copy(kv_part(seat), l_spot, peer))
    for copy in swaps:
        copy.start()
    wq[pl.ds(f * q_rows, q_rows), :] = qpack[f]
    wl[pl.ds(f * l_rows, l_rows), :] = lup[
        :, pl.ds(pl.multiple_of((f * 2 + y) * width, LANES), width)
    ]

    index = lax.broadcasted_iota(jnp.int32, (length, 1), 0).astype(f32)
    seg = seg_col[...]
    doc_start = jnp.zeros((length, 1), f32)
    for number in range(1, 4):
        start = jnp.sum((seg_row[...] < number).astype(f32), axis=1, keepdims=True)
        doc_start = jnp.where(seg == number, start, doc_start)
    theta = (index - doc_start) * freq[...]
    lane = lax.broadcasted_iota(jnp.int32, (length, LANES), 1)
    turned = (lane >= DN) & (lane < DN + DR)
    cos_out[...] = jnp.where(turned, jnp.cos(theta), jnp.where(lane < DN, 1.0, 0.0))
    sin_out[...] = jnp.where(turned, jnp.sin(theta), 0.0)

    gains_x.wait_recv()
    gains_r.start()
    gains_m.wait_recv()
    gains_r.wait_recv()
    shard = gain_a.shape[1]
    full = [gains_all[i] for i in range(4)]
    g_attn = jnp.concatenate([full[i][0:1, :shard] for i in range(4)], axis=1)
    g_ffn = jnp.concatenate([full[i][1:2, :shard] for i in range(4)], axis=1)
    placed = [full[0]]
    for i in range(1, 4):
        placed.append(pltpu.roll(full[i], i * gain_q.shape[1], 1))
    g_query = sum(p[2:3] for p in placed)
    placed = [full[0]]
    for i in range(1, 4):
        placed.append(pltpu.roll(full[i], i * gain_l.shape[1], 1))
    g_latent = sum(p[3:4] for p in placed)[:, :KR]
    gains_out[...] = jnp.zeros_like(gains_out)
    gains_out[0:1, :] = g_attn
    gains_out[1:2, :] = g_ffn
    gains_out[2:3, :QR] = g_query
    gains_out[3:4, :KR] = g_latent

    inputs = x[...].astype(f32)
    n_out[...] = normalize(inputs, g_attn).astype(bf16)

    def term(owner):
        left = n_out[:, pl.ds(pl.multiple_of(owner * rows, LANES), rows)]
        return dot(left, w_in[pl.ds(owner * rows, rows), :])

    raw_out[...] = term(f)
    for i in range(pieces):
        across[i].wait_recv()
        trade[i].start()
        to_mate[i].start()
    mine.wait_recv()
    raw_out[...] += term(m_f)
    for i in range(pieces):
        trade[i].wait_recv()
        rest[i].start()
    raw_out[...] += term(x_f)
    for copy in to_mate + rest:
        copy.wait_recv()
    raw_out[...] += term(c_f)

    me = y * 4 + f
    cos = cos_out[pl.ds(me * span, span), :]
    sin = sin_out[pl.ds(me * span, span), :]
    own[:, :QR] = normalize(raw_out[:, :QR], g_query).astype(bf16)
    own[:, QR : QR + KR] = normalize(raw_out[:, QR : QR + KR], g_latent).astype(bf16)
    rope = pltpu.roll(raw_out[:, QR + KR :], DN, 1)
    own[:, QR + KR :] = (rope * cos - swapped(rope) * sin).astype(bf16)
    gather_plane_steps(wires, own, lat)

    for copy in swaps:
        copy.wait_recv()
    for copy in [gains_x, gains_m, gains_r, mine] + across + trade + to_mate + rest + swaps:
        copy.wait_send()


def front(x, qd, ld, gains, qup, lup, seg_col, seg_row, heads, name_id):
    freq = ROPE_BASE ** (-np.arange(DR // 2, dtype=np.float32) / (DR // 2))
    freq = np.concatenate([np.zeros(DN), freq, freq, np.zeros(LANES - DN - DR)])
    freq = jnp.asarray(freq[None], f32)
    span, length = x.shape[0], seg_col.shape[0]
    rows, width = qd.shape[0], heads * LANES
    shape = jax.ShapeDtypeStruct
    shapes = (
        shape((length, PACK), bf16),
        shape((QR, width), bf16),
        shape((KR, width), bf16),
        shape((4 * rows, PACK), bf16),
        shape((span, PACK), f32),
        shape((span, D), bf16),
        shape((8, D), f32),
        shape((length, LANES), f32),
        shape((length, LANES), f32),
    )
    pieces = 4
    scratch = [
        pltpu.VMEM((rows, PACK), bf16),
        pltpu.VMEM((8, QR), f32),
        pltpu.VMEM((4, 8, QR), f32),
        pltpu.VMEM((4, qup.shape[0], width), bf16),
        pltpu.VMEM((span, PACK), bf16),
    ]
    operands = (x, qd, ld) + tuple(g[None] for g in gains) + (qup, lup, seg_col, seg_row, freq)
    return remote_call(
        functools.partial(front_kernel, pieces, heads),
        name_id,
        shapes,
        scratch,
        4 + 4 * pieces + 6 + 9,
        operands,
    )


def ffn_group_kernel(
    columns,
    x,
    cot_all,
    w_gu,
    w_down,
    h_out,
    g_out,
    gx_out,
    y_keep,
    y_send,
    x_all,
    wg,
    wd,
    xs,
    cs,
    hv,
    gv,
    ht,
    gt,
    gx_part,
    y_part,
    g_mate,
    y_mate,
    sent,
    from_x,
    local,
    send,
    recv,
):
    units = wd.shape[0]
    span = x.shape[0]
    block = 2 * span
    width = D // columns
    y, f, core, mate, along_x, along_y = seats()
    group = y * 4 * span
    chip = lax.div(f, 2)
    load_gu = pltpu.make_async_copy(w_gu, wg, local.at[0])
    load_down = pltpu.make_async_copy(w_down, wd, local.at[1])
    load_gu.start()
    load_down.start()
    load_cot = []
    for at, which in enumerate((chip, 1 - chip)):
        where = pl.ds(pl.multiple_of(group + which * block, LANES), block)
        load_cot.append(pltpu.make_async_copy(cot_all.at[where], cs.at[at], local.at[6 + at]))
        load_cot[at].start()
    greet([mate, along_x, along_y])
    wires = Wires(send, recv)
    x_f = lax.rem(f + 2, 4)
    me, y_seat, far = y * 4 + f, (1 - y) * 4 + f, (1 - y) * 4 + x_f
    half = span // 2
    place = lambda seat, first, rows: x_all.at[
        pl.ds(pl.multiple_of(seat * span + first, 16), rows)
    ]
    mine = pl.ds(core * span, span)
    other = pl.ds((1 - core) * span, span)
    x_x = wires.copy(x, xs.at[1, mine], along_x)
    x_m = wires.copy(x, xs.at[0, mine], mate)
    x_x.start()
    x_m.start()
    xs[0, mine] = x[...]
    x_r = wires.copy(xs.at[1, mine], xs.at[1, mine], mate)
    x_y = wires.copy(x, place(me, 0, span), along_y)
    x_y.start()
    pass_y = wires.copy(
        xs.at[1, pl.ds(core * span, half)], place(y * 4 + x_f, 0, half), along_y
    )
    pass_x = wires.copy(place(y_seat, half, half), place(y_seat, half, half), along_x)
    mate_y = wires.copy(place(y_seat, 0, span), place(y_seat, 0, span), mate)
    mate_u = wires.copy(place(far, 0, half), place(far, 0, half), mate)
    mate_l = wires.copy(place(far, half, half), place(far, half, half), mate)
    keep_x = [
        pltpu.make_async_copy(
            xs.at[at], place(y * 4 + which * 2, 0, block), local.at[8 + at]
        )
        for at, which in enumerate((chip, 1 - chip))
    ]
    y_m = [wires.copy(y_part.at[i, other], y_mate.at[i], mate) for i in range(2)]
    cols = [slice(i * width, (i + 1) * width) for i in range(columns)]
    to_mate = lambda at: [
        wires.copy(gx_part.at[at, other, c], g_mate.at[at, :, c], mate) for c in cols
    ]
    g_near, g_far = to_mate(0), to_mate(1)
    g_x = [wires.copy(sent.at[:, c], from_x.at[:, c], along_x) for c in cols]

    cut = units // 2 // LANES * LANES

    def hidden(at):
        tokens = slice(at * block, (at + 1) * block)
        for rows in (slice(0, cut), slice(cut, units)):
            gate = dot(wg[0, rows, :], xs[at], NT)
            upper = dot(wg[1, rows, :], xs[at], NT)
            grad = dot(wd[rows, :], cs[at], NT) * RESIDUAL_SCALE
            sigma = jax.nn.sigmoid(gate)
            silu = gate * sigma
            value = silu * upper
            hv[at, rows, :] = value.astype(bf16)
            ht[tokens, rows] = value.T.astype(bf16)
            value = grad * upper * sigma * (1.0 + gate * (1.0 - sigma))
            gv[at, 0, rows, :] = value.astype(bf16)
            gt[0, tokens, rows] = value.T.astype(bf16)
            value = grad * silu
            gv[at, 1, rows, :] = value.astype(bf16)
            gt[1, tokens, rows] = value.T.astype(bf16)
        which = chip if at == 0 else 1 - chip
        where = pl.ds(pl.multiple_of(group + which * block, LANES), block)
        out_h = pltpu.make_async_copy(hv.at[at], h_out.at[:, where], local.at[2 + 2 * at])
        out_g = pltpu.make_async_copy(gv.at[at], g_out.at[:, :, where], local.at[3 + 2 * at])
        out_h.start()
        out_g.start()
        return [out_h, out_g]

    load_gu.wait()
    load_down.wait()
    x_m.wait_recv()
    for copy in load_cot:
        copy.wait()
    stores = hidden(0)
    x_x.wait_recv()
    x_r.start()
    pass_y.start()
    x_y.wait_recv()
    pass_x.start()
    mate_y.start()
    x_r.wait_recv()
    for copy in keep_x:
        copy.start()
    stores += hidden(1) + keep_x

    def pass_on(i):
        g_far[i].wait_recv()
        sent[:, cols[i]] = gx_part[1, mine, cols[i]] + g_mate[1, :, cols[i]]
        g_x[i].start()

    for i, c in enumerate(cols):
        total = dot(gt[0], wg[0, :, c]) + dot(gt[1], wg[1, :, c])
        gx_part[:, :, c] = total.astype(bf16).reshape(2, block, width)
        g_far[i].start()
        g_near[i].start()
        if i > 0:
            pass_on(i - 1)
    pass_y.wait_recv()
    mate_u.start()
    pass_x.wait_recv()
    mate_l.start()
    for i, c in enumerate(cols):
        y_part[:, :, c] = dot(ht[...], wd[:, c]).astype(bf16).reshape(2, block, width)
        if i == 0:
            pass_on(columns - 1)
    for copy in y_m:
        copy.start()
    for i, c in enumerate(cols):
        g_near[i].wait_recv()
        g_x[i].wait_recv()
        keep = gx_part[0, mine, c].astype(f32) + g_mate[0, :, c].astype(f32)
        gx_out[:, c] = (keep + from_x[:, c].astype(f32)).astype(bf16)
    for copy in y_m:
        copy.wait_recv()
    y_keep[...] = y_part[0, mine] + y_mate[0]
    y_send[...] = y_part[1, mine] + y_mate[1]
    for copy in (mate_y, mate_u, mate_l):
        copy.wait_recv()
    plane = [x_y, pass_y, pass_x, mate_y, mate_u, mate_l]
    for copy in [x_x, x_m, x_r] + y_m + g_near + g_far + g_x + plane:
        copy.wait_send()
    for copy in stores:
        copy.wait()


def ffn_group(x, cot_all, w_gu, w_down, name_id):
    tokens = cot_all.shape[0]
    span = x.shape[0]
    units = w_down.shape[0]
    columns = 5
    wires = 11 + 3 * columns
    anywhere = pl.BlockSpec(memory_space=pl.ANY)
    vmem = pl.BlockSpec(memory_space=pltpu.VMEM)
    buffer = lambda *shape: pltpu.VMEM(shape, bf16)
    return pl.pallas_call(
        functools.partial(ffn_group_kernel, columns),
        out_shape=ffn_shapes(units, tokens)
        + [jax.ShapeDtypeStruct((span, D), bf16)] * 3
        + [jax.ShapeDtypeStruct((tokens, D), bf16)],
        in_specs=[vmem, anywhere, anywhere, anywhere],
        out_specs=[anywhere, anywhere, vmem, vmem, vmem, anywhere],
        scratch_shapes=[
            buffer(2, units, D),
            buffer(units, D),
            buffer(2, 2 * span, D),
            buffer(2, 2 * span, D),
            buffer(2, units, 2 * span),
            buffer(2, 2, units, 2 * span),
            buffer(4 * span, units),
            buffer(2, 4 * span, units),
            buffer(2, 2 * span, D),
            buffer(2, 2 * span, D),
            buffer(2, span, D),
            buffer(2, span, D),
            buffer(span, D),
            buffer(span, D),
            pltpu.SemaphoreType.DMA((10,)),
            pltpu.SemaphoreType.DMA((wires,)),
            pltpu.SemaphoreType.DMA((wires,)),
        ],
        compiler_params=pltpu.CompilerParams(
            collective_id=name_id, has_side_effects=True, vmem_limit_bytes=62 * MIB
        ),
        cost_estimate=pl.CostEstimate(
            flops=12 * 4 * span * units * D, bytes_accessed=6 * units * D, transcendentals=0
        ),
    )(x, cot_all, w_gu, w_down)


def ffn_others_kernel(
    span,
    x_z,
    cot_z,
    x_far,
    cot_far,
    x_in,
    cot_in,
    h_in,
    g_in,
    w_gu,
    w_down,
    x_all,
    cot_all,
    h_out,
    g_out,
    wg,
    wd,
    xb,
    cb,
    hb,
    gb,
    stage,
    loads,
    local,
    slots_in,
    slots_out,
    send,
    recv,
):
    length = 8 * span
    block = 2 * span
    y = lax.axis_index("ctx")
    load_gu = pltpu.make_async_copy(w_gu, wg, loads.at[0])
    load_down = pltpu.make_async_copy(w_down, wd, loads.at[1])
    load_gu.start()
    load_down.start()
    greet(seats()[3:])
    wires = Wires(send, recv)
    def unit(r, own, far, out, at):
        z = turn_z(r)
        return Light(
            wires, own.at[z], far.at[z], stage.at[at], out, r * length, local.at[at]
        )

    x_unit = {r: unit(r, x_z, x_far, x_all, r - 2) for r in (2, 3)}
    c_unit = {r: unit(r, cot_z, cot_far, cot_all, r) for r in (2, 3)}
    for one in (x_unit[2], c_unit[2], x_unit[3], c_unit[3]):
        one.load()
    x_unit[2].start()
    c_unit[2].start()

    def where(i):
        first = jnp.where(i < 2, (1 - y) * 4 * span + i * block, length + (i - 2) * block)
        return pl.ds(pl.multiple_of(first, LANES), block)

    def fetch(i):
        slot = lax.rem(i, 2)
        return [
            pltpu.make_async_copy(x_all.at[where(i)], xb.at[slot], slots_in.at[0, slot]),
            pltpu.make_async_copy(cot_all.at[where(i)], cb.at[slot], slots_in.at[1, slot]),
        ]

    def store(i):
        slot = lax.rem(i, 2)
        return [
            pltpu.make_async_copy(hb.at[slot], h_out.at[:, where(i)], slots_out.at[0, slot]),
            pltpu.make_async_copy(gb.at[slot], g_out.at[:, :, where(i)], slots_out.at[1, slot]),
        ]

    count = 14
    for copy in fetch(0):
        copy.start()
    load_gu.wait()
    load_down.wait()

    def step(i, carry):
        slot = lax.rem(i, 2)
        for copy in fetch(i):
            copy.wait()

        @pl.when(i >= 2)
        def _():
            for copy in store(i - 2):
                copy.wait()

        def between(number, *steps):
            @pl.when(i == number)
            def _():
                for one in steps:
                    one()

        between(3, x_unit[2].relay, c_unit[2].relay, x_unit[3].start)
        between(4, c_unit[3].start)
        between(5, x_unit[2].finish, c_unit[2].finish)
        between(8, x_unit[3].relay, c_unit[3].relay)
        between(9, x_unit[3].finish, c_unit[3].finish)

        @pl.when(i + 1 < count)
        def _():
            for copy in fetch(i + 1):
                copy.start()

        hidden_block(xb[slot], cb[slot], wg, wd, hb.at[slot], gb.at[slot], 2)
        for copy in store(i):
            copy.start()
        return carry

    lax.fori_loop(0, count, step, 0)
    for i in (count - 2, count - 1):
        for copy in store(i):
            copy.wait()


def ffn_others(x_z, cot_z, x_far, cot_far, x_all, cot_all, h_all, g_all, w_gu, w_down, name_id):
    units = w_down.shape[0]
    tokens = x_all.shape[0]
    span = x_z.shape[1]
    block = 2 * span
    wires = 4 * Light.wires_needed
    anywhere = pl.BlockSpec(memory_space=pl.ANY)
    buffer = lambda *shape: pltpu.VMEM(shape, bf16)
    return pl.pallas_call(
        functools.partial(ffn_others_kernel, span),
        out_shape=[jax.ShapeDtypeStruct((tokens, D), bf16)] * 2 + ffn_shapes(units, tokens),
        in_specs=[anywhere] * 10,
        out_specs=[anywhere] * 4,
        input_output_aliases={4: 0, 5: 1, 6: 2, 7: 3},
        scratch_shapes=[
            buffer(2, units, D),
            buffer(units, D),
            buffer(2, block, D),
            buffer(2, block, D),
            buffer(2, units, block),
            buffer(2, 2, units, block),
            buffer(4, 2, span, D),
            pltpu.SemaphoreType.DMA((2,)),
            pltpu.SemaphoreType.DMA((4, 4)),
            pltpu.SemaphoreType.DMA((2, 2)),
            pltpu.SemaphoreType.DMA((2, 2)),
            pltpu.SemaphoreType.DMA((wires,)),
            pltpu.SemaphoreType.DMA((wires,)),
        ],
        compiler_params=pltpu.CompilerParams(
            collective_id=name_id, has_side_effects=True, vmem_limit_bytes=60 * MIB
        ),
        cost_estimate=pl.CostEstimate(
            flops=6 * (tokens - 4 * span) * units * D,
            bytes_accessed=6 * units * D + 10 * tokens * D,
            transcendentals=0,
        ),
    )(x_z, cot_z, x_far, cot_far, x_all, cot_all, h_all, g_all, w_gu, w_down)


def ffn_grads_kernel(g, h, x, cot, gu_out, down_out, h_kept, sem):
    which, column = pl.program_id(0), pl.program_id(1)
    load = pltpu.make_async_copy(h, h_kept, sem.at[0])
    units = h.shape[0]
    cut = units // 2

    @pl.when((which == 0) & (column == 0))
    def _():
        load.start()

    @pl.when((which == 2) & (column == 0))
    def _():
        load.wait()

    @pl.when(which < 2)
    def _():
        for rows in (slice(0, cut), slice(cut, units)):
            gu_out[0, rows, :] = dot(g[0, rows, :], x[...])

    @pl.when(which == 2)
    def _():
        for rows in (slice(0, cut), slice(cut, units)):
            down_out[rows, :] = dot(h_kept[rows, :], cot[...]) * RESIDUAL_SCALE


def ffn_grads(g_all, h_all, x_all, cot_all):
    units, tokens = h_all.shape
    width = 256
    columns = D // width
    shape = jax.ShapeDtypeStruct
    last = columns - 1
    gate_up = lambda m, n: jnp.where(m < 2, n, last)
    only_down = lambda m, n: jnp.where(m < 2, 0, n)
    return pl.pallas_call(
        ffn_grads_kernel,
        grid=(3, columns),
        in_specs=[
            pl.BlockSpec((1, units, tokens), lambda m, n: (jnp.minimum(m, 1), 0, 0)),
            pl.BlockSpec(memory_space=pl.ANY),
            pl.BlockSpec((tokens, width), lambda m, n: (0, gate_up(m, n))),
            pl.BlockSpec((tokens, width), lambda m, n: (0, only_down(m, n))),
        ],
        out_specs=[
            pl.BlockSpec((1, units, width), lambda m, n: (jnp.minimum(m, 1), 0, gate_up(m, n))),
            pl.BlockSpec((units, width), lambda m, n: (0, only_down(m, n))),
        ],
        out_shape=[shape((2, units, D), f32), shape((units, D), f32)],
        scratch_shapes=[pltpu.VMEM((units, tokens), bf16), pltpu.SemaphoreType.DMA((1,))],
        compiler_params=pltpu.CompilerParams(vmem_limit_bytes=62 * MIB),
        cost_estimate=pl.CostEstimate(
            flops=6 * tokens * units * D,
            bytes_accessed=6 * units * tokens + 6 * tokens * D + 12 * units * D,
            transcendentals=0,
        ),
    )(g_all, h_all, x_all, cot_all)


def norm_back_rows(values, gain, grad):
    inverse = lax.rsqrt(jnp.mean(values * values, axis=-1, keepdims=True) + EPS)
    unit = values * inverse
    scaled = gain * grad
    return (scaled - unit * jnp.mean(unit * scaled, axis=-1, keepdims=True)) * inverse


def finish_kernel(
    gq,
    gkv,
    rope,
    lat,
    wq,
    wl,
    w_in,
    raw,
    n,
    x,
    grad_resid,
    gains,
    cos_all,
    sin_all,
    ffn_gain,
    part,
    input_grad,
    lat_part,
    lat_sum,
    own,
    from_mate,
    from_x,
    from_y,
    last,
    relay,
    n_all,
    ups,
    raw_own,
    raw_all,
    down,
    traded,
    send,
    recv,
):
    span = x.shape[0]
    length = gq.shape[0]
    width = gq.shape[1]
    rows = w_in.shape[0] // 4
    q_rows, l_rows = QR // 4, KR // 4
    y, f, core, mate, along_x, along_y = seats()
    x_f, m_f, c_f = lax.rem(f + 2, 4), f + 1 - 2 * core, 3 - f
    cross = {"fsdp": c_f}
    others = ((x_f, along_x), (c_f, cross), (m_f, mate))
    greet([mate, along_x, along_y, cross])
    wires = Wires(send, recv)
    columns = lambda seat: pl.ds(pl.multiple_of(seat * rows, LANES), rows)
    mine = pl.ds(f * span, span)
    n_sends = [wires.copy(n.at[:, columns(seat)], n_all.at[mine], peer) for seat, peer in others]
    for copy in n_sends:
        copy.start()
    n_all[mine, :] = n[:, columns(f)]

    each = span + EXTRA
    for first in range(0, length, 512):
        some = slice(first, first + 512)
        q_part = dot(gq[some, :], wq[...], NT).astype(bf16)
        l_part = dot(gkv[some, :], wl[...], NT).astype(bf16)
        r_part = rope[some, :].astype(bf16)
        for at in range(0, 512, span):
            here = (first + at) // span * each
            lat_part[here : here + span, :QR] = q_part[at : at + span]
            lat_part[here : here + span, QR : QR + KR] = l_part[at : at + span]
            lat_part[here : here + span, QR + KR :] = r_part[at : at + span]
    for seat in range(8):
        here = seat * each + span
        piece = ffn_gain[:, seat % 4 * rows : (seat % 4 + 1) * rows]
        lat_part[here : here + EXTRA, :] = jnp.zeros((EXTRA, PACK), bf16)
        lat_part[here : here + EXTRA, :rows] = jnp.broadcast_to(piece, (EXTRA, rows)).astype(bf16)

    swap_rows = q_rows + l_rows
    swaps = [
        wires.copy(ups.at[seat], part.at[pl.ds(f * swap_rows, swap_rows)], peer)
        for seat, peer in others
    ]

    def column_gradients():
        q_grad = dot(lat[:, :QR], gq[...], TN).astype(bf16)
        l_grad = dot(lat[:, QR : QR + KR], gkv[...], TN).astype(bf16)
        for seat in range(4):
            ups[seat, :q_rows] = q_grad[seat * q_rows : (seat + 1) * q_rows]
            ups[seat, q_rows:] = l_grad[seat * l_rows : (seat + 1) * l_rows]
        part[pl.ds(f * swap_rows, swap_rows), :] = ups[f]

    scatter_plane_steps(
        wires, lat_part, lat_sum, own, from_mate, from_x, from_y, last, relay, column_gradients
    )

    me = pl.ds((y * 4 + f) * span, span)
    grad = lat_sum[:span, :].astype(f32)
    raw_own[:, :QR] = norm_back_rows(raw[:, :QR], gains[2:3, :QR], grad[:, :QR]).astype(bf16)
    raw_own[:, QR : QR + KR] = norm_back_rows(
        raw[:, QR : QR + KR], gains[3:4, :KR], grad[:, QR : QR + KR]
    ).astype(bf16)
    turned = grad[:, QR + KR :]
    lane = lax.broadcasted_iota(jnp.int32, turned.shape, 1)
    turned = turned * cos_all[me, :] + swapped(turned) * sin_all[me, :]
    turned = jnp.where((lane >= DN) & (lane < DN + DR), turned, 0.0)
    raw_own[:, QR + KR :] = pltpu.roll(turned, LANES - DN, 1).astype(bf16)
    raw_x = wires.copy(raw_own, raw_all.at[mine], along_x)
    raw_m = wires.copy(raw_own, raw_all.at[mine], mate)
    theirs = raw_all.at[pl.ds(x_f * span, span)]
    raw_r = wires.copy(theirs, theirs, mate)
    raw_x.start()
    raw_m.start()
    for copy in swaps:
        copy.start()
    raw_all[mine, :] = raw_own[...]
    for copy in n_sends:
        copy.wait_recv()
    raw_x.wait_recv()
    raw_r.start()
    raw_m.wait_recv()
    raw_r.wait_recv()

    down[...] = dot(n_all[...], raw_all[...], TN).astype(bf16)
    half = rows // 2
    trade = wires.copy(down.at[pl.ds((1 - y) * half, half)], traded, along_y)
    trade.start()
    inputs = x[...].astype(f32)
    grad_in = dot(raw_own[...], w_in[...], NT)
    input_grad[...] = grad_resid[...] + norm_back_rows(inputs, gains[0:1, :], grad_in)
    first = 4 * swap_rows
    last_rows = part.shape[0] - first - 2 * half
    part[first + 2 * half :, :] = jnp.zeros((last_rows, width), bf16)
    part[first + 2 * half :, :rows] = lat_sum[span : span + last_rows, :rows]
    trade.wait_recv()
    kept = down[pl.ds(y * half, half), :] + traded[...]
    part[first : first + half, :] = kept[:, :width]
    part[first + half : first + 2 * half, :] = jnp.zeros((half, width), bf16)
    part[first + half : first + 2 * half, : PACK - width] = kept[:, width:]
    for copy in swaps:
        copy.wait_recv()
    for copy in n_sends + swaps + [raw_x, raw_m, raw_r, trade]:
        copy.wait_send()


def finish(operands, name_id):
    gq, x, w_in = operands[0], operands[9], operands[6]
    span, width, rows = x.shape[0], gq.shape[1], w_in.shape[0] // 4
    part_rows = QR + KR + rows + 16
    each = span + EXTRA
    buffer = lambda *shape: pltpu.VMEM(shape, bf16)
    return remote_call(
        finish_kernel,
        name_id,
        (jax.ShapeDtypeStruct((part_rows, width), bf16), jax.ShapeDtypeStruct((span, D), f32)),
        [
            buffer(8 * each, PACK),
            buffer(each, PACK),
            buffer(4, each, PACK),
            buffer(4, each, PACK),
        ]
        + [buffer(2, each // 2, PACK)] * 4
        + [
            buffer(4 * span, rows),
            buffer(4, (QR + KR) // 4, width),
            buffer(span, PACK),
            buffer(4 * span, PACK),
            buffer(rows, PACK),
            buffer(rows // 2, PACK),
        ],
        20,
        operands,
    )


def gain_grad(gain, pairs):
    return sum(jnp.sum(w.astype(f32) * grad, axis=1) for w, grad in pairs) / gain


def unpack_kernel(
    total, qup, lup, qd, ld, gain_a, gain_q, gain_l, up, lu, out, qg, lg, a_out, q_out, l_out, f_out
):
    width = total.shape[2]
    heads = width // LANES
    q_rows, l_rows = qup.shape[0], lup.shape[0]
    rows = q_rows + l_rows
    each = heads * DV
    base = D // width * each
    lane = lax.broadcasted_iota(jnp.int32, (q_rows, LANES), 1)
    own = DN + DR

    def head(number):
        seat, side = number // (2 * heads), number // heads % 2
        at = number % heads * LANES
        begin = base + seat * rows
        return total[side, begin : begin + q_rows, at : at + LANES].astype(f32)

    turn = lambda values, by: pltpu.roll(values, by % LANES, 1)
    q_sum = jnp.zeros((q_rows, 1), f32)
    for first in range(0, H, 4):
        a, b, c, d = (head(first + i) for i in range(4))
        merged = (
            jnp.where(lane < own, a, turn(b, own)),
            jnp.where(lane < 2 * own - LANES, turn(b, -32), turn(c, 2 * own - LANES)),
            jnp.where(lane < own - DN, turn(c, -DN), turn(d, own - DN)),
        )
        for i, values in enumerate(merged):
            at = first * own + i * LANES
            up[:, at : at + LANES] = values
            q_sum += jnp.sum(values * qup[:, at : at + LANES].astype(f32), axis=1, keepdims=True)
    q_out[...] = q_sum / gain_q[...].astype(f32)
    l_sum = jnp.zeros((l_rows, 1), f32)
    for seat in range(4):
        for side in range(2):
            at = (seat * 2 + side) * width
            first = base + seat * rows + q_rows
            values = total[side, first : first + l_rows, :].astype(f32)
            lu[:, at : at + width] = values
            l_sum += jnp.sum(values * lup[:, at : at + width].astype(f32), axis=1, keepdims=True)
    l_out[...] = l_sum / gain_l[...].astype(f32)
    for part in range(D // width):
        for side in range(2):
            at = part * each
            out[side * each : (side + 1) * each, part * width : (part + 1) * width] = total[
                side, at : at + each, :
            ].astype(f32)
    first = base + 4 * rows
    half = qd.shape[0] // 2
    f_out[...] = total[0, first + 2 * half : first + 2 * half + 1, : f_out.shape[1]].astype(f32)
    for side in range(2):
        mine = slice(side * half, (side + 1) * half)
        left = total[side, first : first + half, :].astype(f32)
        right = total[side, first + half : first + 2 * half, : PACK - width].astype(f32)
        qg[mine, :width] = left
        qg[mine, width:] = right[:, : QR - width]
        lg[mine, :] = right[:, QR - width : DOWN - width]
        weighted = jnp.sum(left * qd[mine, :width].astype(f32), axis=1, keepdims=True)
        weighted += jnp.sum(
            right[:, : QR - width] * qd[mine, width:].astype(f32), axis=1, keepdims=True
        )
        weighted += jnp.sum(
            right[:, QR - width : DOWN - width] * ld[mine, :].astype(f32), axis=1, keepdims=True
        )
        a_out[mine, :] = weighted / gain_a[mine, :].astype(f32)


def unpack(total, qup, lup, qd, ld, gain_a, gain_q, gain_l):
    shape = lambda *dims: jax.ShapeDtypeStruct(dims, f32)
    rows = lambda weight: weight.shape[0]
    return pl.pallas_call(
        unpack_kernel,
        out_shape=(
            shape(*qup.shape),
            shape(*lup.shape),
            shape(rows(qd), D),
            shape(*qd.shape),
            shape(*ld.shape),
            shape(rows(qd), 1),
            shape(rows(qup), 1),
            shape(rows(lup), 1),
            shape(1, rows(qd)),
        ),
        compiler_params=pltpu.CompilerParams(vmem_limit_bytes=60 * MIB),
        cost_estimate=pl.CostEstimate(flops=0, bytes_accessed=24 * MIB, transcendentals=0),
    )(total, qup, lup, qd, ld, gain_a[:, None], gain_q[:, None], gain_l[:, None])


def body(
    layer_input,
    segment_ids,
    attn_gain,
    query_down,
    query_gain,
    query_up,
    latent_down,
    latent_gain,
    latent_up,
    attn_output,
    ffn_gain,
    gate_up,
    down_proj,
    cotangent,
):
    span = layer_input.shape[1]
    length = segment_ids.shape[1]
    n_f = lax.axis_size("fsdp")
    n_c = lax.axis_size("ctx")
    n_h = n_c if H % (n_f * n_c) == 0 else 1
    square = n_f == 4 and n_c == 2 and lax.axis_size("dp") == 4
    heads = H // (n_f * n_h)
    ctx = lax.axis_index("ctx") if n_h > 1 else 0
    fsdp = lax.axis_index("fsdp")
    group = lax.axis_index(("dp", "ctx"))
    place = jnp.reshape(group, (1,)).astype(jnp.int32)
    offset = lax.axis_index(PLANE) * span

    seg = segment_ids[0]
    seg_col = seg[:, None]
    seg_row = seg[None, :]
    own_q = heads * (DN + DR)
    own_kv = heads * (DN + DV)

    def own_columns(weight, width):
        rows = weight.shape[0]
        parts = weight.reshape(rows, n_f, n_h, width)
        parts = lax.dynamic_index_in_dim(parts, ctx, 2, keepdims=False)
        parts = jnp.transpose(parts, (1, 0, 2))
        return lax.all_to_all(parts, "fsdp", 0, 0, tiled=False).reshape(rows * n_f, width)

    wo = lax.dynamic_slice_in_dim(attn_output, ctx * heads * DV, heads * DV, 0)
    wo = jnp.pad(wo.reshape(heads, DV, D), ((0, 0), (LANES - DV, 0), (0, 0)))
    wo = wo.reshape(heads * LANES, D)
    def gather_plane(shard, name_id):
        if square:
            return plane_gather(shard, name_id)
        return lax.all_gather(shard, PLANE, axis=0, tiled=True)

    def scatter_plane(part, name_id):
        if square:
            return plane_scatter(part, name_id)
        if n_h > 1:
            return lax.psum_scatter(part, PLANE, scatter_dimension=0, tiled=True)
        half = length // n_c
        part = lax.dynamic_slice_in_dim(part, lax.axis_index("ctx") * half, half, 0)
        return lax.psum_scatter(part, "fsdp", scatter_dimension=0, tiled=True)

    def gather_heads(part):
        return lax.all_gather(part, "ctx", axis=0) if n_h > 1 else part[None]

    inputs = layer_input[0].astype(f32)
    grad_out = cotangent[0].astype(f32)
    if square:
        lat, wq, wl, w_down_in, raw, normed_in, gains, cos_all, sin_all = front(
            layer_input[0],
            query_down,
            latent_down,
            (attn_gain, ffn_gain, query_gain, latent_gain),
            query_up,
            latent_up,
            seg_col,
            seg_row,
            heads,
            1,
        )
        g_attn, g_ffn, g_query, g_latent = gains[0], gains[1], gains[2, :QR], gains[3, :KR]
    else:
        gather = lambda shard: lax.all_gather(shard, "fsdp", axis=0, tiled=True)
        g_attn, g_ffn, g_query, g_latent = (
            gather(g).astype(f32) for g in (attn_gain, ffn_gain, query_gain, latent_gain)
        )
        blank = jnp.zeros((query_down.shape[0], PACK - DOWN), bf16)
        w_down_in = gather(jnp.concatenate([query_down, latent_down, blank], axis=1))
        wq = own_columns(query_up, own_q).reshape(QR, heads, DN + DR)
        wq = jnp.pad(wq, ((0, 0), (0, 0), (0, LANES - DN - DR))).reshape(QR, heads * LANES)
        wl = own_columns(latent_up, own_kv)
        starts = [jnp.sum((seg < number).astype(jnp.int32)) for number in range(4)]
        doc_start = sum(jnp.where(seg == number, starts[number], 0) for number in range(1, 4))
        cosine, sine = angles((jnp.arange(length, dtype=jnp.int32) - doc_start).astype(f32))
        ones = jnp.ones((length, DN), f32)
        rest = jnp.zeros((length, LANES - DN - DR), f32)
        cos_all = jnp.concatenate([ones, cosine, cosine, rest], axis=1)
        sin_all = jnp.concatenate([0.0 * ones, sine, sine, rest], axis=1)
        cos_own = lax.dynamic_slice_in_dim(cosine, offset, span, 0)
        sin_own = lax.dynamic_slice_in_dim(sine, offset, span, 0)
        normed_in = normalize(inputs, g_attn).astype(bf16)
        raw = dot(normed_in, w_down_in)
        query_normed = normalize(raw[:, :QR], g_query).astype(bf16)
        latent = normalize(raw[:, QR : QR + KR], g_latent).astype(bf16)
        key_rope = rotate(raw[:, QR + KR : DOWN], cos_own, sin_own).astype(bf16)
        key_rope = jnp.pad(key_rope, ((0, 0), (DN, LANES - DN - DR)))
        lat = jnp.concatenate([query_normed, latent, key_rope], axis=1)
        lat = lax.all_gather(lat, PLANE, axis=0, tiled=True)
    query_latent = raw[:, :QR]
    latent_pre = raw[:, QR : QR + KR]
    operands = (lat, wq, wl, cos_all, sin_all, seg_col, seg_row)
    if square:
        cot_z = lax.all_gather(cotangent[0], "dp", axis=0)
        q, k, kv, o, lse, cot_all = attend(*operands, cotangent[0], 4 * length, 2)
        diagonal = ((1 - ctx) * 4 + (fsdp + 2) % 4) * span
        cot_far = lax.all_gather(
            lax.dynamic_slice(cot_all, (diagonal, 0), (span, D)), "dp", axis=0
        )
    else:
        cot_all = lax.all_gather(cotangent[0], ALL, axis=0, tiled=True)
        q, k, kv, o, lse = attend(*operands)
    branch = scatter_plane(dot(o, wo).astype(bf16), 3)
    resid = inputs + RESIDUAL_SCALE * branch.astype(f32)

    ffn_in = normalize(resid, g_ffn).astype(bf16)
    own = n_f * span
    if square:
        ffn_in, cot_z = lax.optimization_barrier((ffn_in, cot_z))
        x_z = lax.all_gather(ffn_in, "dp", axis=0)
        h_all, g_all, gx, y_keep, y_send, x_all = ffn_group(
            ffn_in, cot_all, gate_up, down_proj, 4
        )
        x_far = lax.all_gather(lax.dynamic_slice(x_all, (diagonal, 0), (span, D)), "dp", axis=0)
    else:
        x_own = lax.all_gather(ffn_in, "fsdp", axis=0, tiled=True)
        h_all, g_all, y_part, gx_part = ffn_own(place, x_own, cot_all, gate_up, down_proj)
        gx = lax.psum_scatter(gx_part, "fsdp", scatter_dimension=0, tiled=True)
        y = lax.psum_scatter(y_part, "fsdp", scatter_dimension=0, tiled=True).astype(f32)
    gx = gx.astype(f32)
    grad_resid_add, ffn_gain_part = norm_back(resid, g_ffn, gx)
    grad_resid = grad_out + grad_resid_add
    gb = (RESIDUAL_SCALE * grad_resid).astype(bf16)
    if square:
        gb, cot_far = lax.optimization_barrier((gb, cot_far))
    gb = gather_plane(gb, 6)
    operands = (gb, wo, q, k, kv, o, lse, cos_all, sin_all, seg_col, seg_row)
    if square:
        bulk = (x_z, cot_z, cot_far, x_all, cot_all)
        gq, gkv, rope, out_part, x_all, cot_all = attend_back(*operands, bulk, 4 * length, 9)
        rope, out_part, x_z, x_far = lax.optimization_barrier((rope, out_part, x_z, x_far))
        width = heads * LANES
        out_part = [out_part[:, at : at + width] for at in range(0, D, width)]
        out_total = lax.psum(jnp.concatenate(out_part[:-1], axis=0), "dp")
    else:
        x_all = lax.all_gather(ffn_in, ALL, axis=0, tiled=True)
        gq, gkv, rope, out_part = attend_back(*operands)
    width = heads * LANES
    q_rows, l_rows = QR // n_f, KR // n_f
    if square:
        part, input_grad = finish(
            (
                gq,
                gkv,
                rope,
                lat,
                wq,
                wl,
                w_down_in,
                raw,
                normed_in,
                layer_input[0],
                grad_resid,
                gains,
                cos_all,
                sin_all,
                ffn_gain_part[None],
            ),
            7,
        )
    else:
        lat_part = jnp.concatenate([dot(gq, wq, NT), dot(gkv, wl, NT), rope], axis=1).astype(bf16)
        extra = jnp.pad(ffn_gain_part.astype(bf16).reshape(n_f, -1), ((0, 0), (0, PACK - D // n_f)))
        extra = jnp.broadcast_to(extra[None, :, None], (n_c, n_f, EXTRA, PACK))
        extra = extra.reshape(n_c * n_f, EXTRA, PACK)
        lat_part = jnp.concatenate([lat_part.reshape(n_c * n_f, span, PACK), extra], axis=1)
        lat_sum = scatter_plane(lat_part.reshape(-1, PACK), 7).astype(f32)
        lat_grad = lat_sum[:span]
        ffn_gain_plane = lat_sum[span, : D // n_f]
        query_pre = norm_back(query_latent, g_query, lat_grad[:, :QR])[0]
        latent_back = norm_back(latent_pre, g_latent, lat_grad[:, QR : QR + KR])[0]
        rope_back = unrotate(lat_grad[:, QR + KR + DN : QR + KR + DN + DR], cos_own, sin_own)
        raw_grad = jnp.concatenate(
            [query_pre, latent_back, rope_back, jnp.zeros((span, PACK - DOWN), f32)], axis=1
        ).astype(bf16)
        input_add = norm_back(inputs, g_attn, dot(raw_grad, w_down_in, NT))[0]
        input_grad = grad_resid + input_add

        own_rows = D // n_f
        n_all = lax.all_to_all(
            jnp.transpose(normed_in.reshape(span, n_f, own_rows), (1, 0, 2)), "fsdp", 0, 0
        ).reshape(n_f * span, own_rows)
        raw_all = lax.all_gather(raw_grad, "fsdp", axis=0, tiled=True)
        down_in_part = dot(n_all, raw_all, TN)[:, :DOWN]
        gain_column = ffn_gain_plane[:, None] / n_c
        blank = jnp.zeros((own_rows, PACK - DOWN - 1), f32)
        down_in_part = jnp.concatenate([down_in_part, gain_column, blank], axis=1).astype(bf16)
        width = heads * LANES
        out_part = [out_part[:, at : at + width] for at in range(0, D, width)]
        up_part = dot(lat[:, :QR], gq, TN).astype(bf16).reshape(n_f, -1, width)
        lup_part = dot(lat[:, QR : QR + KR], gkv, TN).astype(bf16).reshape(n_f, -1, width)
        swap = lax.all_to_all(jnp.concatenate([up_part, lup_part], axis=1), "fsdp", 0, 0)
        q_rows, l_rows = QR // n_f, KR // n_f
        pieces = [swap.reshape(-1, width)] + out_part
        part = jnp.concatenate(pieces, axis=0)

    if square:
        part, x_z, y_keep, y_send, out_total = lax.optimization_barrier(
            (part, x_z, y_keep, y_send, out_total)
        )
        total = lax.psum(jnp.concatenate([out_part[-1], part], axis=0), "dp")
        y_far = lax.ppermute(y_send, "fsdp", [(i, (i + 2) % 4) for i in range(4)])
        y = y_keep.astype(f32) + y_far.astype(f32)
        x_all, cot_all, h_all, g_all = ffn_others(
            x_z, cot_z, x_far, cot_far, x_all, cot_all, h_all, g_all, gate_up, down_proj, 10
        )
    else:
        part, x_all = lax.optimization_barrier((part, x_all))
        total = lax.psum(part, "dp")
        h_all, g_all = ffn_rest(place, x_all, cot_all, gate_up, down_proj, h_all, g_all, own)
    output = resid + RESIDUAL_SCALE * y
    if square:
        out_total, total, h_all = lax.optimization_barrier((out_total, total, h_all))
        total = jnp.concatenate([out_total, total], axis=0)
    else:
        total, h_all = lax.optimization_barrier((total, h_all))
    total = gather_heads(total)
    if square:
        gate_up_grad, down_grad = ffn_grads(g_all, h_all, x_all, cot_all)
    else:
        gate_up_grad = lax.dot_general(
            g_all, x_all, (((2,), (0,)), ((), ())), preferred_element_type=f32
        )
        down_grad = dot(h_all, cot_all) * RESIDUAL_SCALE

    if square:
        up_grad, lup_grad, out_grad, q_down_grad, l_down_grad, ga, gq, gl, gf = unpack(
            total,
            query_up,
            latent_up,
            query_down,
            latent_down,
            attn_gain,
            query_gain,
            latent_gain,
        )
        gain_grads = [ga[:, 0], gq[:, 0], gl[:, 0], gf[0]]
    else:
        down_in_sum = lax.psum(down_in_part, ("dp", "ctx")).astype(f32)
        swapped_rows = n_f * (q_rows + l_rows)
        both = total[:, :swapped_rows].reshape(n_h, n_f, q_rows + l_rows, heads, LANES)
        up_grad = jnp.transpose(both[:, :, :q_rows, :, : DN + DR], (2, 1, 0, 3, 4))
        up_grad = up_grad.reshape(q_rows, -1).astype(f32)
        lup_grad = jnp.transpose(both[:, :, q_rows:], (2, 1, 0, 3, 4))
        lup_grad = lup_grad.reshape(l_rows, -1).astype(f32)
        out_grad = total[:, swapped_rows:].reshape(n_h, D // width, heads * DV, width)
        out_grad = jnp.transpose(out_grad, (0, 2, 1, 3)).reshape(-1, D).astype(f32)
        q_down_grad = down_in_sum[:, :QR]
        l_down_grad = down_in_sum[:, QR:DOWN]
        downs = [(query_down, q_down_grad), (latent_down, l_down_grad)]
        gain_grads = [
            gain_grad(attn_gain.astype(f32), downs),
            gain_grad(query_gain.astype(f32), [(query_up, up_grad)]),
            gain_grad(latent_gain.astype(f32), [(latent_up, lup_grad)]),
            down_in_sum[:, DOWN],
        ]

    return (
        output.astype(bf16)[None],
        input_grad[None],
        gain_grads[0],
        q_down_grad,
        gain_grads[1],
        up_grad,
        l_down_grad,
        gain_grads[2],
        lup_grad,
        out_grad,
        gain_grads[3],
        gate_up_grad,
        down_grad,
    )


def solution(mesh):
    in_specs = (
        P("dp", ("ctx", "fsdp"), None),
        P("dp", None),
        P("fsdp"),
        P("fsdp", None),
        P("fsdp"),
        P("fsdp", None),
        P("fsdp", None),
        P("fsdp"),
        P("fsdp", None),
        P("fsdp", None),
        P("fsdp"),
        P(None, "fsdp", None),
        P("fsdp", None),
        P("dp", ("ctx", "fsdp"), None),
    )
    out_specs = (
        P("dp", ("ctx", "fsdp"), None),
        P("dp", ("ctx", "fsdp"), None),
        P("fsdp"),
        P("fsdp", None),
        P("fsdp"),
        P("fsdp", None),
        P("fsdp", None),
        P("fsdp"),
        P("fsdp", None),
        P("fsdp", None),
        P("fsdp"),
        P(None, "fsdp", None),
        P("fsdp", None),
    )
    return jax.shard_map(body, mesh=mesh, in_specs=in_specs, out_specs=out_specs, check_vma=False)
```

```python
import functools
import math

import jax
import jax.numpy as jnp
import numpy as np
from jax import lax
from jax.experimental import pallas as pl
from jax.experimental.pallas import tpu as pltpu
from jax.sharding import PartitionSpec as P

D = 2560
H = 40
DN = 64
DR = 32
DV = 64
QR = 768
KR = 256
LANES = 128
DOWN = QR + KR + DR
PACK = QR + KR + LANES
EXTRA = 32

EPS = 1e-05
RESIDUAL_SCALE = 1.4 / math.sqrt(62.0)
NEGATIVE = -1e30
ROPE_BASE = 10000.0
SCALE = (DN + DR) ** (-0.5)
f32 = jnp.float32
bf16 = jnp.bfloat16

NN = (((1,), (0,)), ((), ()))
NT = (((1,), (1,)), ((), ()))
TN = (((0,), (0,)), ((), ()))
MIB = 1024 * 1024


def dot(left, right, dims=NN):
    return lax.dot_general(left, right, dims, preferred_element_type=f32)


def normalize(values, gain):
    return values * lax.rsqrt(jnp.mean(values * values, axis=-1, keepdims=True) + EPS) * gain


def norm_back(values, gain, grad):
    primal, pullback = jax.vjp(normalize, values, gain)
    return pullback(grad)


def angles(positions):
    half = DR // 2
    frequency = ROPE_BASE ** (-jnp.arange(half, dtype=f32) / half)
    theta = positions[:, None] * frequency[None, :]
    return (jnp.cos(theta), jnp.sin(theta))


def rotate(values, cosine, sine):
    half = values.shape[-1] // 2
    first = values[..., :half]
    second = values[..., half:]
    return jnp.concatenate(
        [first * cosine - second * sine, second * cosine + first * sine], axis=-1
    )


def unrotate(grad, cosine, sine):
    return rotate(grad, cosine, -sine)


def swapped(values):
    lane = lax.broadcasted_iota(jnp.int32, values.shape, 1)
    up = pltpu.roll(values, LANES - DR // 2, 1)
    back = pltpu.roll(values, DR // 2, 1)
    return jnp.where(lane < DN + DR // 2, up, -back)


def allowed(seg_col, seg_row, first, rows, columns):
    query = first + lax.broadcasted_iota(jnp.int32, (rows, columns), 0)
    key = lax.broadcasted_iota(jnp.int32, (rows, columns), 1)
    return (seg_col[first : first + rows, :] == seg_row[:, :columns]) & (key <= query)


PLANE = ("ctx", "fsdp")
ALL = ("dp", "ctx", "fsdp")
MESH = pl.DeviceIdType.MESH


def seats():
    y = lax.axis_index("ctx")
    f = lax.axis_index("fsdp")
    core = lax.rem(f, 2)
    mate = {"fsdp": f + 1 - 2 * core}
    along_x = {"fsdp": lax.rem(f + 2, 4)}
    along_y = {"ctx": 1 - y}
    return y, f, core, mate, along_x, along_y


def greet(peers):
    barrier = pltpu.get_barrier_semaphore()
    for peer in peers:
        pl.semaphore_signal(barrier, inc=1, device_id=peer, device_id_type=MESH)
    pl.semaphore_wait(barrier, len(peers))


class Wires:
    def __init__(self, send, recv):
        self.send, self.recv, self.count = send, recv, 0

    def copy(self, src, dst, peer):
        at = self.count
        self.count += 1
        return pltpu.make_async_remote_copy(
            src_ref=src,
            dst_ref=dst,
            send_sem=self.send.at[at],
            recv_sem=self.recv.at[at],
            device_id=peer,
            device_id_type=MESH,
        )


class Spread:
    wires_needed = 9

    def __init__(self, wires, src, out, base, local):
        rows = src.shape[0]
        half = rows // 2
        y, f, core, mate, along_x, along_y = seats()
        x_f = lax.rem(f + 2, 4)
        me, x_seat, y_seat, far = y * 4 + f, y * 4 + x_f, (1 - y) * 4 + f, (1 - y) * 4 + x_f
        at = lambda seat, first, count: out.at[
            pl.ds(pl.multiple_of(base + seat * rows + first, 16), count)
        ]
        whole = lambda seat: at(seat, 0, rows)
        upper = lambda seat: at(seat, 0, half)
        lower = lambda seat: at(seat, half, half)
        self.keep = pltpu.make_async_copy(src, whole(me), local)
        self.mine = [wires.copy(src, whole(me), peer) for peer in (along_x, along_y, mate)]
        self.pass_y = wires.copy(upper(x_seat), upper(x_seat), along_y)
        self.pass_x = wires.copy(lower(y_seat), lower(y_seat), along_x)
        self.mate_x = wires.copy(whole(x_seat), whole(x_seat), mate)
        self.mate_y = wires.copy(whole(y_seat), whole(y_seat), mate)
        self.mate_u = wires.copy(upper(far), upper(far), mate)
        self.mate_l = wires.copy(lower(far), lower(far), mate)

    def start(self):
        for copy in self.mine:
            copy.start()
        self.keep.start()

    def relay(self):
        self.mine[0].wait_recv()
        self.pass_y.start()
        self.mate_x.start()
        self.mine[1].wait_recv()
        self.pass_x.start()
        self.mate_y.start()

    def finish(self):
        self.pass_y.wait_recv()
        self.mate_u.start()
        self.pass_x.wait_recv()
        self.mate_l.start()
        for copy in (self.mine[2], self.mate_x, self.mate_y, self.mate_u, self.mate_l):
            copy.wait_recv()
        rest = [self.pass_y, self.pass_x, self.mate_x, self.mate_y, self.mate_u, self.mate_l]
        for copy in self.mine + rest:
            copy.wait_send()
        self.keep.wait()


class Light:
    wires_needed = 6

    def __init__(self, wires, src, far_src, stage, out, base, local):
        rows = src.shape[0]
        y, f, core, mate, along_x, along_y = seats()
        x_f = lax.rem(f + 2, 4)
        me, x_seat, y_seat, far = y * 4 + f, y * 4 + x_f, (1 - y) * 4 + f, (1 - y) * 4 + x_f
        at = lambda seat: out.at[pl.ds(pl.multiple_of(base + seat * rows, 16), rows)]
        self.fetch = [
            pltpu.make_async_copy(src, stage.at[0], local.at[0]),
            pltpu.make_async_copy(far_src, stage.at[1], local.at[1]),
        ]
        self.keep = [
            pltpu.make_async_copy(stage.at[0], at(me), local.at[2]),
            pltpu.make_async_copy(stage.at[1], at(far), local.at[3]),
        ]
        self.mine = [wires.copy(stage.at[0], at(me), peer) for peer in (along_x, along_y, mate)]
        self.far = wires.copy(stage.at[1], at(far), mate)
        self.mate_x = wires.copy(at(x_seat), at(x_seat), mate)
        self.mate_y = wires.copy(at(y_seat), at(y_seat), mate)

    def load(self):
        for copy in self.fetch:
            copy.start()

    def start(self):
        for copy in self.fetch:
            copy.wait()
        for copy in self.mine + [self.far] + self.keep:
            copy.start()

    def relay(self):
        self.mine[0].wait_recv()
        self.mate_x.start()
        self.mine[1].wait_recv()
        self.mate_y.start()

    def finish(self):
        for copy in (self.mine[2], self.far, self.mate_x, self.mate_y):
            copy.wait_recv()
        for copy in self.mine + [self.far, self.mate_x, self.mate_y]:
            copy.wait_send()
        for copy in self.keep:
            copy.wait()


def turn_z(step):
    return lax.rem(lax.axis_index("dp") + step, lax.axis_size("dp"))


def attend_kernel(
    block, units, lat, wq, wl, cos, sin, seg_col, seg_row, *rest
):
    sources, rest = rest[: 2 * units], rest[2 * units :]
    (q_out, k_out, kv_out, o_out, lse_out), rest = rest[:5], rest[5:]
    length = lat.shape[0]
    if units:
        out, branch_out, heads_out, local, send, recv = rest
        unit = Spread(Wires(send, recv), sources[0], out, 0, local.at[0])

        @pl.when(pl.program_id(0) == 0)
        def _():
            seat = seats()
            greet(seat[3:])
            unit.start()

        @pl.when(pl.program_id(0) == 3)
        def _():
            unit.relay()

    lane = lax.broadcasted_iota(jnp.int32, (length, LANES), 1)
    query = dot(lat[:, :QR], wq[...])
    query = (query * cos[...] - swapped(query) * sin[...]).astype(bf16)
    both = dot(lat[:, QR : QR + KR], wl[...]).astype(bf16)
    key = jnp.where(lane < DN, both, lat[:, QR + KR :])
    q_out[...] = query
    k_out[...] = key
    kv_out[...] = both
    for first in range(0, length, block):
        last = first + block
        scores = dot(query[first:last], key[:last], NT) * SCALE
        scores = jnp.where(allowed(seg_col, seg_row, first, block, last), scores, NEGATIVE)
        peak = jnp.max(scores, axis=-1, keepdims=True)
        weights = jnp.exp(scores - peak)
        total = jnp.sum(weights, axis=-1, keepdims=True)
        probs = (weights * (1.0 / total)).astype(bf16)
        o_out[first:last, :] = dot(probs, both[:last]).astype(bf16)
        lse_out[0, first:last, :] = peak + jnp.log(total)
    if units:
        here = pl.ds(pl.multiple_of(pl.program_id(0) * LANES, LANES), LANES)
        heads_out[:, here] = o_out[...]

        @pl.when(pl.program_id(0) == pl.num_programs(0) - 1)
        def _():
            for first in range(0, length, block):
                rows = slice(first, first + block)
                branch_out[rows, :] = dot(heads_out[rows, :], sources[1][...]).astype(bf16)
            unit.finish()


def attend(lat, wq, wl, cos, sin, seg_col, seg_row, cot=None, wo=None, tokens=0, name_id=0):
    length = lat.shape[0]
    heads = wq.shape[1] // LANES
    whole = lambda shape: pl.BlockSpec(shape, lambda h: (0,) * len(shape))
    mine = lambda rows: pl.BlockSpec((rows, LANES), lambda h: (0, h))
    anywhere = [pl.BlockSpec(memory_space=pl.ANY)]
    wide = jax.ShapeDtypeStruct((length, heads * LANES), bf16)
    units = 0 if cot is None else 1
    wires = Spread.wires_needed
    params = dict(collective_id=name_id, has_side_effects=True) if units else {}
    return pl.pallas_call(
        functools.partial(attend_kernel, min(256, length), units),
        grid=(heads,),
        in_specs=[
            whole((length, PACK)),
            mine(QR),
            mine(KR),
            whole((length, LANES)),
            whole((length, LANES)),
            whole((length, 1)),
            whole((1, length)),
        ]
        + [whole((length // 8, D)), whole((heads * LANES, D))] * units,
        out_specs=[mine(length)] * 4
        + [pl.BlockSpec((1, length, 1), lambda h: (h, 0, 0))]
        + (anywhere + [whole((length, D))]) * units,
        out_shape=[wide] * 4
        + [jax.ShapeDtypeStruct((heads, length, 1), f32)]
        + [jax.ShapeDtypeStruct((tokens, D), bf16), jax.ShapeDtypeStruct((length, D), bf16)] * units,
        scratch_shapes=[
            pltpu.VMEM((length, heads * LANES), bf16),
            pltpu.SemaphoreType.DMA((1,)),
            pltpu.SemaphoreType.DMA((wires,)),
            pltpu.SemaphoreType.DMA((wires,)),
        ]
        if units
        else [],
        compiler_params=pltpu.CompilerParams(vmem_limit_bytes=56 * MIB, **params),
        cost_estimate=pl.CostEstimate(
            flops=heads * length * (length * 4 * LANES + 2 * LANES * (QR + KR)),
            bytes_accessed=heads * length * LANES * 16,
            transcendentals=heads * length * length,
        ),
    )(lat, wq, wl, cos, sin, seg_col, seg_row, *([cot, wo] if units else []))


def attend_back_kernel(
    block, units, gb, wo, q, k, kv, o, lse, cos, sin, seg_col, seg_row, *rest
):
    sources, rest = rest[: 5 * units], rest[5 * units :]
    (gq_out, gkv_out, rope_out, wo_out), rest = rest[:4], rest[4:]
    length = gb.shape[0]
    if units:
        x_z, cot_z, cot_far, _, _ = sources
        x_all, cot_all, dk, dv, stage, local, send, recv = rest
        wires = Wires(send, recv)
        z = turn_z(1)
        fetch = pltpu.make_async_copy(x_z.at[z], stage.at[2], local.at[5])
        first_unit = Spread(wires, stage.at[2], x_all, length, local.at[4])
        second_unit = Light(
            wires, cot_z.at[z], cot_far.at[z], stage, cot_all, length, local
        )

        @pl.when(pl.program_id(0) == 0)
        def _():
            fetch.start()
            second_unit.load()
            seat = seats()
            greet(seat[3:])
            fetch.wait()
            first_unit.start()
            second_unit.start()

        @pl.when(pl.program_id(0) == 3)
        def _():
            first_unit.relay()
            second_unit.relay()

    else:
        dk, dv = rest
    wo_out[...] = dot(o[...], gb[...], TN)[LANES - DV :].astype(bf16)
    lane = lax.broadcasted_iota(jnp.int32, (length, LANES), 1)
    grad = dot(gb[...], wo[...], NT).astype(bf16)
    dk[...] = jnp.zeros_like(dk)
    dv[...] = jnp.zeros_like(dv)
    for first in range(0, length, block):
        last = first + block
        scores = dot(q[first:last, :], k[:last, :], NT) * SCALE
        probs = jnp.exp(scores - lse[0, first:last, :])
        probs = jnp.where(allowed(seg_col, seg_row, first, block, last), probs, 0.0)
        grad_probs = dot(grad[first:last], kv[:last, :], NT)
        delta = jnp.sum(probs * grad_probs, axis=-1, keepdims=True)
        grad_scores = (probs * (grad_probs - delta)).astype(bf16)
        gq = dot(grad_scores, k[:last, :]) * SCALE
        gq = gq * cos[first:last, :] + swapped(gq) * sin[first:last, :]
        gq_out[first:last, :] = gq.astype(bf16)
        dk[:last, :] += dot(grad_scores, q[first:last, :], TN) * SCALE
        dv[:last, :] += dot(probs.astype(bf16), grad[first:last], TN)
    gkv_out[...] = jnp.where(lane < DN, dk[...], dv[...]).astype(bf16)

    @pl.when(pl.program_id(0) == 0)
    def _():
        rope_out[...] = dk[...]

    @pl.when(pl.program_id(0) > 0)
    def _():
        rope_out[...] += dk[...]

    if units:

        @pl.when(pl.program_id(0) == pl.num_programs(0) - 1)
        def _():
            first_unit.finish()
            second_unit.finish()


def attend_back(gb, wo, q, k, kv, o, lse, cos, sin, seg_col, seg_row, bulk=(), tokens=0, name_id=0):
    units = 1 if bulk else 0
    wires = Spread.wires_needed + Light.wires_needed
    anywhere = [pl.BlockSpec(memory_space=pl.ANY)]
    params = dict(collective_id=name_id, has_side_effects=True) if units else {}
    length = gb.shape[0]
    heads = q.shape[1] // LANES
    whole = lambda shape: pl.BlockSpec(shape, lambda h: (0,) * len(shape))
    mine = pl.BlockSpec((length, LANES), lambda h: (0, h))
    wide = jax.ShapeDtypeStruct((length, heads * LANES), bf16)
    return pl.pallas_call(
        functools.partial(attend_back_kernel, min(256, length), units),
        grid=(heads,),
        in_specs=[
            whole((length, D)),
            pl.BlockSpec((LANES, D), lambda h: (h, 0)),
            mine,
            mine,
            mine,
            mine,
            pl.BlockSpec((1, length, 1), lambda h: (h, 0, 0)),
            whole((length, LANES)),
            whole((length, LANES)),
            whole((length, 1)),
            whole((1, length)),
        ]
        + anywhere * (5 * units),
        out_specs=[
            mine,
            mine,
            whole((length, LANES)),
            pl.BlockSpec((DV, D), lambda h: (h, 0)),
        ]
        + anywhere * (2 * units),
        input_output_aliases={14: 4, 15: 5} if units else {},
        out_shape=[
            wide,
            wide,
            jax.ShapeDtypeStruct((length, LANES), f32),
            jax.ShapeDtypeStruct((heads * DV, D), bf16),
        ]
        + [jax.ShapeDtypeStruct((tokens, D), bf16)] * (2 * units),
        scratch_shapes=[pltpu.VMEM((length, LANES), f32), pltpu.VMEM((length, LANES), f32)]
        + [
            pltpu.VMEM((3, length // 8, D), bf16),
            pltpu.SemaphoreType.DMA((6,)),
            pltpu.SemaphoreType.DMA((wires,)),
            pltpu.SemaphoreType.DMA((wires,)),
        ]
        * units,
        compiler_params=pltpu.CompilerParams(vmem_limit_bytes=56 * MIB, **params),
        cost_estimate=pl.CostEstimate(
            flops=heads * length * (length * 10 * LANES + 4 * LANES * D),
            bytes_accessed=heads * length * LANES * 16 + length * D * 2,
            transcendentals=heads * length * length,
        ),
    )(gb, wo, q, k, kv, o, lse, cos, sin, seg_col, seg_row, *bulk)


def hidden_block(x, cot, w_gu, w_down, h_out, g_out, parts):
    units = w_down.shape[0]
    step = units // parts
    for part in range(parts):
        rows = slice(part * step, (part + 1) * step)
        gate = dot(w_gu[0, rows, :], x, NT)
        upper = dot(w_gu[1, rows, :], x, NT)
        grad = dot(w_down[rows, :], cot, NT) * RESIDUAL_SCALE
        sigma = jax.nn.sigmoid(gate)
        silu = gate * sigma
        h_out[rows, :] = (silu * upper).astype(bf16)
        g_out[0, rows, :] = (grad * upper * sigma * (1.0 + gate * (1.0 - sigma))).astype(bf16)
        g_out[1, rows, :] = (grad * silu).astype(bf16)


def ffn_own_kernel(place, x, cot, w_gu, w_down, h_out, g_out, y_out, gx_out):
    hidden_block(x[...], cot[...], w_gu, w_down, h_out, g_out, 2)
    y_out[...] = dot(h_out[...], w_down[...], TN).astype(bf16)
    gx_out[...] = (dot(g_out[0], w_gu[0], TN) + dot(g_out[1], w_gu[1], TN)).astype(bf16)


def ffn_rest_kernel(place, x, cot, w_gu, w_down, h_in, g_in, h_out, g_out):
    hidden_block(x[...], cot[...], w_gu, w_down, h_out, g_out, 2)


def ffn_shapes(units, tokens):
    return [
        jax.ShapeDtypeStruct((units, tokens), bf16),
        jax.ShapeDtypeStruct((2, units, tokens), bf16),
    ]


def ffn_own(place, x, cot_all, w_gu, w_down):
    units = w_down.shape[0]
    tokens = cot_all.shape[0]
    block = min(256, x.shape[0])
    steps = x.shape[0] // block
    kept = pl.Buffered(1)
    return pl.pallas_call(
        ffn_own_kernel,
        grid_spec=pltpu.PrefetchScalarGridSpec(
            num_scalar_prefetch=1,
            grid=(steps,),
            in_specs=[
                pl.BlockSpec((block, D), lambda i, p: (i, 0)),
                pl.BlockSpec((block, D), lambda i, p: (p[0] * steps + i, 0)),
                pl.BlockSpec((2, units, D), lambda i, p: (0, 0, 0), pipeline_mode=kept),
                pl.BlockSpec((units, D), lambda i, p: (0, 0), pipeline_mode=kept),
            ],
            out_specs=[
                pl.BlockSpec((units, block), lambda i, p: (0, p[0] * steps + i)),
                pl.BlockSpec((2, units, block), lambda i, p: (0, 0, p[0] * steps + i)),
                pl.BlockSpec((block, D), lambda i, p: (i, 0)),
                pl.BlockSpec((block, D), lambda i, p: (i, 0)),
            ],
        ),
        out_shape=ffn_shapes(units, tokens) + [jax.ShapeDtypeStruct((x.shape[0], D), bf16)] * 2,
        compiler_params=pltpu.CompilerParams(vmem_limit_bytes=60 * MIB),
        cost_estimate=pl.CostEstimate(
            flops=12 * x.shape[0] * units * D, bytes_accessed=6 * units * D, transcendentals=0
        ),
    )(place, x, cot_all, w_gu, w_down)


def ffn_rest(place, x_all, cot_all, w_gu, w_down, h_all, g_all, own):
    units = w_down.shape[0]
    tokens = x_all.shape[0]
    block = min(256, own)
    steps = own // block
    blocks = tokens // block
    kept = pl.Buffered(1)
    at = lambda i, p: lax.rem((p[0] + 1) * steps + i, blocks)
    return pl.pallas_call(
        ffn_rest_kernel,
        grid_spec=pltpu.PrefetchScalarGridSpec(
            num_scalar_prefetch=1,
            grid=(blocks - steps,),
            in_specs=[
                pl.BlockSpec((block, D), lambda i, p: (at(i, p), 0)),
                pl.BlockSpec((block, D), lambda i, p: (at(i, p), 0)),
                pl.BlockSpec((2, units, D), lambda i, p: (0, 0, 0), pipeline_mode=kept),
                pl.BlockSpec((units, D), lambda i, p: (0, 0), pipeline_mode=kept),
                pl.BlockSpec(memory_space=pl.ANY),
                pl.BlockSpec(memory_space=pl.ANY),
            ],
            out_specs=[
                pl.BlockSpec((units, block), lambda i, p: (0, at(i, p))),
                pl.BlockSpec((2, units, block), lambda i, p: (0, 0, at(i, p))),
            ],
        ),
        out_shape=ffn_shapes(units, tokens),
        input_output_aliases={5: 0, 6: 1},
        compiler_params=pltpu.CompilerParams(vmem_limit_bytes=60 * MIB),
        cost_estimate=pl.CostEstimate(
            flops=6 * (tokens - own) * units * D,
            bytes_accessed=6 * units * D + 10 * tokens * D,
            transcendentals=0,
        ),
    )(place, x_all, cot_all, w_gu, w_down, h_all, g_all)


def remote_call(kernel, name_id, out_shape, scratch, wires, operands):
    return pl.pallas_call(
        kernel,
        out_shape=out_shape,
        in_specs=[pl.BlockSpec(memory_space=pltpu.VMEM)] * len(operands),
        out_specs=jax.tree.map(lambda _: pl.BlockSpec(memory_space=pltpu.VMEM), out_shape),
        scratch_shapes=scratch
        + [pltpu.SemaphoreType.DMA((wires,)), pltpu.SemaphoreType.DMA((wires,))],
        compiler_params=pltpu.CompilerParams(
            collective_id=name_id, has_side_effects=True, vmem_limit_bytes=56 * MIB
        ),
    )(*operands)


def gather_plane_steps(wires, x, out):
    rows = x.shape[0]
    half = rows // 2
    y, f, core, mate, along_x, along_y = seats()
    me = y * 4 + f
    x_seat = y * 4 + lax.rem(f + 2, 4)
    y_seat = (1 - y) * 4 + f
    far = (1 - y) * 4 + lax.rem(f + 2, 4)
    whole = lambda seat: out.at[pl.ds(seat * rows, rows)]
    upper = lambda seat: out.at[pl.ds(seat * rows, half)]
    lower = lambda seat: out.at[pl.ds(seat * rows + half, half)]
    mine_x = wires.copy(x, whole(me), along_x)
    mine_y = wires.copy(x, whole(me), along_y)
    mine_m = wires.copy(x, whole(me), mate)
    mine_x.start()
    mine_y.start()
    mine_m.start()
    out[pl.ds(me * rows, rows), :] = x[...]
    pass_y = wires.copy(upper(x_seat), upper(x_seat), along_y)
    pass_x = wires.copy(lower(y_seat), lower(y_seat), along_x)
    mate_x = wires.copy(whole(x_seat), whole(x_seat), mate)
    mate_y = wires.copy(whole(y_seat), whole(y_seat), mate)
    mate_u = wires.copy(upper(far), upper(far), mate)
    mate_l = wires.copy(lower(far), lower(far), mate)
    mine_x.wait_recv()
    pass_y.start()
    mate_x.start()
    mine_y.wait_recv()
    pass_x.start()
    mate_y.start()
    pass_y.wait_recv()
    mate_u.start()
    pass_x.wait_recv()
    mate_l.start()
    for copy in (mine_m, mate_x, mate_y, mate_u, mate_l):
        copy.wait_recv()
    for copy in (mine_x, mine_y, mine_m, pass_y, pass_x, mate_x, mate_y, mate_u, mate_l):
        copy.wait_send()


def plane_gather_kernel(x, out, send, recv):
    y, f, core, mate, along_x, along_y = seats()
    greet([mate, along_x, along_y])
    gather_plane_steps(Wires(send, recv), x, out)


def plane_gather(x, name_id):
    shape = jax.ShapeDtypeStruct((8 * x.shape[0], x.shape[1]), x.dtype)
    return remote_call(plane_gather_kernel, name_id, shape, [], 9, (x,))


def scatter_plane_steps(wires, part, out, own, from_mate, from_x, from_y, last, relay, fill=None):
    rows = out.shape[0]
    half = rows // 2
    y, f, core, mate, along_x, along_y = seats()
    x_f = lax.rem(f + 2, 4)
    turn = 1 - 2 * core
    seat = [(1 - y) * 4 + x_f, y * 4 + x_f, (1 - y) * 4 + f, y * 4 + f]
    upper, lower = slice(0, half), slice(half, rows)
    to_mate = [
        wires.copy(part.at[pl.ds((s + turn) * rows, rows)], from_mate.at[i], mate)
        for i, s in enumerate(seat)
    ]
    for copy in to_mate:
        copy.start()
    far_x = wires.copy(own.at[0, upper], from_x.at[0], along_x)
    far_y = wires.copy(own.at[0, lower], from_y.at[0], along_y)
    near_x = wires.copy(own.at[1, upper], from_x.at[1], along_x)
    near_y = wires.copy(own.at[2, lower], from_y.at[1], along_y)
    relay_y = wires.copy(relay.at[0], last.at[0], along_y)
    relay_x = wires.copy(relay.at[1], last.at[1], along_x)
    starts = ([far_x, far_y], [near_x], [near_y], [])
    for i in range(4):
        to_mate[i].wait_recv()
        own[i] = part[pl.ds(seat[i] * rows, rows), :] + from_mate[i]
        for copy in starts[i]:
            copy.start()
    if fill is not None:
        fill()
    far_x.wait_recv()
    relay[0] = own[2, upper] + from_x[0]
    relay_y.start()
    far_y.wait_recv()
    relay[1] = own[1, lower] + from_y[0]
    relay_x.start()
    near_x.wait_recv()
    near_y.wait_recv()
    relay_y.wait_recv()
    relay_x.wait_recv()
    add = lambda a, b, c: (a.astype(f32) + b.astype(f32) + c.astype(f32)).astype(out.dtype)
    out[upper, :] = add(own[3, upper], from_x[1], last[0])
    out[lower, :] = add(own[3, lower], from_y[1], last[1])
    for copy in to_mate + [far_x, far_y, near_x, near_y, relay_y, relay_x]:
        copy.wait_send()


def plane_scatter_kernel(part, out, own, from_mate, from_x, from_y, last, relay, send, recv):
    greet(seats()[3:])
    wires = Wires(send, recv)
    scatter_plane_steps(wires, part, out, own, from_mate, from_x, from_y, last, relay)


def plane_scatter(part, name_id):
    rows, width = part.shape[0] // 8, part.shape[1]
    shape = jax.ShapeDtypeStruct((rows, width), part.dtype)
    buffer = lambda count, depth: pltpu.VMEM((count, depth, width), part.dtype)
    scratch = [buffer(4, rows), buffer(4, rows)] + [buffer(2, rows // 2)] * 4
    return remote_call(plane_scatter_kernel, name_id, shape, scratch, 10, (part,))


def take_columns(weight, first, width):
    begin = min(first // LANES * LANES, weight.shape[1] - 2 * LANES)
    window = weight[:, begin : begin + 2 * LANES].astype(f32)
    shift = (2 * LANES - (first - begin)) % (2 * LANES)
    window = (pltpu.roll(window, shift, 1) if shift else window)[:, :LANES]
    lane = lax.broadcasted_iota(jnp.int32, window.shape, 1)
    return jnp.where(lane < width, window, 0.0).astype(bf16)


def front_kernel(
    pieces,
    heads,
    x,
    qd,
    ld,
    gain_a,
    gain_f,
    gain_q,
    gain_l,
    qup,
    lup,
    seg_col,
    seg_row,
    freq,
    lat,
    wq,
    wl,
    w_in,
    raw_out,
    n_out,
    gains_out,
    cos_out,
    sin_out,
    w,
    gains,
    gains_all,
    qpack,
    own,
    send,
    recv,
):
    rows = w.shape[0]
    half = rows // 2
    piece = half // pieces
    span = x.shape[0]
    length = cos_out.shape[0]
    y, f, core, mate, along_x, along_y = seats()
    x_f = lax.rem(f + 2, 4)
    m_f = f + 1 - 2 * core
    c_f = 3 - f
    cross = {"fsdp": c_f}
    wires = Wires(send, recv)

    w[:, :QR] = qd[...]
    w[:, QR:] = jnp.zeros((rows, PACK - QR), bf16)
    w[:, QR:DOWN] = ld[...]
    gains[...] = jnp.zeros_like(gains)
    gains[0:1, : gain_a.shape[1]] = gain_a[...].astype(f32)
    gains[1:2, : gain_f.shape[1]] = gain_f[...].astype(f32)
    gains[2:3, : gain_q.shape[1]] = gain_q[...].astype(f32)
    gains[3:4, : gain_l.shape[1]] = gain_l[...].astype(f32)
    greet([mate, along_x, along_y, cross])

    gains_x = wires.copy(gains, gains_all.at[f], along_x)
    gains_m = wires.copy(gains, gains_all.at[f], mate)
    gains_r = wires.copy(gains_all.at[x_f], gains_all.at[x_f], mate)
    spot = lambda owner, side, i: pl.ds(owner * rows + side * half + i * piece, piece)
    across = [
        wires.copy(w.at[pl.ds(y * half + i * piece, piece)], w_in.at[spot(f, y, i)], along_x)
        for i in range(pieces)
    ]
    mine = wires.copy(w, w_in.at[pl.ds(f * rows, rows)], mate)
    same = lambda side, peer: [
        wires.copy(w_in.at[spot(x_f, side, i)], w_in.at[spot(x_f, side, i)], peer)
        for i in range(pieces)
    ]
    trade = same(y, along_y)
    to_mate = same(y, mate)
    rest = same(1 - y, mate)
    gains_x.start()
    gains_m.start()
    for copy in across:
        copy.start()
    mine.start()
    gains_all[f] = gains[...]
    w_in[pl.ds(f * rows, rows), :] = w[...]

    q_rows, l_rows = qup.shape[0], lup.shape[0]
    for seat in range(4):
        for head in range(heads):
            first = lambda ctx: ((seat * 2 + ctx) * heads + head) * (DN + DR)
            column = jnp.where(
                y == 0,
                take_columns(qup, first(0), DN + DR).astype(f32),
                take_columns(qup, first(1), DN + DR).astype(f32),
            )
            qpack[seat, :, head * LANES : (head + 1) * LANES] = column.astype(bf16)
    width = heads * LANES
    kv_part = lambda seat: lup.at[:, pl.ds(pl.multiple_of((seat * 2 + y) * width, LANES), width)]
    q_spot = wq.at[pl.ds(f * q_rows, q_rows)]
    l_spot = wl.at[pl.ds(f * l_rows, l_rows)]
    swaps = []
    for seat, peer in ((x_f, along_x), (c_f, cross), (m_f, mate)):
        swaps.append(wires.copy(qpack.at[seat], q_spot, peer))
        swaps.append(wires.copy(kv_part(seat), l_spot, peer))
    for copy in swaps:
        copy.start()
    wq[pl.ds(f * q_rows, q_rows), :] = qpack[f]
    wl[pl.ds(f * l_rows, l_rows), :] = lup[
        :, pl.ds(pl.multiple_of((f * 2 + y) * width, LANES), width)
    ]

    index = lax.broadcasted_iota(jnp.int32, (length, 1), 0).astype(f32)
    seg = seg_col[...]
    doc_start = jnp.zeros((length, 1), f32)
    for number in range(1, 4):
        start = jnp.sum((seg_row[...] < number).astype(f32), axis=1, keepdims=True)
        doc_start = jnp.where(seg == number, start, doc_start)
    theta = (index - doc_start) * freq[...]
    lane = lax.broadcasted_iota(jnp.int32, (length, LANES), 1)
    turned = (lane >= DN) & (lane < DN + DR)
    cos_out[...] = jnp.where(turned, jnp.cos(theta), jnp.where(lane < DN, 1.0, 0.0))
    sin_out[...] = jnp.where(turned, jnp.sin(theta), 0.0)

    gains_x.wait_recv()
    gains_r.start()
    gains_m.wait_recv()
    gains_r.wait_recv()
    shard = gain_a.shape[1]
    full = [gains_all[i] for i in range(4)]
    g_attn = jnp.concatenate([full[i][0:1, :shard] for i in range(4)], axis=1)
    g_ffn = jnp.concatenate([full[i][1:2, :shard] for i in range(4)], axis=1)
    placed = [full[0]]
    for i in range(1, 4):
        placed.append(pltpu.roll(full[i], i * gain_q.shape[1], 1))
    g_query = sum(p[2:3] for p in placed)
    placed = [full[0]]
    for i in range(1, 4):
        placed.append(pltpu.roll(full[i], i * gain_l.shape[1], 1))
    g_latent = sum(p[3:4] for p in placed)[:, :KR]
    gains_out[...] = jnp.zeros_like(gains_out)
    gains_out[0:1, :] = g_attn
    gains_out[1:2, :] = g_ffn
    gains_out[2:3, :QR] = g_query
    gains_out[3:4, :KR] = g_latent

    inputs = x[...].astype(f32)
    n_out[...] = normalize(inputs, g_attn).astype(bf16)

    def term(owner):
        left = n_out[:, pl.ds(pl.multiple_of(owner * rows, LANES), rows)]
        return dot(left, w_in[pl.ds(owner * rows, rows), :])

    raw_out[...] = term(f)
    for i in range(pieces):
        across[i].wait_recv()
        trade[i].start()
        to_mate[i].start()
    mine.wait_recv()
    raw_out[...] += term(m_f)
    for i in range(pieces):
        trade[i].wait_recv()
        rest[i].start()
    raw_out[...] += term(x_f)
    for copy in to_mate + rest:
        copy.wait_recv()
    raw_out[...] += term(c_f)

    me = y * 4 + f
    cos = cos_out[pl.ds(me * span, span), :]
    sin = sin_out[pl.ds(me * span, span), :]
    own[:, :QR] = normalize(raw_out[:, :QR], g_query).astype(bf16)
    own[:, QR : QR + KR] = normalize(raw_out[:, QR : QR + KR], g_latent).astype(bf16)
    rope = pltpu.roll(raw_out[:, QR + KR :], DN, 1)
    own[:, QR + KR :] = (rope * cos - swapped(rope) * sin).astype(bf16)
    gather_plane_steps(wires, own, lat)

    for copy in swaps:
        copy.wait_recv()
    for copy in [gains_x, gains_m, gains_r, mine] + across + trade + to_mate + rest + swaps:
        copy.wait_send()


def front(x, qd, ld, gains, qup, lup, seg_col, seg_row, heads, name_id):
    freq = ROPE_BASE ** (-np.arange(DR // 2, dtype=np.float32) / (DR // 2))
    freq = np.concatenate([np.zeros(DN), freq, freq, np.zeros(LANES - DN - DR)])
    freq = jnp.asarray(freq[None], f32)
    span, length = x.shape[0], seg_col.shape[0]
    rows, width = qd.shape[0], heads * LANES
    shape = jax.ShapeDtypeStruct
    shapes = (
        shape((length, PACK), bf16),
        shape((QR, width), bf16),
        shape((KR, width), bf16),
        shape((4 * rows, PACK), bf16),
        shape((span, PACK), f32),
        shape((span, D), bf16),
        shape((8, D), f32),
        shape((length, LANES), f32),
        shape((length, LANES), f32),
    )
    pieces = 4
    scratch = [
        pltpu.VMEM((rows, PACK), bf16),
        pltpu.VMEM((8, QR), f32),
        pltpu.VMEM((4, 8, QR), f32),
        pltpu.VMEM((4, qup.shape[0], width), bf16),
        pltpu.VMEM((span, PACK), bf16),
    ]
    operands = (x, qd, ld) + tuple(g[None] for g in gains) + (qup, lup, seg_col, seg_row, freq)
    return remote_call(
        functools.partial(front_kernel, pieces, heads),
        name_id,
        shapes,
        scratch,
        4 + 4 * pieces + 6 + 9,
        operands,
    )


def ffn_group_kernel(
    columns,
    x,
    cot_all,
    w_gu,
    w_down,
    h_out,
    g_out,
    gx_out,
    y_keep,
    y_send,
    x_all,
    wg,
    wd,
    xs,
    cs,
    hv,
    gv,
    ht,
    gt,
    gx_part,
    y_part,
    g_mate,
    y_mate,
    sent,
    from_x,
    local,
    send,
    recv,
):
    units = wd.shape[0]
    span = x.shape[0]
    block = 2 * span
    width = D // columns
    y, f, core, mate, along_x, along_y = seats()
    group = y * 4 * span
    chip = lax.div(f, 2)
    load_gu = pltpu.make_async_copy(w_gu, wg, local.at[0])
    load_down = pltpu.make_async_copy(w_down, wd, local.at[1])
    load_gu.start()
    load_down.start()
    load_cot = []
    for at, which in enumerate((chip, 1 - chip)):
        where = pl.ds(pl.multiple_of(group + which * block, LANES), block)
        load_cot.append(pltpu.make_async_copy(cot_all.at[where], cs.at[at], local.at[6 + at]))
        load_cot[at].start()
    greet([mate, along_x, along_y])
    wires = Wires(send, recv)
    x_f = lax.rem(f + 2, 4)
    me, y_seat, far = y * 4 + f, (1 - y) * 4 + f, (1 - y) * 4 + x_f
    half = span // 2
    place = lambda seat, first, rows: x_all.at[
        pl.ds(pl.multiple_of(seat * span + first, 16), rows)
    ]
    mine = pl.ds(core * span, span)
    other = pl.ds((1 - core) * span, span)
    x_x = wires.copy(x, xs.at[1, mine], along_x)
    x_m = wires.copy(x, xs.at[0, mine], mate)
    x_x.start()
    x_m.start()
    xs[0, mine] = x[...]
    x_r = wires.copy(xs.at[1, mine], xs.at[1, mine], mate)
    x_y = wires.copy(x, place(me, 0, span), along_y)
    x_y.start()
    pass_y = wires.copy(
        xs.at[1, pl.ds(core * span, half)], place(y * 4 + x_f, 0, half), along_y
    )
    pass_x = wires.copy(place(y_seat, half, half), place(y_seat, half, half), along_x)
    mate_y = wires.copy(place(y_seat, 0, span), place(y_seat, 0, span), mate)
    mate_u = wires.copy(place(far, 0, half), place(far, 0, half), mate)
    mate_l = wires.copy(place(far, half, half), place(far, half, half), mate)
    keep_x = [
        pltpu.make_async_copy(
            xs.at[at], place(y * 4 + which * 2, 0, block), local.at[8 + at]
        )
        for at, which in enumerate((chip, 1 - chip))
    ]
    y_m = [wires.copy(y_part.at[i, other], y_mate.at[i], mate) for i in range(2)]
    cols = [slice(i * width, (i + 1) * width) for i in range(columns)]
    to_mate = lambda at: [
        wires.copy(gx_part.at[at, other, c], g_mate.at[at, :, c], mate) for c in cols
    ]
    g_near, g_far = to_mate(0), to_mate(1)
    g_x = [wires.copy(sent.at[:, c], from_x.at[:, c], along_x) for c in cols]

    cut = units // 2 // LANES * LANES

    def hidden(at):
        tokens = slice(at * block, (at + 1) * block)
        for rows in (slice(0, cut), slice(cut, units)):
            gate = dot(wg[0, rows, :], xs[at], NT)
            upper = dot(wg[1, rows, :], xs[at], NT)
            grad = dot(wd[rows, :], cs[at], NT) * RESIDUAL_SCALE
            sigma = jax.nn.sigmoid(gate)
            silu = gate * sigma
            value = silu * upper
            hv[at, rows, :] = value.astype(bf16)
            ht[tokens, rows] = value.T.astype(bf16)
            value = grad * upper * sigma * (1.0 + gate * (1.0 - sigma))
            gv[at, 0, rows, :] = value.astype(bf16)
            gt[0, tokens, rows] = value.T.astype(bf16)
            value = grad * silu
            gv[at, 1, rows, :] = value.astype(bf16)
            gt[1, tokens, rows] = value.T.astype(bf16)
        which = chip if at == 0 else 1 - chip
        where = pl.ds(pl.multiple_of(group + which * block, LANES), block)
        out_h = pltpu.make_async_copy(hv.at[at], h_out.at[:, where], local.at[2 + 2 * at])
        out_g = pltpu.make_async_copy(gv.at[at], g_out.at[:, :, where], local.at[3 + 2 * at])
        out_h.start()
        out_g.start()
        return [out_h, out_g]

    load_gu.wait()
    load_down.wait()
    x_m.wait_recv()
    for copy in load_cot:
        copy.wait()
    stores = hidden(0)
    x_x.wait_recv()
    x_r.start()
    pass_y.start()
    x_y.wait_recv()
    pass_x.start()
    mate_y.start()
    x_r.wait_recv()
    for copy in keep_x:
        copy.start()
    stores += hidden(1) + keep_x

    def pass_on(i):
        g_far[i].wait_recv()
        sent[:, cols[i]] = gx_part[1, mine, cols[i]] + g_mate[1, :, cols[i]]
        g_x[i].start()

    for i, c in enumerate(cols):
        total = dot(gt[0], wg[0, :, c]) + dot(gt[1], wg[1, :, c])
        gx_part[:, :, c] = total.astype(bf16).reshape(2, block, width)
        g_far[i].start()
        g_near[i].start()
        if i > 0:
            pass_on(i - 1)
    pass_y.wait_recv()
    mate_u.start()
    pass_x.wait_recv()
    mate_l.start()
    for i, c in enumerate(cols):
        y_part[:, :, c] = dot(ht[...], wd[:, c]).astype(bf16).reshape(2, block, width)
        if i == 0:
            pass_on(columns - 1)
    for copy in y_m:
        copy.start()
    for i, c in enumerate(cols):
        g_near[i].wait_recv()
        g_x[i].wait_recv()
        keep = gx_part[0, mine, c].astype(f32) + g_mate[0, :, c].astype(f32)
        gx_out[:, c] = (keep + from_x[:, c].astype(f32)).astype(bf16)
    for copy in y_m:
        copy.wait_recv()
    y_keep[...] = y_part[0, mine] + y_mate[0]
    y_send[...] = y_part[1, mine] + y_mate[1]
    for copy in (mate_y, mate_u, mate_l):
        copy.wait_recv()
    plane = [x_y, pass_y, pass_x, mate_y, mate_u, mate_l]
    for copy in [x_x, x_m, x_r] + y_m + g_near + g_far + g_x + plane:
        copy.wait_send()
    for copy in stores:
        copy.wait()


def ffn_group(x, cot_all, w_gu, w_down, name_id):
    tokens = cot_all.shape[0]
    span = x.shape[0]
    units = w_down.shape[0]
    columns = 5
    wires = 11 + 3 * columns
    anywhere = pl.BlockSpec(memory_space=pl.ANY)
    vmem = pl.BlockSpec(memory_space=pltpu.VMEM)
    buffer = lambda *shape: pltpu.VMEM(shape, bf16)
    return pl.pallas_call(
        functools.partial(ffn_group_kernel, columns),
        out_shape=ffn_shapes(units, tokens)
        + [jax.ShapeDtypeStruct((span, D), bf16)] * 3
        + [jax.ShapeDtypeStruct((tokens, D), bf16)],
        in_specs=[vmem, anywhere, anywhere, anywhere],
        out_specs=[anywhere, anywhere, vmem, vmem, vmem, anywhere],
        scratch_shapes=[
            buffer(2, units, D),
            buffer(units, D),
            buffer(2, 2 * span, D),
            buffer(2, 2 * span, D),
            buffer(2, units, 2 * span),
            buffer(2, 2, units, 2 * span),
            buffer(4 * span, units),
            buffer(2, 4 * span, units),
            buffer(2, 2 * span, D),
            buffer(2, 2 * span, D),
            buffer(2, span, D),
            buffer(2, span, D),
            buffer(span, D),
            buffer(span, D),
            pltpu.SemaphoreType.DMA((10,)),
            pltpu.SemaphoreType.DMA((wires,)),
            pltpu.SemaphoreType.DMA((wires,)),
        ],
        compiler_params=pltpu.CompilerParams(
            collective_id=name_id, has_side_effects=True, vmem_limit_bytes=62 * MIB
        ),
        cost_estimate=pl.CostEstimate(
            flops=12 * 4 * span * units * D, bytes_accessed=6 * units * D, transcendentals=0
        ),
    )(x, cot_all, w_gu, w_down)


def ffn_others_kernel(
    span,
    x_z,
    cot_z,
    x_far,
    cot_far,
    x_in,
    cot_in,
    h_in,
    g_in,
    w_gu,
    w_down,
    x_all,
    cot_all,
    h_out,
    g_out,
    wg,
    wd,
    xb,
    cb,
    hb,
    gb,
    stage,
    loads,
    local,
    slots_in,
    slots_out,
    send,
    recv,
):
    length = 8 * span
    block = 2 * span
    y = lax.axis_index("ctx")
    load_gu = pltpu.make_async_copy(w_gu, wg, loads.at[0])
    load_down = pltpu.make_async_copy(w_down, wd, loads.at[1])
    load_gu.start()
    load_down.start()
    greet(seats()[3:])
    wires = Wires(send, recv)
    def unit(r, own, far, out, at):
        z = turn_z(r)
        return Light(
            wires, own.at[z], far.at[z], stage.at[at], out, r * length, local.at[at]
        )

    x_unit = {r: unit(r, x_z, x_far, x_all, r - 2) for r in (2, 3)}
    c_unit = {r: unit(r, cot_z, cot_far, cot_all, r) for r in (2, 3)}
    for one in (x_unit[2], c_unit[2], x_unit[3], c_unit[3]):
        one.load()
    x_unit[2].start()
    c_unit[2].start()

    def where(i):
        first = jnp.where(i < 2, (1 - y) * 4 * span + i * block, length + (i - 2) * block)
        return pl.ds(pl.multiple_of(first, LANES), block)

    def fetch(i):
        slot = lax.rem(i, 2)
        return [
            pltpu.make_async_copy(x_all.at[where(i)], xb.at[slot], slots_in.at[0, slot]),
            pltpu.make_async_copy(cot_all.at[where(i)], cb.at[slot], slots_in.at[1, slot]),
        ]

    def store(i):
        slot = lax.rem(i, 2)
        return [
            pltpu.make_async_copy(hb.at[slot], h_out.at[:, where(i)], slots_out.at[0, slot]),
            pltpu.make_async_copy(gb.at[slot], g_out.at[:, :, where(i)], slots_out.at[1, slot]),
        ]

    count = 14
    for copy in fetch(0):
        copy.start()
    load_gu.wait()
    load_down.wait()

    def step(i, carry):
        slot = lax.rem(i, 2)
        for copy in fetch(i):
            copy.wait()

        @pl.when(i >= 2)
        def _():
            for copy in store(i - 2):
                copy.wait()

        def between(number, *steps):
            @pl.when(i == number)
            def _():
                for one in steps:
                    one()

        between(3, x_unit[2].relay, c_unit[2].relay, x_unit[3].start)
        between(4, c_unit[3].start)
        between(5, x_unit[2].finish, c_unit[2].finish)
        between(8, x_unit[3].relay, c_unit[3].relay)
        between(9, x_unit[3].finish, c_unit[3].finish)

        @pl.when(i + 1 < count)
        def _():
            for copy in fetch(i + 1):
                copy.start()

        hidden_block(xb[slot], cb[slot], wg, wd, hb.at[slot], gb.at[slot], 2)
        for copy in store(i):
            copy.start()
        return carry

    lax.fori_loop(0, count, step, 0)
    for i in (count - 2, count - 1):
        for copy in store(i):
            copy.wait()


def ffn_others(x_z, cot_z, x_far, cot_far, x_all, cot_all, h_all, g_all, w_gu, w_down, name_id):
    units = w_down.shape[0]
    tokens = x_all.shape[0]
    span = x_z.shape[1]
    block = 2 * span
    wires = 4 * Light.wires_needed
    anywhere = pl.BlockSpec(memory_space=pl.ANY)
    buffer = lambda *shape: pltpu.VMEM(shape, bf16)
    return pl.pallas_call(
        functools.partial(ffn_others_kernel, span),
        out_shape=[jax.ShapeDtypeStruct((tokens, D), bf16)] * 2 + ffn_shapes(units, tokens),
        in_specs=[anywhere] * 10,
        out_specs=[anywhere] * 4,
        input_output_aliases={4: 0, 5: 1, 6: 2, 7: 3},
        scratch_shapes=[
            buffer(2, units, D),
            buffer(units, D),
            buffer(2, block, D),
            buffer(2, block, D),
            buffer(2, units, block),
            buffer(2, 2, units, block),
            buffer(4, 2, span, D),
            pltpu.SemaphoreType.DMA((2,)),
            pltpu.SemaphoreType.DMA((4, 4)),
            pltpu.SemaphoreType.DMA((2, 2)),
            pltpu.SemaphoreType.DMA((2, 2)),
            pltpu.SemaphoreType.DMA((wires,)),
            pltpu.SemaphoreType.DMA((wires,)),
        ],
        compiler_params=pltpu.CompilerParams(
            collective_id=name_id, has_side_effects=True, vmem_limit_bytes=60 * MIB
        ),
        cost_estimate=pl.CostEstimate(
            flops=6 * (tokens - 4 * span) * units * D,
            bytes_accessed=6 * units * D + 10 * tokens * D,
            transcendentals=0,
        ),
    )(x_z, cot_z, x_far, cot_far, x_all, cot_all, h_all, g_all, w_gu, w_down)


def ffn_grads_kernel(g, h, x, cot, gu_out, down_out, h_kept, sem):
    which, column = pl.program_id(0), pl.program_id(1)
    load = pltpu.make_async_copy(h, h_kept, sem.at[0])
    units = h.shape[0]
    cut = units // 2

    @pl.when((which == 0) & (column == 0))
    def _():
        load.start()

    @pl.when((which == 2) & (column == 0))
    def _():
        load.wait()

    @pl.when(which < 2)
    def _():
        for rows in (slice(0, cut), slice(cut, units)):
            gu_out[0, rows, :] = dot(g[0, rows, :], x[...])

    @pl.when(which == 2)
    def _():
        for rows in (slice(0, cut), slice(cut, units)):
            down_out[rows, :] = dot(h_kept[rows, :], cot[...]) * RESIDUAL_SCALE


def ffn_grads(g_all, h_all, x_all, cot_all):
    units, tokens = h_all.shape
    width = 256
    columns = D // width
    shape = jax.ShapeDtypeStruct
    last = columns - 1
    gate_up = lambda m, n: jnp.where(m < 2, n, last)
    only_down = lambda m, n: jnp.where(m < 2, 0, n)
    return pl.pallas_call(
        ffn_grads_kernel,
        grid=(3, columns),
        in_specs=[
            pl.BlockSpec((1, units, tokens), lambda m, n: (jnp.minimum(m, 1), 0, 0)),
            pl.BlockSpec(memory_space=pl.ANY),
            pl.BlockSpec((tokens, width), lambda m, n: (0, gate_up(m, n))),
            pl.BlockSpec((tokens, width), lambda m, n: (0, only_down(m, n))),
        ],
        out_specs=[
            pl.BlockSpec((1, units, width), lambda m, n: (jnp.minimum(m, 1), 0, gate_up(m, n))),
            pl.BlockSpec((units, width), lambda m, n: (0, only_down(m, n))),
        ],
        out_shape=[shape((2, units, D), f32), shape((units, D), f32)],
        scratch_shapes=[pltpu.VMEM((units, tokens), bf16), pltpu.SemaphoreType.DMA((1,))],
        compiler_params=pltpu.CompilerParams(vmem_limit_bytes=62 * MIB),
        cost_estimate=pl.CostEstimate(
            flops=6 * tokens * units * D,
            bytes_accessed=6 * units * tokens + 6 * tokens * D + 12 * units * D,
            transcendentals=0,
        ),
    )(g_all, h_all, x_all, cot_all)


def norm_back_rows(values, gain, grad):
    inverse = lax.rsqrt(jnp.mean(values * values, axis=-1, keepdims=True) + EPS)
    unit = values * inverse
    scaled = gain * grad
    return (scaled - unit * jnp.mean(unit * scaled, axis=-1, keepdims=True)) * inverse


def finish_kernel(
    gq,
    gkv,
    rope,
    lat,
    wq,
    wl,
    w_in,
    raw,
    n,
    x,
    grad_resid,
    gains,
    cos_all,
    sin_all,
    ffn_gain,
    part,
    input_grad,
    lat_part,
    lat_sum,
    own,
    from_mate,
    from_x,
    from_y,
    last,
    relay,
    n_all,
    ups,
    raw_own,
    raw_all,
    down,
    traded,
    send,
    recv,
):
    span = x.shape[0]
    length = gq.shape[0]
    width = gq.shape[1]
    rows = w_in.shape[0] // 4
    q_rows, l_rows = QR // 4, KR // 4
    y, f, core, mate, along_x, along_y = seats()
    x_f, m_f, c_f = lax.rem(f + 2, 4), f + 1 - 2 * core, 3 - f
    cross = {"fsdp": c_f}
    others = ((x_f, along_x), (c_f, cross), (m_f, mate))
    greet([mate, along_x, along_y, cross])
    wires = Wires(send, recv)
    columns = lambda seat: pl.ds(pl.multiple_of(seat * rows, LANES), rows)
    mine = pl.ds(f * span, span)
    n_sends = [wires.copy(n.at[:, columns(seat)], n_all.at[mine], peer) for seat, peer in others]
    for copy in n_sends:
        copy.start()
    n_all[mine, :] = n[:, columns(f)]

    each = span + EXTRA
    for first in range(0, length, 512):
        some = slice(first, first + 512)
        q_part = dot(gq[some, :], wq[...], NT).astype(bf16)
        l_part = dot(gkv[some, :], wl[...], NT).astype(bf16)
        r_part = rope[some, :].astype(bf16)
        for at in range(0, 512, span):
            here = (first + at) // span * each
            lat_part[here : here + span, :QR] = q_part[at : at + span]
            lat_part[here : here + span, QR : QR + KR] = l_part[at : at + span]
            lat_part[here : here + span, QR + KR :] = r_part[at : at + span]
    for seat in range(8):
        here = seat * each + span
        piece = ffn_gain[:, seat % 4 * rows : (seat % 4 + 1) * rows]
        lat_part[here : here + EXTRA, :] = jnp.zeros((EXTRA, PACK), bf16)
        lat_part[here : here + EXTRA, :rows] = jnp.broadcast_to(piece, (EXTRA, rows)).astype(bf16)

    swap_rows = q_rows + l_rows
    swaps = [
        wires.copy(ups.at[seat], part.at[pl.ds(f * swap_rows, swap_rows)], peer)
        for seat, peer in others
    ]

    def column_gradients():
        q_grad = dot(lat[:, :QR], gq[...], TN).astype(bf16)
        l_grad = dot(lat[:, QR : QR + KR], gkv[...], TN).astype(bf16)
        for seat in range(4):
            ups[seat, :q_rows] = q_grad[seat * q_rows : (seat + 1) * q_rows]
            ups[seat, q_rows:] = l_grad[seat * l_rows : (seat + 1) * l_rows]
        part[pl.ds(f * swap_rows, swap_rows), :] = ups[f]

    scatter_plane_steps(
        wires, lat_part, lat_sum, own, from_mate, from_x, from_y, last, relay, column_gradients
    )

    me = pl.ds((y * 4 + f) * span, span)
    grad = lat_sum[:span, :].astype(f32)
    raw_own[:, :QR] = norm_back_rows(raw[:, :QR], gains[2:3, :QR], grad[:, :QR]).astype(bf16)
    raw_own[:, QR : QR + KR] = norm_back_rows(
        raw[:, QR : QR + KR], gains[3:4, :KR], grad[:, QR : QR + KR]
    ).astype(bf16)
    turned = grad[:, QR + KR :]
    lane = lax.broadcasted_iota(jnp.int32, turned.shape, 1)
    turned = turned * cos_all[me, :] + swapped(turned) * sin_all[me, :]
    turned = jnp.where((lane >= DN) & (lane < DN + DR), turned, 0.0)
    raw_own[:, QR + KR :] = pltpu.roll(turned, LANES - DN, 1).astype(bf16)
    raw_x = wires.copy(raw_own, raw_all.at[mine], along_x)
    raw_m = wires.copy(raw_own, raw_all.at[mine], mate)
    theirs = raw_all.at[pl.ds(x_f * span, span)]
    raw_r = wires.copy(theirs, theirs, mate)
    raw_x.start()
    raw_m.start()
    for copy in swaps:
        copy.start()
    raw_all[mine, :] = raw_own[...]
    for copy in n_sends:
        copy.wait_recv()
    raw_x.wait_recv()
    raw_r.start()
    raw_m.wait_recv()
    raw_r.wait_recv()

    down[...] = dot(n_all[...], raw_all[...], TN).astype(bf16)
    half = rows // 2
    trade = wires.copy(down.at[pl.ds((1 - y) * half, half)], traded, along_y)
    trade.start()
    inputs = x[...].astype(f32)
    grad_in = dot(raw_own[...], w_in[...], NT)
    input_grad[...] = grad_resid[...] + norm_back_rows(inputs, gains[0:1, :], grad_in)
    first = 4 * swap_rows
    last_rows = part.shape[0] - first - 2 * half
    part[first + 2 * half :, :] = jnp.zeros((last_rows, width), bf16)
    part[first + 2 * half :, :rows] = lat_sum[span : span + last_rows, :rows]
    trade.wait_recv()
    kept = down[pl.ds(y * half, half), :] + traded[...]
    part[first : first + half, :] = kept[:, :width]
    part[first + half : first + 2 * half, :] = jnp.zeros((half, width), bf16)
    part[first + half : first + 2 * half, : PACK - width] = kept[:, width:]
    for copy in swaps:
        copy.wait_recv()
    for copy in n_sends + swaps + [raw_x, raw_m, raw_r, trade]:
        copy.wait_send()


def finish(operands, name_id):
    gq, x, w_in = operands[0], operands[9], operands[6]
    span, width, rows = x.shape[0], gq.shape[1], w_in.shape[0] // 4
    part_rows = QR + KR + rows + 16
    each = span + EXTRA
    buffer = lambda *shape: pltpu.VMEM(shape, bf16)
    return remote_call(
        finish_kernel,
        name_id,
        (jax.ShapeDtypeStruct((part_rows, width), bf16), jax.ShapeDtypeStruct((span, D), f32)),
        [
            buffer(8 * each, PACK),
            buffer(each, PACK),
            buffer(4, each, PACK),
            buffer(4, each, PACK),
        ]
        + [buffer(2, each // 2, PACK)] * 4
        + [
            buffer(4 * span, rows),
            buffer(4, (QR + KR) // 4, width),
            buffer(span, PACK),
            buffer(4 * span, PACK),
            buffer(rows, PACK),
            buffer(rows // 2, PACK),
        ],
        20,
        operands,
    )


def gain_grad(gain, pairs):
    return sum(jnp.sum(w.astype(f32) * grad, axis=1) for w, grad in pairs) / gain


def unpack_kernel(
    total, qup, lup, qd, ld, gain_a, gain_q, gain_l, up, lu, out, qg, lg, a_out, q_out, l_out, f_out
):
    width = total.shape[2]
    heads = width // LANES
    q_rows, l_rows = qup.shape[0], lup.shape[0]
    rows = q_rows + l_rows
    each = heads * DV
    base = D // width * each
    lane = lax.broadcasted_iota(jnp.int32, (q_rows, LANES), 1)
    own = DN + DR

    def head(number):
        seat, side = number // (2 * heads), number // heads % 2
        at = number % heads * LANES
        begin = base + seat * rows
        return total[side, begin : begin + q_rows, at : at + LANES].astype(f32)

    turn = lambda values, by: pltpu.roll(values, by % LANES, 1)
    q_sum = jnp.zeros((q_rows, 1), f32)
    for first in range(0, H, 4):
        a, b, c, d = (head(first + i) for i in range(4))
        merged = (
            jnp.where(lane < own, a, turn(b, own)),
            jnp.where(lane < 2 * own - LANES, turn(b, -32), turn(c, 2 * own - LANES)),
            jnp.where(lane < own - DN, turn(c, -DN), turn(d, own - DN)),
        )
        for i, values in enumerate(merged):
            at = first * own + i * LANES
            up[:, at : at + LANES] = values
            q_sum += jnp.sum(values * qup[:, at : at + LANES].astype(f32), axis=1, keepdims=True)
    q_out[...] = q_sum / gain_q[...].astype(f32)
    l_sum = jnp.zeros((l_rows, 1), f32)
    for seat in range(4):
        for side in range(2):
            at = (seat * 2 + side) * width
            first = base + seat * rows + q_rows
            values = total[side, first : first + l_rows, :].astype(f32)
            lu[:, at : at + width] = values
            l_sum += jnp.sum(values * lup[:, at : at + width].astype(f32), axis=1, keepdims=True)
    l_out[...] = l_sum / gain_l[...].astype(f32)
    for part in range(D // width):
        for side in range(2):
            at = part * each
            out[side * each : (side + 1) * each, part * width : (part + 1) * width] = total[
                side, at : at + each, :
            ].astype(f32)
    first = base + 4 * rows
    half = qd.shape[0] // 2
    f_out[...] = total[0, first + 2 * half : first + 2 * half + 1, : f_out.shape[1]].astype(f32)
    for side in range(2):
        mine = slice(side * half, (side + 1) * half)
        left = total[side, first : first + half, :].astype(f32)
        right = total[side, first + half : first + 2 * half, : PACK - width].astype(f32)
        qg[mine, :width] = left
        qg[mine, width:] = right[:, : QR - width]
        lg[mine, :] = right[:, QR - width : DOWN - width]
        weighted = jnp.sum(left * qd[mine, :width].astype(f32), axis=1, keepdims=True)
        weighted += jnp.sum(
            right[:, : QR - width] * qd[mine, width:].astype(f32), axis=1, keepdims=True
        )
        weighted += jnp.sum(
            right[:, QR - width : DOWN - width] * ld[mine, :].astype(f32), axis=1, keepdims=True
        )
        a_out[mine, :] = weighted / gain_a[mine, :].astype(f32)


def unpack(total, qup, lup, qd, ld, gain_a, gain_q, gain_l):
    shape = lambda *dims: jax.ShapeDtypeStruct(dims, f32)
    rows = lambda weight: weight.shape[0]
    return pl.pallas_call(
        unpack_kernel,
        out_shape=(
            shape(*qup.shape),
            shape(*lup.shape),
            shape(rows(qd), D),
            shape(*qd.shape),
            shape(*ld.shape),
            shape(rows(qd), 1),
            shape(rows(qup), 1),
            shape(rows(lup), 1),
            shape(1, rows(qd)),
        ),
        compiler_params=pltpu.CompilerParams(vmem_limit_bytes=60 * MIB),
        cost_estimate=pl.CostEstimate(flops=0, bytes_accessed=24 * MIB, transcendentals=0),
    )(total, qup, lup, qd, ld, gain_a[:, None], gain_q[:, None], gain_l[:, None])


def body(
    layer_input,
    segment_ids,
    attn_gain,
    query_down,
    query_gain,
    query_up,
    latent_down,
    latent_gain,
    latent_up,
    attn_output,
    ffn_gain,
    gate_up,
    down_proj,
    cotangent,
):
    span = layer_input.shape[1]
    length = segment_ids.shape[1]
    n_f = lax.axis_size("fsdp")
    n_c = lax.axis_size("ctx")
    n_h = n_c if H % (n_f * n_c) == 0 else 1
    square = n_f == 4 and n_c == 2 and lax.axis_size("dp") == 4
    heads = H // (n_f * n_h)
    ctx = lax.axis_index("ctx") if n_h > 1 else 0
    fsdp = lax.axis_index("fsdp")
    group = lax.axis_index(("dp", "ctx"))
    place = jnp.reshape(group, (1,)).astype(jnp.int32)
    offset = lax.axis_index(PLANE) * span

    seg = segment_ids[0]
    seg_col = seg[:, None]
    seg_row = seg[None, :]
    own_q = heads * (DN + DR)
    own_kv = heads * (DN + DV)

    def own_columns(weight, width):
        rows = weight.shape[0]
        parts = weight.reshape(rows, n_f, n_h, width)
        parts = lax.dynamic_index_in_dim(parts, ctx, 2, keepdims=False)
        parts = jnp.transpose(parts, (1, 0, 2))
        return lax.all_to_all(parts, "fsdp", 0, 0, tiled=False).reshape(rows * n_f, width)

    wo = lax.dynamic_slice_in_dim(attn_output, ctx * heads * DV, heads * DV, 0)
    wo = jnp.pad(wo.reshape(heads, DV, D), ((0, 0), (LANES - DV, 0), (0, 0)))
    wo = wo.reshape(heads * LANES, D)
    def gather_plane(shard, name_id):
        if square:
            return plane_gather(shard, name_id)
        return lax.all_gather(shard, PLANE, axis=0, tiled=True)

    def scatter_plane(part, name_id):
        if square:
            return plane_scatter(part, name_id)
        if n_h > 1:
            return lax.psum_scatter(part, PLANE, scatter_dimension=0, tiled=True)
        half = length // n_c
        part = lax.dynamic_slice_in_dim(part, lax.axis_index("ctx") * half, half, 0)
        return lax.psum_scatter(part, "fsdp", scatter_dimension=0, tiled=True)

    def gather_heads(part):
        return lax.all_gather(part, "ctx", axis=0) if n_h > 1 else part[None]

    inputs = layer_input[0].astype(f32)
    grad_out = cotangent[0].astype(f32)
    if square:
        lat, wq, wl, w_down_in, raw, normed_in, gains, cos_all, sin_all = front(
            layer_input[0],
            query_down,
            latent_down,
            (attn_gain, ffn_gain, query_gain, latent_gain),
            query_up,
            latent_up,
            seg_col,
            seg_row,
            heads,
            1,
        )
        g_attn, g_ffn, g_query, g_latent = gains[0], gains[1], gains[2, :QR], gains[3, :KR]
    else:
        gather = lambda shard: lax.all_gather(shard, "fsdp", axis=0, tiled=True)
        g_attn, g_ffn, g_query, g_latent = (
            gather(g).astype(f32) for g in (attn_gain, ffn_gain, query_gain, latent_gain)
        )
        blank = jnp.zeros((query_down.shape[0], PACK - DOWN), bf16)
        w_down_in = gather(jnp.concatenate([query_down, latent_down, blank], axis=1))
        wq = own_columns(query_up, own_q).reshape(QR, heads, DN + DR)
        wq = jnp.pad(wq, ((0, 0), (0, 0), (0, LANES - DN - DR))).reshape(QR, heads * LANES)
        wl = own_columns(latent_up, own_kv)
        starts = [jnp.sum((seg < number).astype(jnp.int32)) for number in range(4)]
        doc_start = sum(jnp.where(seg == number, starts[number], 0) for number in range(1, 4))
        cosine, sine = angles((jnp.arange(length, dtype=jnp.int32) - doc_start).astype(f32))
        ones = jnp.ones((length, DN), f32)
        rest = jnp.zeros((length, LANES - DN - DR), f32)
        cos_all = jnp.concatenate([ones, cosine, cosine, rest], axis=1)
        sin_all = jnp.concatenate([0.0 * ones, sine, sine, rest], axis=1)
        cos_own = lax.dynamic_slice_in_dim(cosine, offset, span, 0)
        sin_own = lax.dynamic_slice_in_dim(sine, offset, span, 0)
        normed_in = normalize(inputs, g_attn).astype(bf16)
        raw = dot(normed_in, w_down_in)
        query_normed = normalize(raw[:, :QR], g_query).astype(bf16)
        latent = normalize(raw[:, QR : QR + KR], g_latent).astype(bf16)
        key_rope = rotate(raw[:, QR + KR : DOWN], cos_own, sin_own).astype(bf16)
        key_rope = jnp.pad(key_rope, ((0, 0), (DN, LANES - DN - DR)))
        lat = jnp.concatenate([query_normed, latent, key_rope], axis=1)
        lat = lax.all_gather(lat, PLANE, axis=0, tiled=True)
    query_latent = raw[:, :QR]
    latent_pre = raw[:, QR : QR + KR]
    operands = (lat, wq, wl, cos_all, sin_all, seg_col, seg_row)
    if square:
        cot_z = lax.all_gather(cotangent[0], "dp", axis=0)
        q, k, kv, o, lse, cot_all, branch = attend(*operands, cotangent[0], wo, 4 * length, 2)
        diagonal = ((1 - ctx) * 4 + (fsdp + 2) % 4) * span
        cot_far = lax.all_gather(
            lax.dynamic_slice(cot_all, (diagonal, 0), (span, D)), "dp", axis=0
        )
    else:
        cot_all = lax.all_gather(cotangent[0], ALL, axis=0, tiled=True)
        q, k, kv, o, lse = attend(*operands)
        branch = dot(o, wo).astype(bf16)
    branch = scatter_plane(branch, 3)
    resid = inputs + RESIDUAL_SCALE * branch.astype(f32)

    ffn_in = normalize(resid, g_ffn).astype(bf16)
    own = n_f * span
    if square:
        ffn_in, cot_z = lax.optimization_barrier((ffn_in, cot_z))
        x_z = lax.all_gather(ffn_in, "dp", axis=0)
        h_all, g_all, gx, y_keep, y_send, x_all = ffn_group(
            ffn_in, cot_all, gate_up, down_proj, 4
        )
        x_far = lax.all_gather(lax.dynamic_slice(x_all, (diagonal, 0), (span, D)), "dp", axis=0)
    else:
        x_own = lax.all_gather(ffn_in, "fsdp", axis=0, tiled=True)
        h_all, g_all, y_part, gx_part = ffn_own(place, x_own, cot_all, gate_up, down_proj)
        gx = lax.psum_scatter(gx_part, "fsdp", scatter_dimension=0, tiled=True)
        y = lax.psum_scatter(y_part, "fsdp", scatter_dimension=0, tiled=True).astype(f32)
    gx = gx.astype(f32)
    grad_resid_add, ffn_gain_part = norm_back(resid, g_ffn, gx)
    grad_resid = grad_out + grad_resid_add
    gb = (RESIDUAL_SCALE * grad_resid).astype(bf16)
    if square:
        gb, cot_far = lax.optimization_barrier((gb, cot_far))
    gb = gather_plane(gb, 6)
    operands = (gb, wo, q, k, kv, o, lse, cos_all, sin_all, seg_col, seg_row)
    if square:
        bulk = (x_z, cot_z, cot_far, x_all, cot_all)
        gq, gkv, rope, out_part, x_all, cot_all = attend_back(*operands, bulk, 4 * length, 9)
        rope, out_part, x_z, x_far = lax.optimization_barrier((rope, out_part, x_z, x_far))
        width = heads * LANES
        out_part = [out_part[:, at : at + width] for at in range(0, D, width)]
        out_total = lax.psum(jnp.concatenate(out_part[:-1], axis=0), "dp")
    else:
        x_all = lax.all_gather(ffn_in, ALL, axis=0, tiled=True)
        gq, gkv, rope, out_part = attend_back(*operands)
    width = heads * LANES
    q_rows, l_rows = QR // n_f, KR // n_f
    if square:
        part, input_grad = finish(
            (
                gq,
                gkv,
                rope,
                lat,
                wq,
                wl,
                w_down_in,
                raw,
                normed_in,
                layer_input[0],
                grad_resid,
                gains,
                cos_all,
                sin_all,
                ffn_gain_part[None],
            ),
            7,
        )
    else:
        lat_part = jnp.concatenate([dot(gq, wq, NT), dot(gkv, wl, NT), rope], axis=1).astype(bf16)
        extra = jnp.pad(ffn_gain_part.astype(bf16).reshape(n_f, -1), ((0, 0), (0, PACK - D // n_f)))
        extra = jnp.broadcast_to(extra[None, :, None], (n_c, n_f, EXTRA, PACK))
        extra = extra.reshape(n_c * n_f, EXTRA, PACK)
        lat_part = jnp.concatenate([lat_part.reshape(n_c * n_f, span, PACK), extra], axis=1)
        lat_sum = scatter_plane(lat_part.reshape(-1, PACK), 7).astype(f32)
        lat_grad = lat_sum[:span]
        ffn_gain_plane = lat_sum[span, : D // n_f]
        query_pre = norm_back(query_latent, g_query, lat_grad[:, :QR])[0]
        latent_back = norm_back(latent_pre, g_latent, lat_grad[:, QR : QR + KR])[0]
        rope_back = unrotate(lat_grad[:, QR + KR + DN : QR + KR + DN + DR], cos_own, sin_own)
        raw_grad = jnp.concatenate(
            [query_pre, latent_back, rope_back, jnp.zeros((span, PACK - DOWN), f32)], axis=1
        ).astype(bf16)
        input_add = norm_back(inputs, g_attn, dot(raw_grad, w_down_in, NT))[0]
        input_grad = grad_resid + input_add

        own_rows = D // n_f
        n_all = lax.all_to_all(
            jnp.transpose(normed_in.reshape(span, n_f, own_rows), (1, 0, 2)), "fsdp", 0, 0
        ).reshape(n_f * span, own_rows)
        raw_all = lax.all_gather(raw_grad, "fsdp", axis=0, tiled=True)
        down_in_part = dot(n_all, raw_all, TN)[:, :DOWN]
        gain_column = ffn_gain_plane[:, None] / n_c
        blank = jnp.zeros((own_rows, PACK - DOWN - 1), f32)
        down_in_part = jnp.concatenate([down_in_part, gain_column, blank], axis=1).astype(bf16)
        width = heads * LANES
        out_part = [out_part[:, at : at + width] for at in range(0, D, width)]
        up_part = dot(lat[:, :QR], gq, TN).astype(bf16).reshape(n_f, -1, width)
        lup_part = dot(lat[:, QR : QR + KR], gkv, TN).astype(bf16).reshape(n_f, -1, width)
        swap = lax.all_to_all(jnp.concatenate([up_part, lup_part], axis=1), "fsdp", 0, 0)
        q_rows, l_rows = QR // n_f, KR // n_f
        pieces = [swap.reshape(-1, width)] + out_part
        part = jnp.concatenate(pieces, axis=0)

    if square:
        part, x_z, y_keep, y_send, out_total = lax.optimization_barrier(
            (part, x_z, y_keep, y_send, out_total)
        )
        total = lax.psum(jnp.concatenate([out_part[-1], part], axis=0), "dp")
        y_far = lax.ppermute(y_send, "fsdp", [(i, (i + 2) % 4) for i in range(4)])
        y = y_keep.astype(f32) + y_far.astype(f32)
        x_all, cot_all, h_all, g_all = ffn_others(
            x_z, cot_z, x_far, cot_far, x_all, cot_all, h_all, g_all, gate_up, down_proj, 10
        )
    else:
        part, x_all = lax.optimization_barrier((part, x_all))
        total = lax.psum(part, "dp")
        h_all, g_all = ffn_rest(place, x_all, cot_all, gate_up, down_proj, h_all, g_all, own)
    output = resid + RESIDUAL_SCALE * y
    if square:
        out_total, total, h_all = lax.optimization_barrier((out_total, total, h_all))
        total = jnp.concatenate([out_total, total], axis=0)
    else:
        total, h_all = lax.optimization_barrier((total, h_all))
    total = gather_heads(total)
    if square:
        gate_up_grad, down_grad = ffn_grads(g_all, h_all, x_all, cot_all)
    else:
        gate_up_grad = lax.dot_general(
            g_all, x_all, (((2,), (0,)), ((), ())), preferred_element_type=f32
        )
        down_grad = dot(h_all, cot_all) * RESIDUAL_SCALE

    if square:
        up_grad, lup_grad, out_grad, q_down_grad, l_down_grad, ga, gq, gl, gf = unpack(
            total,
            query_up,
            latent_up,
            query_down,
            latent_down,
            attn_gain,
            query_gain,
            latent_gain,
        )
        gain_grads = [ga[:, 0], gq[:, 0], gl[:, 0], gf[0]]
    else:
        down_in_sum = lax.psum(down_in_part, ("dp", "ctx")).astype(f32)
        swapped_rows = n_f * (q_rows + l_rows)
        both = total[:, :swapped_rows].reshape(n_h, n_f, q_rows + l_rows, heads, LANES)
        up_grad = jnp.transpose(both[:, :, :q_rows, :, : DN + DR], (2, 1, 0, 3, 4))
        up_grad = up_grad.reshape(q_rows, -1).astype(f32)
        lup_grad = jnp.transpose(both[:, :, q_rows:], (2, 1, 0, 3, 4))
        lup_grad = lup_grad.reshape(l_rows, -1).astype(f32)
        out_grad = total[:, swapped_rows:].reshape(n_h, D // width, heads * DV, width)
        out_grad = jnp.transpose(out_grad, (0, 2, 1, 3)).reshape(-1, D).astype(f32)
        q_down_grad = down_in_sum[:, :QR]
        l_down_grad = down_in_sum[:, QR:DOWN]
        downs = [(query_down, q_down_grad), (latent_down, l_down_grad)]
        gain_grads = [
            gain_grad(attn_gain.astype(f32), downs),
            gain_grad(query_gain.astype(f32), [(query_up, up_grad)]),
            gain_grad(latent_gain.astype(f32), [(latent_up, lup_grad)]),
            down_in_sum[:, DOWN],
        ]

    return (
        output.astype(bf16)[None],
        input_grad[None],
        gain_grads[0],
        q_down_grad,
        gain_grads[1],
        up_grad,
        l_down_grad,
        gain_grads[2],
        lup_grad,
        out_grad,
        gain_grads[3],
        gate_up_grad,
        down_grad,
    )


def solution(mesh):
    in_specs = (
        P("dp", ("ctx", "fsdp"), None),
        P("dp", None),
        P("fsdp"),
        P("fsdp", None),
        P("fsdp"),
        P("fsdp", None),
        P("fsdp", None),
        P("fsdp"),
        P("fsdp", None),
        P("fsdp", None),
        P("fsdp"),
        P(None, "fsdp", None),
        P("fsdp", None),
        P("dp", ("ctx", "fsdp"), None),
    )
    out_specs = (
        P("dp", ("ctx", "fsdp"), None),
        P("dp", ("ctx", "fsdp"), None),
        P("fsdp"),
        P("fsdp", None),
        P("fsdp"),
        P("fsdp", None),
        P("fsdp", None),
        P("fsdp"),
        P("fsdp", None),
        P("fsdp", None),
        P("fsdp"),
        P(None, "fsdp", None),
        P("fsdp", None),
    )
    return jax.shard_map(body, mesh=mesh, in_specs=in_specs, out_specs=out_specs, check_vma=False)
```
